512 devices in a mesh: ctx: 32 (over y, z_lo), head: 16 (over x, z_hi, core).
Axes of the slice: x: 4, y: 8, z: 8 (z_hi: 2, z_lo: 4; z = z_hi * 4 + z_lo), core: 2. Of those that a mesh axis runs over, the one named last changes fastest.
Arguments:
- queries: bfloat16 [2, 512, 4096], P(None, ('ctx', 'head')), may hold values from -40 to 40
- cache_kv: bfloat16 [32, 2, 512, 4096], P('ctx', None, None, 'head'), may hold values from -24 to 24
- lengths: int32 [32], P('ctx'), may hold values from 64 to 512, as said below
- evict: int32 [1], replicated, may hold values from 0 to 31
- own_kv: bfloat16 [2, 2, 512, 4096], P(None, None, 'ctx', 'head'), may hold values from -6 to 6
- clean_kv: bfloat16 [2, 512, 4096], P(None, 'ctx', 'head'), may hold values from -6 to 6
Outputs:
- attended: bfloat16 [2, 512, 4096], P(None, ('ctx', 'head'))
- new_cache: bfloat16 [32, 2, 512, 4096], P('ctx', None, None, 'head')
The draws below stay inside these ranges and needn't reach their ends.
Inputs may be any that keep to these rules, and one draw needn't show every extreme that they name: `lengths`: at least one slot is full.
All inputs are finite; a program needn't handle non-finite values.
Results may differ from the reference program's by a relative error of at most 0.0065.
Values may be sent and summed in bfloat16 or wider, within the bound.
No kernel may reach another device: no remote copies, remote signals or barrier semaphores. Data moves between devices by JAX's collectives and lax.ppermute only.
A program may use at most 64 MiB of HBM per device.

```python
import math
import jax
import jax.numpy as jnp
from jax import lax

HD = 128
SPAN = 512
STEPS = 2
HEADS = 32
SLOTS = 32


def cache_base(key):
    return jax.random.truncated_normal(key, -6.0, 6.0, (SLOTS, 2, SPAN, HEADS * HD), jnp.float32)


def draw_cache_kv(key, part):
    base = cache_base(key)
    return base.astype(jnp.bfloat16)


def draw_queries(key, part):
    key = jax.random.fold_in(key, 12)
    drawn = 3.0 * jax.random.truncated_normal(key, -6.0, 6.0, (STEPS, SPAN, HEADS * HD), jnp.float32)
    return drawn.astype(jnp.bfloat16)


def draw_lengths(key, part):
    key = jax.random.fold_in(key, 13)
    first_key, second_key = jax.random.split(key)
    counts = jax.random.randint(first_key, (SLOTS,), SPAN // 8, SPAN + 1)
    full_slot = jax.random.randint(second_key, (), 0, SLOTS)
    counts = jnp.where(jnp.arange(SLOTS, dtype=jnp.int32) == full_slot, SPAN, counts)
    return counts.astype(jnp.int32)


def steps_of(key, shape, cuts, least, largest):
    factor_of, own = 1.0, jax.random.fold_in(key, 6)
    for position, parts in cuts:
        draws = jnp.exp(jax.random.uniform(jax.random.fold_in(own, position), (parts,), jnp.float32, least / len(cuts), largest / len(cuts)))
        factor_of = factor_of * jnp.repeat(draws, shape[position] // parts).reshape([-1 if axis == position else 1 for axis in range(len(shape))])
    return factor_of


def centred(own_key, shape, deviation, most, pieces=(), held_as=jnp.bfloat16):
    entries = deviation * jax.random.normal(own_key, shape, jnp.float32)
    if pieces:
        entries = entries * steps_of(own_key, shape, pieces, -0.22, 0.18)
    return jnp.clip(entries, -most, most).astype(held_as)


def setup_inputs(seed: int = 0) -> dict:
    splits = jax.random.split(jax.random.key(seed), 7)
    return {
        "queries": draw_queries(jax.random.fold_in(splits[6], 71), 0),
        "cache_kv": draw_cache_kv(jax.random.fold_in(splits[6], 71), 0),
        "lengths": draw_lengths(jax.random.fold_in(splits[6], 71), 0),
        "evict": jax.random.randint(splits[3], (1,), 0, SLOTS).astype(jnp.int32),
        "own_kv": centred(splits[4], (STEPS, 2, SPAN, HEADS * HD), 1.0, 6.0, ((2, 32), (3, 16))),
        "clean_kv": centred(splits[5], (2, SPAN, HEADS * HD), 1.0, 6.0, ((1, 32), (2, 16))),
    }


def attend_head(query_head, key_slots, value_slots, key_own, value_own, valid):
    rows = SPAN // SLOTS
    keys = jnp.concatenate([key_slots, key_own.reshape(SLOTS, rows, HD)], axis=1).astype(jnp.float32)
    values = jnp.concatenate([value_slots, value_own.reshape(SLOTS, rows, HD)], axis=1).astype(jnp.float32)
    mask = jnp.concatenate([valid, jnp.ones((SLOTS, rows), dtype=bool)], axis=1)
    scores = jnp.einsum('qd,jkd->qjk', query_head.astype(jnp.float32), keys) * (1.0 / math.sqrt(HD))
    masked = jnp.where(mask[None], scores, -jnp.inf)
    local = lax.optimization_barrier(jnp.max(masked, axis=2))
    top = lax.optimization_barrier(jnp.max(local, axis=1, keepdims=True))
    weights = jnp.where(mask[None], jnp.exp(masked - local[..., None]), 0.0).astype(jnp.bfloat16)
    part_total = lax.optimization_barrier(jnp.sum(weights.astype(jnp.float32), axis=2))
    part_accum = jnp.einsum('qjk,jkd->qjd', weights.astype(jnp.float32), values)
    scale = jnp.exp(local - top)
    total = lax.optimization_barrier(jnp.sum(scale * part_total, axis=1))
    accum = jnp.einsum('qj,qjd->qd', scale, part_accum)
    return (accum / total[:, None]).astype(jnp.bfloat16)

def one_step(query_step, cache, valid_cache, own):
    width = HEADS * HD
    key_slots = cache[:, 0].reshape(SLOTS, SPAN, HEADS, HD).transpose(2, 0, 1, 3)
    value_slots = cache[:, 1].reshape(SLOTS, SPAN, HEADS, HD).transpose(2, 0, 1, 3)
    key_own = own[0].reshape(SPAN, HEADS, HD).transpose(1, 0, 2)
    value_own = own[1].reshape(SPAN, HEADS, HD).transpose(1, 0, 2)
    query_heads = query_step.reshape(SPAN, HEADS, HD).transpose(1, 0, 2)
    result = lax.map(lambda items: attend_head(items[0], items[1], items[2], items[3], items[4], valid_cache), (query_heads, key_slots, value_slots, key_own, value_own))
    return result.transpose(1, 0, 2).reshape(SPAN, width)

def reference(queries, cache_kv, lengths, evict, own_kv, clean_kv):
    positions = jnp.arange(SPAN, dtype=jnp.int32)
    valid = positions[None, :] < lengths[:, None]
    first = one_step(queries[0], cache_kv, valid, own_kv[0])
    chosen = jnp.arange(SLOTS, dtype=jnp.int32) == evict[0]
    new_cache = jnp.where(chosen[:, None, None, None], clean_kv[None], cache_kv)
    new_valid = jnp.logical_or(valid, chosen[:, None])
    second = one_step(queries[1], new_cache, new_valid, own_kv[1])
    return (jnp.stack([first, second]), new_cache)
```

```python
import math

import jax
import jax.numpy as jnp
from jax import lax
from jax.experimental import pallas as pl
from jax.experimental.pallas import tpu as pltpu
from jax.sharding import PartitionSpec as P

HD = 128
EXP2_SCALE = math.log2(math.e) / math.sqrt(HD)
NEG = -1e30
VMEM = pl.BlockSpec(memory_space=pltpu.VMEM)
SMEM = pl.BlockSpec(memory_space=pltpu.SMEM)
NT = (((1,), (1,)), ((), ()))
NN = (((1,), (0,)), ((), ()))


def split_queries_kernel(q_ref, out_ref):
    for group in range(out_ref.shape[0]):
        for half in range(2):
            start = (group * 2 + half) * HD
            piece = q_ref[:, start:start + HD].astype(jnp.float32)
            for step in range(2):
                part = step * 2 + half
                out_ref[group, part:part + 1, :] = piece[step:step + 1].astype(out_ref.dtype)


def spread_kernel(q_ref, clean_ref, out_ref, rows):
    tokens = q_ref.shape[0]
    for token in range(tokens):
        piece = q_ref[token].astype(jnp.float32)
        for part in range(4):
            rows[token:token + 1, part * HD:(part + 1) * HD] = piece[part:part + 1]
    message = rows[...].astype(out_ref.dtype)
    for dest in range(out_ref.shape[0]):
        out_ref[dest, :, 0:4 * HD] = message
        out_ref[dest, :, 4 * HD:6 * HD] = clean_ref[0]
        out_ref[dest, :, 6 * HD:8 * HD] = clean_ref[1]


def attend_kernel(length_ref, evict_ref, recv_ref, cache_ref, own_ref, clean_ref, out_ref, new_ref):
    devices, rows, _ = recv_ref.shape
    span = cache_ref.shape[2]
    owner = lax.axis_index("ctx") == evict_ref[0]
    length = length_ref[0]

    @pl.when(owner)
    def _():
        for index in range(2):
            lanes = slice((4 + 2 * index) * HD, (6 + 2 * index) * HD)
            new_ref[0, index] = recv_ref[:, :, lanes].reshape(span, 2 * HD)

    @pl.when(jnp.logical_not(owner))
    def _():
        new_ref[...] = cache_ref[...]

    key = lax.broadcasted_iota(jnp.int32, (1, span), 1)
    extra = lax.broadcasted_iota(jnp.int32, (1, HD), 1)
    lane = lax.broadcasted_iota(jnp.int32, (1, HD), 1)
    block_devices = 16
    block = block_devices * rows
    ones = jnp.ones((span, HD), jnp.bfloat16)
    for step in range(2):
        limit = length if step == 0 else jnp.where(owner, 0, length)
        bias = jnp.where(key < limit, 0.0, NEG)
        extra_bias = jnp.where(extra < rows * (1 + step), 0.0, NEG)
        pad = jnp.zeros((HD - 2 * rows, 2 * HD), jnp.bfloat16)
        extra_keys = jnp.concatenate([own_ref[step, 0], clean_ref[0], pad], axis=0)
        extra_values = jnp.concatenate([own_ref[step, 1], clean_ref[1], pad], axis=0)
        for start in range(0, devices, block_devices):
            stats = jnp.zeros((block, HD), jnp.float32)
            out_rows = slice(start * rows, start * rows + block)
            for half in range(2):
                part = step * 2 + half
                lanes = slice(half * HD, (half + 1) * HD)
                query = recv_ref[start:start + block_devices, :, part * HD:(part + 1) * HD].reshape(block, HD)
                scores = lax.dot_general(query, cache_ref[0, 0, :, lanes], NT, preferred_element_type=jnp.float32) + bias
                scores_x = (
                    lax.dot_general(query, extra_keys[:, lanes], NT, preferred_element_type=jnp.float32) + extra_bias
                )
                top = jnp.maximum(
                    jnp.max(scores, axis=1, keepdims=True), jnp.max(scores_x, axis=1, keepdims=True)
                )
                top = jnp.ceil(top)
                weights = jnp.exp2((scores - top) * EXP2_SCALE).astype(jnp.bfloat16)
                weights_x = jnp.exp2((scores_x - top) * EXP2_SCALE).astype(jnp.bfloat16)
                values = jnp.concatenate([cache_ref[0, 1, :, lanes], ones], axis=1)
                values_x = jnp.concatenate([extra_values[:, lanes], ones[:HD]], axis=1)
                accum = lax.dot_general(weights, values, NN, preferred_element_type=jnp.float32)
                accum = accum + lax.dot_general(weights_x, values_x, NN, preferred_element_type=jnp.float32)
                out_ref[out_rows, part * HD:(part + 1) * HD] = accum[:, :HD].astype(jnp.bfloat16)
                total = accum[:, HD:]
                top = jnp.broadcast_to(top, (block, HD))
                top_hi = top.astype(jnp.bfloat16).astype(jnp.float32)
                total_hi = total.astype(jnp.bfloat16).astype(jnp.float32)
                for place, value in enumerate((top_hi, top - top_hi, total_hi, total - total_hi)):
                    stats = jnp.where(lane == 32 * place + half, value, stats)
            out_ref[out_rows, (4 + step) * HD:(5 + step) * HD] = stats.astype(jnp.bfloat16)


def combine_kernel(recv_ref, out_ref):
    devices, rows, _ = recv_ref.shape
    for step in range(2):
        stats = recv_ref[:, :, (4 + step) * HD:(5 + step) * HD].astype(jnp.float32)
        for half in range(2):
            part = step * 2 + half
            local = stats[:, :, half:half + 1] + stats[:, :, 32 + half:33 + half]
            total = stats[:, :, 64 + half:65 + half] + stats[:, :, 96 + half:97 + half]
            top = jnp.max(local, axis=0, keepdims=True)
            scale = jnp.exp2((local - top) * EXP2_SCALE)
            whole = jnp.sum(scale * total, axis=0)
            accum = recv_ref[:, :, part * HD:(part + 1) * HD].astype(jnp.float32)
            result = jnp.sum(scale * accum, axis=0) / whole
            for token in range(rows):
                out_ref[token, part:part + 1, :] = result[token:token + 1].astype(jnp.bfloat16)


def merge_kernel(recv_ref, out_ref):
    for group in range(recv_ref.shape[0]):
        piece = recv_ref[group].astype(jnp.float32)
        for step in range(2):
            for half in range(2):
                start = (group * 2 + half) * HD
                part = step * 2 + half
                out_ref[step:step + 1, start:start + HD] = piece[part:part + 1].astype(jnp.bfloat16)


def call(kernel, out_shape, in_specs, scratch=(), name=None, cost=None):
    several = isinstance(out_shape, (tuple, list))
    return pl.pallas_call(
        kernel,
        out_shape=out_shape,
        in_specs=in_specs,
        out_specs=[VMEM] * len(out_shape) if several else VMEM,
        scratch_shapes=list(scratch),
        compiler_params=pltpu.CompilerParams(vmem_limit_bytes=32 * 1024 * 1024),
        cost_estimate=cost,
        name=name,
    )


def body(queries, cache_kv, lengths, evict, own_kv, clean_kv):
    steps, _, features = queries.shape
    span = cache_kv.shape[2]
    ctx = lax.axis_size("ctx")
    groups = lax.axis_size("head")
    rows = span // ctx
    bf16 = jnp.bfloat16
    split = call(split_queries_kernel, jax.ShapeDtypeStruct((groups, 4, HD), bf16), [VMEM], name="split_queries")(
        queries.reshape(steps, features)
    )
    mine = lax.all_to_all(split, "head", split_axis=0, concat_axis=0, tiled=True)

    def spread(q_ref, clean_ref, out_ref, scratch):
        spread_kernel(q_ref, clean_ref, out_ref, scratch)

    message = call(
        spread,
        jax.ShapeDtypeStruct((ctx, rows, 8 * HD), bf16),
        [VMEM] * 2,
        [pltpu.VMEM((rows, 4 * HD), jnp.float32)],
        name="spread_queries",
    )(mine, clean_kv)
    recv = lax.all_to_all(message, "ctx", split_axis=0, concat_axis=0, tiled=True)
    parts, new_cache = call(
        attend_kernel,
        (
            jax.ShapeDtypeStruct((span, 6 * HD), bf16),
            jax.ShapeDtypeStruct(cache_kv.shape, bf16),
        ),
        [SMEM, SMEM] + [VMEM] * 4,
        name="attend",
    )(lengths, evict, recv, cache_kv, own_kv, clean_kv)
    back = lax.all_to_all(parts.reshape(ctx, rows, 6 * HD), "ctx", split_axis=0, concat_axis=0, tiled=True)
    outputs = call(combine_kernel, jax.ShapeDtypeStruct((groups, 4, HD), bf16), [VMEM], name="combine")(back)
    outputs = lax.all_to_all(outputs, "head", split_axis=0, concat_axis=0, tiled=True)
    attended = call(merge_kernel, jax.ShapeDtypeStruct((steps, features), bf16), [VMEM], name="merge")(outputs)
    return (attended.reshape(steps, 1, features), new_cache)


def solution(mesh):
    in_specs = (
        P(None, ("ctx", "head"), None),
        P("ctx", None, None, "head"),
        P("ctx"),
        P(),
        P(None, None, "ctx", "head"),
        P(None, "ctx", "head"),
    )
    out_specs = (P(None, ("ctx", "head"), None), P("ctx", None, None, "head"))
    return jax.shard_map(body, mesh=mesh, in_specs=in_specs, out_specs=out_specs, check_vma=False)
```

```python
import math

import jax
import jax.numpy as jnp
from jax import lax
from jax.experimental import pallas as pl
from jax.experimental.pallas import tpu as pltpu
from jax.sharding import PartitionSpec as P

HD = 128
PARTS = 4
BACK = 6
EXP2_SCALE = math.log2(math.e) / math.sqrt(HD)
NEG = -1e30
VMEM = pl.BlockSpec(memory_space=pltpu.VMEM)
SMEM = pl.BlockSpec(memory_space=pltpu.SMEM)
NT = (((1,), (1,)), ((), ()))
NN = (((1,), (0,)), ((), ()))


def spread_kernel(q_ref, out_ref, rows):
    count = rows.shape[0]
    for row in range(count):
        group, step, half = row // 4, row // 2 % 2, row % 2
        start = (group * 2 + half) * HD
        rows[row:row + 1, :] = q_ref[step:step + 1, start:start + HD].astype(jnp.float32)
    message = rows[...].astype(out_ref.dtype)
    for dest in range(out_ref.shape[0] // count):
        out_ref[dest * count:(dest + 1) * count, :] = message


def attend_kernel(length_ref, evict_ref, recv_ref, cache_ref, own_ref, clean_ref, out_ref, wide, wide_out):
    span = cache_ref.shape[2]
    rows = clean_ref.shape[1]
    owner = lax.axis_index("ctx") == evict_ref[0]
    length = length_ref[0]
    wide[...] = recv_ref[...].astype(jnp.float32)
    key = lax.broadcasted_iota(jnp.int32, (1, span), 1)
    lane = lax.broadcasted_iota(jnp.int32, (1, HD), 1)
    block = 256
    ones = jnp.ones((span, HD), jnp.bfloat16)
    pad = jnp.zeros((HD - 2 * rows, 2 * HD), jnp.bfloat16)
    for step in range(2):
        limit = length if step == 0 else jnp.where(owner, 0, length)
        bias = jnp.where(key < limit, 0.0, NEG)
        extra_bias = jnp.where(lane < rows * (1 + step), 0.0, NEG)
        extra_keys = jnp.concatenate([own_ref[step, 0], clean_ref[0], pad], axis=0)
        extra_values = jnp.concatenate([own_ref[step, 1], clean_ref[1], pad], axis=0)
        for start in range(0, span, block):
            stats = jnp.zeros((block, HD), jnp.float32)
            for half in range(2):
                part = step * 2 + half
                lanes = slice(half * HD, (half + 1) * HD)
                query = wide[pl.ds(start * PARTS + part, block, stride=PARTS), :].astype(jnp.bfloat16)
                scores = lax.dot_general(query, cache_ref[0, 0, :, lanes], NT, preferred_element_type=jnp.float32) + bias
                scores_x = (
                    lax.dot_general(query, extra_keys[:, lanes], NT, preferred_element_type=jnp.float32) + extra_bias
                )
                top = jnp.maximum(
                    jnp.max(scores, axis=1, keepdims=True), jnp.max(scores_x, axis=1, keepdims=True)
                )
                top = jnp.ceil(top)
                weights = jnp.exp2((scores - top) * EXP2_SCALE).astype(jnp.bfloat16)
                weights_x = jnp.exp2((scores_x - top) * EXP2_SCALE).astype(jnp.bfloat16)
                values = jnp.concatenate([cache_ref[0, 1, :, lanes], ones], axis=1)
                values_x = jnp.concatenate([extra_values[:, lanes], ones[:HD]], axis=1)
                accum = lax.dot_general(weights, values, NN, preferred_element_type=jnp.float32)
                accum = accum + lax.dot_general(weights_x, values_x, NN, preferred_element_type=jnp.float32)
                wide_out[pl.ds(start * BACK + half * 2 + step, block, stride=BACK), :] = accum[:, :HD]
                total = accum[:, HD:]
                top = jnp.broadcast_to(top, (block, HD))
                top_hi = top.astype(jnp.bfloat16).astype(jnp.float32)
                total_hi = total.astype(jnp.bfloat16).astype(jnp.float32)
                for place, value in enumerate((top_hi, top - top_hi, total_hi, total - total_hi)):
                    stats = jnp.where(lane == 32 * place + half, value, stats)
            wide_out[pl.ds(start * BACK + 4 + step, block, stride=BACK), :] = stats
    out_ref[...] = wide_out[...].astype(jnp.bfloat16)


def combine_kernel(recv_ref, out_ref, wide):
    groups = out_ref.shape[1] // (2 * HD)
    senders = recv_ref.shape[0] // BACK
    devices = senders // groups
    wide[...] = recv_ref[...].astype(jnp.float32)

    def rows_of(place):
        return wide[pl.ds(place, senders, stride=BACK), :].reshape(devices, groups, HD)

    for step in range(2):
        stats = rows_of(4 + step)
        for half in range(2):
            local = stats[:, :, half:half + 1] + stats[:, :, 32 + half:33 + half]
            total = stats[:, :, 64 + half:65 + half] + stats[:, :, 96 + half:97 + half]
            top = jnp.max(local, axis=0, keepdims=True)
            scale = jnp.exp2((local - top) * EXP2_SCALE)
            whole = jnp.sum(scale * total, axis=0)
            result = jnp.sum(scale * rows_of(half * 2 + step), axis=0) / whole
            for group in range(groups):
                begin = (group * 2 + half) * HD
                out_ref[step:step + 1, begin:begin + HD] = result[group:group + 1].astype(jnp.bfloat16)


def renew_kernel(evict_ref, clean_ref, cache_ref, new_ref):
    devices, _, rows, _ = clean_ref.shape
    owner = lax.axis_index("ctx") == evict_ref[0]

    @pl.when(owner)
    def _():
        for device in range(devices):
            for index in range(2):
                new_ref[0, index, device * rows:(device + 1) * rows, :] = clean_ref[device, index]

    @pl.when(jnp.logical_not(owner))
    def _():
        new_ref[...] = cache_ref[...]


def call(kernel, out_shape, in_specs, scratch=(), name=None):
    return pl.pallas_call(
        kernel,
        out_shape=out_shape,
        in_specs=in_specs,
        out_specs=VMEM,
        scratch_shapes=list(scratch),
        compiler_params=pltpu.CompilerParams(vmem_limit_bytes=32 * 1024 * 1024),
        name=name,
    )


def body(queries, cache_kv, lengths, evict, own_kv, clean_kv):
    steps, _, features = queries.shape
    span = cache_kv.shape[2]
    ctx = lax.axis_size("ctx")
    groups = lax.axis_size("head")
    bf16, f32 = jnp.bfloat16, jnp.float32
    message = call(
        spread_kernel,
        jax.ShapeDtypeStruct((span * PARTS, HD), bf16),
        [VMEM],
        [pltpu.VMEM((groups * PARTS, HD), f32)],
        name="spread_queries",
    )(queries.reshape(steps, features))
    recv = lax.all_to_all(
        message.reshape(span, PARTS, HD), ("ctx", "head"), split_axis=0, concat_axis=0, tiled=True
    ).reshape(span * PARTS, HD)
    parts = call(
        attend_kernel,
        jax.ShapeDtypeStruct((span * BACK, HD), bf16),
        [SMEM, SMEM] + [VMEM] * 4,
        [pltpu.VMEM((span * PARTS, HD), f32), pltpu.VMEM((span * BACK, HD), f32)],
        name="attend",
    )(lengths, evict, recv, cache_kv, own_kv, clean_kv)
    back = lax.all_to_all(
        parts.reshape(span * BACK // 2, 2, HD), ("ctx", "head"), split_axis=0, concat_axis=0, tiled=True
    ).reshape(span * BACK, HD)
    attended = call(
        combine_kernel,
        jax.ShapeDtypeStruct((steps, features), bf16),
        [VMEM],
        [pltpu.VMEM((span * BACK, HD), f32)],
        name="combine",
    )(back)
    copies = jnp.broadcast_to(clean_kv[None], (ctx,) + clean_kv.shape)
    _, copies = lax.optimization_barrier((recv, copies))
    whole = lax.all_to_all(copies, "ctx", split_axis=0, concat_axis=0, tiled=True)
    new_cache = call(
        renew_kernel, jax.ShapeDtypeStruct(cache_kv.shape, bf16), [SMEM, VMEM, VMEM], name="renew_cache"
    )(evict, whole, cache_kv)
    return (attended.reshape(steps, 1, features), new_cache)


def solution(mesh):
    in_specs = (
        P(None, ("ctx", "head"), None),
        P("ctx", None, None, "head"),
        P("ctx"),
        P(),
        P(None, None, "ctx", "head"),
        P(None, "ctx", "head"),
    )
    out_specs = (P(None, ("ctx", "head"), None), P("ctx", None, None, "head"))
    return jax.shard_map(body, mesh=mesh, in_specs=in_specs, out_specs=out_specs, check_vma=False)
```

```python
import math

import jax
import jax.numpy as jnp
from jax import lax
from jax.experimental import pallas as pl
from jax.experimental.pallas import tpu as pltpu
from jax.sharding import PartitionSpec as P

HD = 128
PARTS = 4
BACK = 6
EXP2_SCALE = math.log2(math.e) / math.sqrt(HD)
NEG = -1e30
VMEM = pl.BlockSpec(memory_space=pltpu.VMEM)
SMEM = pl.BlockSpec(memory_space=pltpu.SMEM)
NT = (((1,), (1,)), ((), ()))
NN = (((1,), (0,)), ((), ()))


def spread_kernel(q_ref, out_ref, rows):
    repeat = rows.shape[0] // PARTS
    groups = q_ref.shape[1] // (2 * HD)
    count = out_ref.shape[0] // groups
    for group in range(groups):
        for part in range(PARTS):
            step, start = part // 2, (group * 2 + part % 2) * HD
            piece = q_ref[step:step + 1, start:start + HD].astype(jnp.float32)
            for copy in range(repeat):
                rows[copy * PARTS + part:copy * PARTS + part + 1, :] = piece
        message = rows[...].astype(out_ref.dtype)
        for place in range(group * count, (group + 1) * count, PARTS * repeat):
            out_ref[place:place + PARTS * repeat, :] = message


def attend_kernel(length_ref, evict_ref, recv_ref, cache_ref, own_ref, clean_ref, out_ref, wide, wide_out):
    span = cache_ref.shape[2]
    rows = clean_ref.shape[1]
    owner = lax.axis_index("ctx") == evict_ref[0]
    length = length_ref[0]
    wide[...] = recv_ref[...].astype(jnp.float32)
    key = lax.broadcasted_iota(jnp.int32, (1, span), 1)
    lane = lax.broadcasted_iota(jnp.int32, (1, HD), 1)
    block = 256
    ones = jnp.ones((span, HD), jnp.bfloat16)
    pad = jnp.zeros((HD - 2 * rows, 2 * HD), jnp.bfloat16)
    for step in range(2):
        limit = length if step == 0 else jnp.where(owner, 0, length)
        bias = jnp.where(key < limit, 0.0, NEG)
        extra_bias = jnp.where(lane < rows * (1 + step), 0.0, NEG)
        extra_keys = jnp.concatenate([own_ref[step, 0], clean_ref[0], pad], axis=0)
        extra_values = jnp.concatenate([own_ref[step, 1], clean_ref[1], pad], axis=0)
        for start in range(0, span, block):
            stats = jnp.zeros((block, HD), jnp.float32)
            for half in range(2):
                part = step * 2 + half
                lanes = slice(half * HD, (half + 1) * HD)
                query = wide[pl.ds(start * PARTS + part, block, stride=PARTS), :].astype(jnp.bfloat16)
                scores = lax.dot_general(query, cache_ref[0, 0, :, lanes], NT, preferred_element_type=jnp.float32) + bias
                scores_x = (
                    lax.dot_general(query, extra_keys[:, lanes], NT, preferred_element_type=jnp.float32) + extra_bias
                )
                top = jnp.maximum(
                    jnp.max(scores, axis=1, keepdims=True), jnp.max(scores_x, axis=1, keepdims=True)
                )
                top = jnp.ceil(top)
                weights = jnp.exp2((scores - top) * EXP2_SCALE).astype(jnp.bfloat16)
                weights_x = jnp.exp2((scores_x - top) * EXP2_SCALE).astype(jnp.bfloat16)
                values = jnp.concatenate([cache_ref[0, 1, :, lanes], ones], axis=1)
                values_x = jnp.concatenate([extra_values[:, lanes], ones[:HD]], axis=1)
                accum = lax.dot_general(weights, values, NN, preferred_element_type=jnp.float32)
                accum = accum + lax.dot_general(weights_x, values_x, NN, preferred_element_type=jnp.float32)
                wide_out[pl.ds(start * BACK + half * 2 + step, block, stride=BACK), :] = accum[:, :HD]
                total = accum[:, HD:]
                top = jnp.broadcast_to(top, (block, HD))
                top_hi = top.astype(jnp.bfloat16).astype(jnp.float32)
                total_hi = total.astype(jnp.bfloat16).astype(jnp.float32)
                for place, value in enumerate((top_hi, top - top_hi, total_hi, total - total_hi)):
                    stats = jnp.where(lane == 32 * place + half, value, stats)
            wide_out[pl.ds(start * BACK + 4 + step, block, stride=BACK), :] = stats
    out_ref[...] = wide_out[...].astype(jnp.bfloat16)


def combine_kernel(recv_ref, out_ref, wide):
    groups = out_ref.shape[1] // (2 * HD)
    senders = recv_ref.shape[0] // BACK
    devices = senders // groups
    wide[...] = recv_ref[...].astype(jnp.float32)

    def rows_of(place):
        return wide[pl.ds(place, senders, stride=BACK), :].reshape(groups, devices, HD)

    for step in range(2):
        stats = rows_of(4 + step)
        for half in range(2):
            local = stats[:, :, half:half + 1] + stats[:, :, 32 + half:33 + half]
            total = stats[:, :, 64 + half:65 + half] + stats[:, :, 96 + half:97 + half]
            top = jnp.max(local, axis=1, keepdims=True)
            scale = jnp.exp2((local - top) * EXP2_SCALE)
            whole = jnp.sum(scale * total, axis=1, keepdims=True)
            result = jnp.sum(scale * rows_of(half * 2 + step), axis=1, keepdims=True) / whole
            for group in range(groups):
                begin = (group * 2 + half) * HD
                out_ref[step:step + 1, begin:begin + HD] = result[group].astype(jnp.bfloat16)


def renew_kernel(evict_ref, *refs):
    *gathered, cache_ref, new_ref = refs
    runs, depth = gathered[0].shape[0], len(gathered)
    rows = gathered[0].shape[2]
    me = lax.axis_index("ctx")
    owner = me == evict_ref[0]

    @pl.when(owner)
    def _():
        for across in range(depth):
            for along in range(runs):
                source = (me // depth + along) % runs * depth + (me % depth + across) % depth
                place = pl.ds(pl.multiple_of(source * rows, rows), rows)
                for index in range(2):
                    new_ref[0, index, place, :] = gathered[across][along, index]

    @pl.when(jnp.logical_not(owner))
    def _():
        new_ref[...] = cache_ref[...]


def call(kernel, out_shape, in_specs, scratch=(), name=None):
    return pl.pallas_call(
        kernel,
        out_shape=out_shape,
        in_specs=in_specs,
        out_specs=VMEM,
        scratch_shapes=list(scratch),
        compiler_params=pltpu.CompilerParams(vmem_limit_bytes=32 * 1024 * 1024),
        name=name,
    )


def body(queries, cache_kv, lengths, evict, own_kv, clean_kv):
    steps, _, features = queries.shape
    span = cache_kv.shape[2]
    ctx = lax.axis_size("ctx")
    groups = lax.axis_size("head")
    bf16, f32 = jnp.bfloat16, jnp.float32
    message = call(
        spread_kernel,
        jax.ShapeDtypeStruct((span * PARTS, HD), bf16),
        [VMEM],
        [pltpu.VMEM((4 * PARTS, HD), f32)],
        name="spread_queries",
    )(queries.reshape(steps, features))
    recv = lax.all_to_all(
        message.reshape(span, PARTS, HD), ("head", "ctx"), split_axis=0, concat_axis=0, tiled=True
    ).reshape(span * PARTS, HD)
    parts = call(
        attend_kernel,
        jax.ShapeDtypeStruct((span * BACK, HD), bf16),
        [SMEM, SMEM] + [VMEM] * 4,
        [pltpu.VMEM((span * PARTS, HD), f32), pltpu.VMEM((span * BACK, HD), f32)],
        name="attend",
    )(lengths, evict, recv, cache_kv, own_kv, clean_kv)
    back = lax.all_to_all(
        parts.reshape(span * BACK // 2, 2, HD), ("head", "ctx"), split_axis=0, concat_axis=0, tiled=True
    ).reshape(span * BACK, HD)
    attended = call(
        combine_kernel,
        jax.ShapeDtypeStruct((steps, features), bf16),
        [VMEM],
        [pltpu.VMEM((span * BACK, HD), f32)],
        name="combine",
    )(back)
    depth = 4
    runs = ctx // depth

    def fetch(array, along, across):
        pairs = [
            ((me // depth + along) % runs * depth + (me % depth + across) % depth, me) for me in range(ctx)
        ]
        return lax.ppermute(array, "ctx", pairs)

    near = jnp.stack([clean_kv] + [fetch(clean_kv, along, 0) for along in range(1, runs)])
    gathered = [near] + [fetch(near, 0, across) for across in range(1, depth)]
    new_cache = call(
        renew_kernel,
        jax.ShapeDtypeStruct(cache_kv.shape, bf16),
        [SMEM] + [VMEM] * (depth + 1),
        name="renew_cache",
    )(evict, *gathered, cache_kv)
    return (attended.reshape(steps, 1, features), new_cache)


def solution(mesh):
    in_specs = (
        P(None, ("ctx", "head"), None),
        P("ctx", None, None, "head"),
        P("ctx"),
        P(),
        P(None, None, "ctx", "head"),
        P(None, "ctx", "head"),
    )
    out_specs = (P(None, ("ctx", "head"), None), P("ctx", None, None, "head"))
    return jax.shard_map(body, mesh=mesh, in_specs=in_specs, out_specs=out_specs, check_vma=False)
```

```python
import math

import jax
import jax.numpy as jnp
from jax import lax
from jax.experimental import pallas as pl
from jax.experimental.pallas import tpu as pltpu
from jax.sharding import PartitionSpec as P

HD = 128
PARTS = 4
BACK = 6
EXP2_SCALE = math.log2(math.e) / math.sqrt(HD)
NEG = -1e30
VMEM = pl.BlockSpec(memory_space=pltpu.VMEM)
SMEM = pl.BlockSpec(memory_space=pltpu.SMEM)
NT = (((1,), (1,)), ((), ()))
NN = (((1,), (0,)), ((), ()))


def spread_kernel(q_ref, out_ref, rows):
    repeat = rows.shape[0] // PARTS
    groups = q_ref.shape[1] // (2 * HD)
    count = out_ref.shape[0] // groups
    for group in range(groups):
        for part in range(PARTS):
            step, start = part // 2, (group * 2 + part % 2) * HD
            piece = q_ref[step:step + 1, start:start + HD].astype(jnp.float32)
            for copy in range(repeat):
                rows[copy * PARTS + part:copy * PARTS + part + 1, :] = piece
        message = rows[...].astype(out_ref.dtype)
        for place in range(group * count, (group + 1) * count, PARTS * repeat):
            out_ref[place:place + PARTS * repeat, :] = message


def attend_kernel(length_ref, evict_ref, recv_ref, cache_ref, own_ref, clean_ref, out_ref, wide, wide_out):
    span = cache_ref.shape[2]
    rows = clean_ref.shape[1]
    owner = lax.axis_index("ctx") == evict_ref[0]
    length = length_ref[0]
    wide[...] = recv_ref[...].astype(jnp.float32)
    key = lax.broadcasted_iota(jnp.int32, (1, span), 1)
    lane = lax.broadcasted_iota(jnp.int32, (1, HD), 1)
    block = 256
    ones = jnp.ones((span, HD), jnp.bfloat16)
    pad = jnp.zeros((HD - 2 * rows, 2 * HD), jnp.bfloat16)
    for step in range(2):
        limit = length if step == 0 else jnp.where(owner, 0, length)
        bias = jnp.where(key < limit, 0.0, NEG)
        extra_bias = jnp.where(lane < rows * (1 + step), 0.0, NEG)
        extra_keys = jnp.concatenate([own_ref[step, 0], clean_ref[0], pad], axis=0)
        extra_values = jnp.concatenate([own_ref[step, 1], clean_ref[1], pad], axis=0)
        for start in range(0, span, block):
            stats = jnp.zeros((block, HD), jnp.float32)
            for half in range(2):
                part = step * 2 + half
                lanes = slice(half * HD, (half + 1) * HD)
                query = wide[pl.ds(start * PARTS + part, block, stride=PARTS), :].astype(jnp.bfloat16)
                scores = lax.dot_general(query, cache_ref[0, 0, :, lanes], NT, preferred_element_type=jnp.float32) + bias
                scores_x = (
                    lax.dot_general(query, extra_keys[:, lanes], NT, preferred_element_type=jnp.float32) + extra_bias
                )
                top = jnp.maximum(
                    jnp.max(scores, axis=1, keepdims=True), jnp.max(scores_x, axis=1, keepdims=True)
                )
                top = jnp.ceil(top)
                weights = jnp.exp2((scores - top) * EXP2_SCALE).astype(jnp.bfloat16)
                weights_x = jnp.exp2((scores_x - top) * EXP2_SCALE).astype(jnp.bfloat16)
                values = jnp.concatenate([cache_ref[0, 1, :, lanes], ones], axis=1)
                values_x = jnp.concatenate([extra_values[:, lanes], ones[:HD]], axis=1)
                accum = lax.dot_general(weights, values, NN, preferred_element_type=jnp.float32)
                accum = accum + lax.dot_general(weights_x, values_x, NN, preferred_element_type=jnp.float32)
                wide_out[pl.ds(start * BACK + half * 2 + step, block, stride=BACK), :] = accum[:, :HD]
                total = accum[:, HD:]
                top = jnp.broadcast_to(top, (block, HD))
                top_hi = top.astype(jnp.bfloat16).astype(jnp.float32)
                total_hi = total.astype(jnp.bfloat16).astype(jnp.float32)
                for place, value in enumerate((top_hi, top - top_hi, total_hi, total - total_hi)):
                    stats = jnp.where(lane == 32 * place + half, value, stats)
            wide_out[pl.ds(start * BACK + 4 + step, block, stride=BACK), :] = stats
    out_ref[...] = wide_out[...].astype(jnp.bfloat16)


def combine_kernel(recv_ref, out_ref, wide):
    groups = out_ref.shape[1] // (2 * HD)
    senders = recv_ref.shape[0] // BACK
    devices = senders // groups
    wide[...] = recv_ref[...].astype(jnp.float32)

    def rows_of(place):
        return wide[pl.ds(place, senders, stride=BACK), :].reshape(groups, devices, HD)

    for step in range(2):
        stats = rows_of(4 + step)
        for half in range(2):
            local = stats[:, :, half:half + 1] + stats[:, :, 32 + half:33 + half]
            total = stats[:, :, 64 + half:65 + half] + stats[:, :, 96 + half:97 + half]
            top = jnp.max(local, axis=1, keepdims=True)
            scale = jnp.exp2((local - top) * EXP2_SCALE)
            whole = jnp.sum(scale * total, axis=1, keepdims=True)
            result = jnp.sum(scale * rows_of(half * 2 + step), axis=1, keepdims=True) / whole
            for group in range(groups):
                begin = (group * 2 + half) * HD
                out_ref[step:step + 1, begin:begin + HD] = result[group].astype(jnp.bfloat16)


def renew_kernel(evict_ref, clean_ref, cache_ref, new_ref):
    devices, _, rows, _ = clean_ref.shape
    owner = lax.axis_index("ctx") == evict_ref[0]

    @pl.when(owner)
    def _():
        for device in range(devices):
            for index in range(2):
                new_ref[0, index, device * rows:(device + 1) * rows, :] = clean_ref[device, index]

    @pl.when(jnp.logical_not(owner))
    def _():
        new_ref[...] = cache_ref[...]


def call(kernel, out_shape, in_specs, scratch=(), name=None):
    return pl.pallas_call(
        kernel,
        out_shape=out_shape,
        in_specs=in_specs,
        out_specs=VMEM,
        scratch_shapes=list(scratch),
        compiler_params=pltpu.CompilerParams(vmem_limit_bytes=32 * 1024 * 1024),
        name=name,
    )


def body(queries, cache_kv, lengths, evict, own_kv, clean_kv):
    steps, _, features = queries.shape
    span = cache_kv.shape[2]
    ctx = lax.axis_size("ctx")
    groups = lax.axis_size("head")
    bf16, f32 = jnp.bfloat16, jnp.float32
    message = call(
        spread_kernel,
        jax.ShapeDtypeStruct((span * PARTS, HD), bf16),
        [VMEM],
        [pltpu.VMEM((4 * PARTS, HD), f32)],
        name="spread_queries",
    )(queries.reshape(steps, features))
    _, clean_later = lax.optimization_barrier((message, clean_kv))
    copies = jnp.broadcast_to(clean_later[None], (ctx,) + clean_kv.shape)
    whole = lax.all_to_all(copies, "ctx", split_axis=0, concat_axis=0, tiled=True)
    recv = lax.all_to_all(
        message.reshape(span, PARTS, HD), ("head", "ctx"), split_axis=0, concat_axis=0, tiled=True
    ).reshape(span * PARTS, HD)
    parts = call(
        attend_kernel,
        jax.ShapeDtypeStruct((span * BACK, HD), bf16),
        [SMEM, SMEM] + [VMEM] * 4,
        [pltpu.VMEM((span * PARTS, HD), f32), pltpu.VMEM((span * BACK, HD), f32)],
        name="attend",
    )(lengths, evict, recv, cache_kv, own_kv, clean_kv)
    back = lax.all_to_all(
        parts.reshape(span * BACK // 2, 2, HD), ("head", "ctx"), split_axis=0, concat_axis=0, tiled=True
    ).reshape(span * BACK, HD)
    back, whole = lax.optimization_barrier((back, whole))
    attended = call(
        combine_kernel,
        jax.ShapeDtypeStruct((steps, features), bf16),
        [VMEM],
        [pltpu.VMEM((span * BACK, HD), f32)],
        name="combine",
    )(back)
    new_cache = call(
        renew_kernel, jax.ShapeDtypeStruct(cache_kv.shape, bf16), [SMEM, VMEM, VMEM], name="renew_cache"
    )(evict, whole, cache_kv)
    return (attended.reshape(steps, 1, features), new_cache)


def solution(mesh):
    in_specs = (
        P(None, ("ctx", "head"), None),
        P("ctx", None, None, "head"),
        P("ctx"),
        P(),
        P(None, None, "ctx", "head"),
        P(None, "ctx", "head"),
    )
    out_specs = (P(None, ("ctx", "head"), None), P("ctx", None, None, "head"))
    return jax.shard_map(body, mesh=mesh, in_specs=in_specs, out_specs=out_specs, check_vma=False)
```

```python
import math

import jax
import jax.numpy as jnp
from jax import lax
from jax.experimental import pallas as pl
from jax.experimental.pallas import tpu as pltpu
from jax.sharding import PartitionSpec as P

HD = 128
PARTS = 4
BACK = 6
EXP2_SCALE = math.log2(math.e) / math.sqrt(HD)
NEG = -1e30
VMEM = pl.BlockSpec(memory_space=pltpu.VMEM)
SMEM = pl.BlockSpec(memory_space=pltpu.SMEM)
NT = (((1,), (1,)), ((), ()))
NN = (((1,), (0,)), ((), ()))


def spread_kernel(q_ref, out_ref, rows):
    repeat = rows.shape[0] // PARTS
    groups = q_ref.shape[1] // (2 * HD)
    count = out_ref.shape[0] // groups
    for group in range(groups):
        for part in range(PARTS):
            step, start = part // 2, (group * 2 + part % 2) * HD
            piece = q_ref[step:step + 1, start:start + HD].astype(jnp.float32)
            for copy in range(repeat):
                rows[copy * PARTS + part:copy * PARTS + part + 1, :] = piece
        message = rows[...].astype(out_ref.dtype)
        for place in range(group * count, (group + 1) * count, PARTS * repeat):
            out_ref[place:place + PARTS * repeat, :] = message


def attend_kernel(length_ref, evict_ref, recv_ref, cache_ref, own_ref, clean_ref, out_ref, wide, wide_out):
    span = cache_ref.shape[2]
    rows = clean_ref.shape[1]
    owner = lax.axis_index("ctx") == evict_ref[0]
    length = length_ref[0]
    wide[...] = recv_ref[...].astype(jnp.float32)
    key = lax.broadcasted_iota(jnp.int32, (1, span), 1)
    lane = lax.broadcasted_iota(jnp.int32, (1, HD), 1)
    block = 256
    ones = jnp.ones((span, HD), jnp.bfloat16)
    pad = jnp.zeros((HD - 2 * rows, 2 * HD), jnp.bfloat16)
    for step in range(2):
        limit = length if step == 0 else jnp.where(owner, 0, length)
        bias = jnp.where(key < limit, 0.0, NEG)
        extra_bias = jnp.where(lane < rows * (1 + step), 0.0, NEG)
        extra_keys = jnp.concatenate([own_ref[step, 0], clean_ref[0], pad], axis=0)
        extra_values = jnp.concatenate([own_ref[step, 1], clean_ref[1], pad], axis=0)
        for start in range(0, span, block):
            stats = jnp.zeros((block, HD), jnp.float32)
            for half in range(2):
                part = step * 2 + half
                lanes = slice(half * HD, (half + 1) * HD)
                query = wide[pl.ds(start * PARTS + part, block, stride=PARTS), :].astype(jnp.bfloat16)
                scores = lax.dot_general(query, cache_ref[0, 0, :, lanes], NT, preferred_element_type=jnp.float32) + bias
                scores_x = (
                    lax.dot_general(query, extra_keys[:, lanes], NT, preferred_element_type=jnp.float32) + extra_bias
                )
                top = jnp.maximum(
                    jnp.max(scores, axis=1, keepdims=True), jnp.max(scores_x, axis=1, keepdims=True)
                )
                top = jnp.ceil(top)
                weights = jnp.exp2((scores - top) * EXP2_SCALE).astype(jnp.bfloat16)
                weights_x = jnp.exp2((scores_x - top) * EXP2_SCALE).astype(jnp.bfloat16)
                values = jnp.concatenate([cache_ref[0, 1, :, lanes], ones], axis=1)
                values_x = jnp.concatenate([extra_values[:, lanes], ones[:HD]], axis=1)
                accum = lax.dot_general(weights, values, NN, preferred_element_type=jnp.float32)
                accum = accum + lax.dot_general(weights_x, values_x, NN, preferred_element_type=jnp.float32)
                wide_out[pl.ds(start * BACK + half * 2 + step, block, stride=BACK), :] = accum[:, :HD]
                total = accum[:, HD:]
                top = jnp.broadcast_to(top, (block, HD))
                top_hi = top.astype(jnp.bfloat16).astype(jnp.float32)
                total_hi = total.astype(jnp.bfloat16).astype(jnp.float32)
                for place, value in enumerate((top_hi, top - top_hi, total_hi, total - total_hi)):
                    stats = jnp.where(lane == 32 * place + half, value, stats)
            wide_out[pl.ds(start * BACK + 4 + step, block, stride=BACK), :] = stats
    out_ref[...] = wide_out[...].astype(jnp.bfloat16)


def combine_kernel(recv_ref, out_ref, wide):
    groups = out_ref.shape[1] // (2 * HD)
    senders = recv_ref.shape[0] // BACK
    devices = senders // groups
    wide[...] = recv_ref[...].astype(jnp.float32)

    def rows_of(place):
        return wide[pl.ds(place, senders, stride=BACK), :].reshape(groups, devices, HD)

    for step in range(2):
        stats = rows_of(4 + step)
        for half in range(2):
            local = stats[:, :, half:half + 1] + stats[:, :, 32 + half:33 + half]
            total = stats[:, :, 64 + half:65 + half] + stats[:, :, 96 + half:97 + half]
            top = jnp.max(local, axis=1, keepdims=True)
            scale = jnp.exp2((local - top) * EXP2_SCALE)
            whole = jnp.sum(scale * total, axis=1, keepdims=True)
            result = jnp.sum(scale * rows_of(half * 2 + step), axis=1, keepdims=True) / whole
            for group in range(groups):
                begin = (group * 2 + half) * HD
                out_ref[step:step + 1, begin:begin + HD] = result[group].astype(jnp.bfloat16)


def renew_kernel(evict_ref, near_ref, far_ref, cache_ref, new_ref):
    entries, _, rows, _ = near_ref.shape
    me = lax.axis_index("ctx")
    owner = me == evict_ref[0]

    @pl.when(owner)
    def _():
        for last, ref in enumerate((near_ref, far_ref)):
            for entry in range(entries):
                mask = sum(1 << (4 - bit) for bit in range(4) if entry >> bit & 1) + last
                place = pl.ds(pl.multiple_of((me ^ mask) * rows, rows), rows)
                for index in range(2):
                    new_ref[0, index, place, :] = ref[entry, index]

    @pl.when(jnp.logical_not(owner))
    def _():
        new_ref[...] = cache_ref[...]


def call(kernel, out_shape, in_specs, scratch=(), name=None):
    return pl.pallas_call(
        kernel,
        out_shape=out_shape,
        in_specs=in_specs,
        out_specs=VMEM,
        scratch_shapes=list(scratch),
        compiler_params=pltpu.CompilerParams(vmem_limit_bytes=32 * 1024 * 1024),
        name=name,
    )


def body(queries, cache_kv, lengths, evict, own_kv, clean_kv):
    steps, _, features = queries.shape
    span = cache_kv.shape[2]
    ctx = lax.axis_size("ctx")
    groups = lax.axis_size("head")
    bf16, f32 = jnp.bfloat16, jnp.float32
    message = call(
        spread_kernel,
        jax.ShapeDtypeStruct((span * PARTS, HD), bf16),
        [VMEM],
        [pltpu.VMEM((4 * PARTS, HD), f32)],
        name="spread_queries",
    )(queries.reshape(steps, features))
    recv = lax.all_to_all(
        message.reshape(span, PARTS, HD), ("head", "ctx"), split_axis=0, concat_axis=0, tiled=True
    ).reshape(span * PARTS, HD)
    parts = call(
        attend_kernel,
        jax.ShapeDtypeStruct((span * BACK, HD), bf16),
        [SMEM, SMEM] + [VMEM] * 4,
        [pltpu.VMEM((span * PARTS, HD), f32), pltpu.VMEM((span * BACK, HD), f32)],
        name="attend",
    )(lengths, evict, recv, cache_kv, own_kv, clean_kv)
    back = lax.all_to_all(
        parts.reshape(span * BACK // 2, 2, HD), ("head", "ctx"), split_axis=0, concat_axis=0, tiled=True
    ).reshape(span * BACK, HD)
    attended = call(
        combine_kernel,
        jax.ShapeDtypeStruct((steps, features), bf16),
        [VMEM],
        [pltpu.VMEM((span * BACK, HD), f32)],
        name="combine",
    )(back)
    near = clean_kv[None]
    for mask in (16, 8, 4, 2):
        near = jnp.concatenate([near, lax.ppermute(near, "ctx", [(me, me ^ mask) for me in range(ctx)])])
    far = lax.ppermute(near, "ctx", [(me, me ^ 1) for me in range(ctx)])
    new_cache = call(
        renew_kernel, jax.ShapeDtypeStruct(cache_kv.shape, bf16), [SMEM] + [VMEM] * 3, name="renew_cache"
    )(evict, near, far, cache_kv)
    return (attended.reshape(steps, 1, features), new_cache)


def solution(mesh):
    in_specs = (
        P(None, ("ctx", "head"), None),
        P("ctx", None, None, "head"),
        P("ctx"),
        P(),
        P(None, None, "ctx", "head"),
        P(None, "ctx", "head"),
    )
    out_specs = (P(None, ("ctx", "head"), None), P("ctx", None, None, "head"))
    return jax.shard_map(body, mesh=mesh, in_specs=in_specs, out_specs=out_specs, check_vma=False)
```

```python
import math

import jax
import jax.numpy as jnp
from jax import lax
from jax.experimental import pallas as pl
from jax.experimental.pallas import tpu as pltpu
from jax.sharding import PartitionSpec as P

HD = 128
PARTS = 4
BACK = 6
EXP2_SCALE = math.log2(math.e) / math.sqrt(HD)
NEG = -1e30
VMEM = pl.BlockSpec(memory_space=pltpu.VMEM)
SMEM = pl.BlockSpec(memory_space=pltpu.SMEM)
NT = (((1,), (1,)), ((), ()))
NN = (((1,), (0,)), ((), ()))


def spread_kernel(q_ref, out_ref, rows):
    count = rows.shape[0]
    for row in range(count):
        group, step, half = row // 4, row // 2 % 2, row % 2
        start = (group * 2 + half) * HD
        rows[row:row + 1, :] = q_ref[step:step + 1, start:start + HD].astype(jnp.float32)
    message = rows[...].astype(out_ref.dtype)
    for dest in range(out_ref.shape[0] // count):
        out_ref[dest * count:(dest + 1) * count, :] = message


def pack_kernel(length_ref, cache_ref, own_ref, clean_ref, pack_ref, copies_ref):
    span, rows = cache_ref.shape[2], clean_ref.shape[1]
    pack_ref[0:span, :] = cache_ref[0, 0]
    pack_ref[span:2 * span, :] = cache_ref[0, 1]
    place = 2 * span
    for step in range(2):
        for index in range(2):
            pack_ref[place:place + rows, :] = own_ref[step, index]
            place += rows
    for index in range(2):
        pack_ref[place:place + rows, :] = clean_ref[index]
        place += rows
    length = length_ref[0]
    lane = lax.broadcasted_iota(jnp.int32, (rows, 2 * HD), 1)
    digits = jnp.where(lane < HD, length // 8, length % 8)
    pack_ref[place:place + rows, :] = digits.astype(jnp.float32).astype(pack_ref.dtype)
    for dest in range(copies_ref.shape[0]):
        copies_ref[dest] = clean_ref[...]


def attend_kernel(length_ref, evict_ref, recv_ref, cache_ref, own_ref, clean_ref, far_ref, out_ref, wide, wide_out):
    span = cache_ref.shape[2]
    rows = clean_ref.shape[1]
    block = recv_ref.shape[0] // PARTS
    me = lax.axis_index("ca") * 2 + lax.axis_index("cb")
    owner = me == evict_ref[0]
    far_owner = (me ^ 1) == evict_ref[0]
    length = length_ref[0]
    wide[...] = recv_ref[...].astype(jnp.float32)
    key = lax.broadcasted_iota(jnp.int32, (1, span), 1)
    lane = lax.broadcasted_iota(jnp.int32, (1, HD), 1)
    tail = 2 * span
    digits = far_ref[tail + 6 * rows:tail + 7 * rows, :].astype(jnp.float32)[0:1]
    far_length = jnp.concatenate([digits[:, :HD] * 8.0 + digits[:, HD:]] * (span // HD), axis=1)
    ones = jnp.ones((span, HD), jnp.bfloat16)
    pad = jnp.zeros((HD - 4 * rows, 2 * HD), jnp.bfloat16)
    for step in range(2):
        limit = length if step == 0 else jnp.where(owner, 0, length)
        bias = jnp.where(key < limit, 0.0, NEG)
        far_bias = jnp.where(key.astype(jnp.float32) < far_length, 0.0, NEG)
        if step == 1:
            far_bias = jnp.where(far_owner, NEG, far_bias)
        extra_bias = jnp.where((lane % (2 * rows) < rows * (1 + step)) & (lane < 4 * rows), 0.0, NEG)
        extra_keys, extra_values = [
            jnp.concatenate(
                [
                    own_ref[step, index],
                    clean_ref[index],
                    far_ref[tail + (2 * step + index) * rows:tail + (2 * step + index + 1) * rows, :],
                    far_ref[tail + (4 + index) * rows:tail + (5 + index) * rows, :],
                    pad,
                ],
                axis=0,
            )
            for index in range(2)
        ]
        stats = jnp.zeros((block, HD), jnp.float32)
        for half in range(2):
            part = step * 2 + half
            lanes = slice(half * HD, (half + 1) * HD)
            query = wide[pl.ds(part, block, stride=PARTS), :].astype(jnp.bfloat16)
            groups = (
                (cache_ref[0, 0, :, lanes], cache_ref[0, 1, :, lanes], bias),
                (far_ref[0:span, lanes], far_ref[span:2 * span, lanes], far_bias),
                (extra_keys[:, lanes], extra_values[:, lanes], extra_bias),
            )
            scores = [
                lax.dot_general(query, keys, NT, preferred_element_type=jnp.float32) + mask for keys, _, mask in groups
            ]
            top = jnp.max(scores[0], axis=1, keepdims=True)
            for score in scores[1:]:
                top = jnp.maximum(top, jnp.max(score, axis=1, keepdims=True))
            top = jnp.ceil(top)
            accum = jnp.zeros((block, 2 * HD), jnp.float32)
            for score, (_, values, _) in zip(scores, groups):
                weights = jnp.exp2((score - top) * EXP2_SCALE).astype(jnp.bfloat16)
                values = jnp.concatenate([values, ones[:values.shape[0]]], axis=1)
                accum = accum + lax.dot_general(weights, values, NN, preferred_element_type=jnp.float32)
            wide_out[pl.ds(half * 2 + step, block, stride=BACK), :] = accum[:, :HD]
            total = accum[:, HD:]
            top = jnp.broadcast_to(top, (block, HD))
            top_hi = top.astype(jnp.bfloat16).astype(jnp.float32)
            total_hi = total.astype(jnp.bfloat16).astype(jnp.float32)
            for place, value in enumerate((top_hi, top - top_hi, total_hi, total - total_hi)):
                stats = jnp.where(lane == 32 * place + half, value, stats)
        wide_out[pl.ds(4 + step, block, stride=BACK), :] = stats
    out_ref[...] = wide_out[...].astype(jnp.bfloat16)


def combine_kernel(recv_ref, out_ref, wide):
    groups = out_ref.shape[1] // (2 * HD)
    senders = recv_ref.shape[0] // BACK
    devices = senders // groups
    wide[...] = recv_ref[...].astype(jnp.float32)

    def rows_of(place):
        return wide[pl.ds(place, senders, stride=BACK), :].reshape(devices, groups, HD)

    for step in range(2):
        stats = rows_of(4 + step)
        for half in range(2):
            local = stats[:, :, half:half + 1] + stats[:, :, 32 + half:33 + half]
            total = stats[:, :, 64 + half:65 + half] + stats[:, :, 96 + half:97 + half]
            top = jnp.max(local, axis=0, keepdims=True)
            scale = jnp.exp2((local - top) * EXP2_SCALE)
            whole = jnp.sum(scale * total, axis=0)
            result = jnp.sum(scale * rows_of(half * 2 + step), axis=0) / whole
            for group in range(groups):
                begin = (group * 2 + half) * HD
                out_ref[step:step + 1, begin:begin + HD] = result[group:group + 1].astype(jnp.bfloat16)


def renew_kernel(evict_ref, near_ref, far_ref, cache_ref, new_ref):
    devices, _, rows, _ = near_ref.shape
    parity = lax.axis_index("cb")
    owner = lax.axis_index("ca") * 2 + parity == evict_ref[0]

    @pl.when(owner)
    def _():
        for ref, kind in ((near_ref, parity), (far_ref, 1 - parity)):
            for device in range(devices):
                place = pl.ds(pl.multiple_of((device * 2 + kind) * rows, rows), rows)
                for index in range(2):
                    new_ref[0, index, place, :] = ref[device, index]

    @pl.when(jnp.logical_not(owner))
    def _():
        new_ref[...] = cache_ref[...]


def call(kernel, out_shape, in_specs, scratch=(), name=None):
    several = isinstance(out_shape, tuple)
    return pl.pallas_call(
        kernel,
        out_shape=out_shape,
        in_specs=in_specs,
        out_specs=(VMEM,) * len(out_shape) if several else VMEM,
        scratch_shapes=list(scratch),
        compiler_params=pltpu.CompilerParams(vmem_limit_bytes=40 * 1024 * 1024),
        name=name,
    )


def body(queries, cache_kv, lengths, evict, own_kv, clean_kv):
    steps, _, features = queries.shape
    _, kinds, span, width = cache_kv.shape
    pairs = lax.axis_size("ca")
    groups = lax.axis_size("head")
    rows = clean_kv.shape[1]
    tokens = pairs * groups
    bf16, f32 = jnp.bfloat16, jnp.float32
    shape = jax.ShapeDtypeStruct
    swap = [(0, 1), (1, 0)]
    pack, copies = call(
        pack_kernel,
        (shape((2 * span + 7 * rows, width), bf16), shape((pairs,) + clean_kv.shape, bf16)),
        [SMEM] + [VMEM] * 3,
        name="pack",
    )(lengths, cache_kv, own_kv, clean_kv)
    far = lax.ppermute(pack, "cb", swap)
    message = call(
        spread_kernel,
        shape((tokens * PARTS, HD), bf16),
        [VMEM],
        [pltpu.VMEM((groups * PARTS, HD), f32)],
        name="spread_queries",
    )(queries.reshape(steps, features))
    recv = lax.all_to_all(
        message.reshape(tokens, PARTS, HD), ("ca", "head"), split_axis=0, concat_axis=0, tiled=True
    ).reshape(tokens * PARTS, HD)
    parts = call(
        attend_kernel,
        shape((tokens * BACK, HD), bf16),
        [SMEM, SMEM] + [VMEM] * 5,
        [pltpu.VMEM((tokens * PARTS, HD), f32), pltpu.VMEM((tokens * BACK, HD), f32)],
        name="attend",
    )(lengths, evict, recv, cache_kv, own_kv, clean_kv, far)
    _, copies = lax.optimization_barrier((recv, copies))
    near = lax.all_to_all(copies, "ca", split_axis=0, concat_axis=0, tiled=True)
    parts, near = lax.optimization_barrier((parts, near))
    back = lax.all_to_all(
        parts.reshape(tokens * BACK // 2, 2, HD), ("ca", "head"), split_axis=0, concat_axis=0, tiled=True
    ).reshape(tokens * BACK, HD)
    attended = call(
        combine_kernel,
        shape((steps, features), bf16),
        [VMEM],
        [pltpu.VMEM((tokens * BACK, HD), f32)],
        name="combine",
    )(back)
    other = lax.ppermute(near, "cb", swap)
    new_cache = call(renew_kernel, shape(cache_kv.shape, bf16), [SMEM] + [VMEM] * 3, name="renew_cache")(
        evict, near, other, cache_kv
    )
    return (attended.reshape(steps, 1, features), new_cache)


def solution(mesh):
    ctx, heads = mesh.devices.shape
    halves = jax.sharding.Mesh(mesh.devices.reshape(ctx // 2, 2, heads), ("ca", "cb", "head"))
    ctx = ("ca", "cb")
    in_specs = (
        P(None, ctx + ("head",), None),
        P(ctx, None, None, "head"),
        P(ctx),
        P(),
        P(None, None, ctx, "head"),
        P(None, ctx, "head"),
    )
    out_specs = (P(None, ctx + ("head",), None), P(ctx, None, None, "head"))
    return jax.shard_map(body, mesh=halves, in_specs=in_specs, out_specs=out_specs, check_vma=False)
```

```python
import math

import jax
import jax.numpy as jnp
from jax import lax
from jax.experimental import pallas as pl
from jax.experimental.pallas import tpu as pltpu
from jax.sharding import PartitionSpec as P

HD = 128
PARTS = 8
BACK = 10
EXP2_SCALE = math.log2(math.e) / math.sqrt(HD)
NEG = -1e30
VMEM = pl.BlockSpec(memory_space=pltpu.VMEM)
SMEM = pl.BlockSpec(memory_space=pltpu.SMEM)
NT = (((1,), (1,)), ((), ()))
NN = (((1,), (0,)), ((), ()))


def spread_kernel(q_ref, out_ref, rows):
    count = rows.shape[0]
    for row in range(count):
        chip, step, head = row // PARTS, row // 4 % 2, row % 4
        start = (chip * 4 + head) * HD
        rows[row:row + 1, :] = q_ref[step:step + 1, start:start + HD].astype(jnp.float32)
    message = rows[...].astype(out_ref.dtype)
    for dest in range(out_ref.shape[0] // count):
        out_ref[dest * count:(dest + 1) * count, :] = message


def pack_kernel(length_ref, cache_ref, own_ref, clean_ref, pack_ref, copies_ref):
    span, rows = cache_ref.shape[2], clean_ref.shape[1]
    pack_ref[0:span, :] = cache_ref[0, 0]
    pack_ref[span:2 * span, :] = cache_ref[0, 1]
    place = 2 * span
    for step in range(2):
        for index in range(2):
            pack_ref[place:place + rows, :] = own_ref[step, index]
            place += rows
    for index in range(2):
        pack_ref[place:place + rows, :] = clean_ref[index]
        place += rows
    length = length_ref[0]
    lane = lax.broadcasted_iota(jnp.int32, (rows, 2 * HD), 1)
    digits = jnp.where(lane < HD, length // 8, length % 8)
    pack_ref[place:place + rows, :] = digits.astype(jnp.float32).astype(pack_ref.dtype)
    for dest in range(copies_ref.shape[0]):
        copies_ref[dest] = clean_ref[...]


def attend_kernel(evict_ref, recv_ref, pack_ref, far_ref, side_ref, cross_ref, out_ref, wide, wide_out):
    block = recv_ref.shape[0] // PARTS
    rows = 16
    span = (pack_ref.shape[0] - 7 * rows) // 2
    tail = 2 * span
    me = lax.axis_index("ca") * 2 + lax.axis_index("cb")
    core = lax.axis_index("hb")
    owners = [me == evict_ref[0], (me ^ 1) == evict_ref[0]]
    wide[...] = recv_ref[...].astype(jnp.float32)
    key = lax.broadcasted_iota(jnp.int32, (1, span), 1).astype(jnp.float32)
    lane = lax.broadcasted_iota(jnp.int32, (1, HD), 1)
    lengths = []
    for ref in (pack_ref, far_ref):
        digits = ref[tail + 6 * rows:tail + 7 * rows, :].astype(jnp.float32)[0:1]
        lengths.append(jnp.concatenate([digits[:, :HD] * 8.0 + digits[:, HD:]] * (span // HD), axis=1))
    ones = jnp.ones((span, HD), jnp.bfloat16)
    pad = jnp.zeros((HD - 4 * rows, 2 * HD), jnp.bfloat16)
    for step in range(2):
        biases = []
        for length, owner in zip(lengths, owners):
            bias = jnp.where(key < length, 0.0, NEG)
            biases.append(bias if step == 0 else jnp.where(owner, NEG, bias))
        extra_bias = jnp.where((lane % (2 * rows) < rows * (1 + step)) & (lane < 4 * rows), 0.0, NEG)
        stats = jnp.zeros((block, HD), jnp.float32)
        for side, refs in enumerate(((pack_ref, far_ref), (side_ref, cross_ref))):
            extras = []
            for index in range(2):
                pieces = []
                for ref in refs:
                    own = tail + (2 * step + index) * rows
                    clean = tail + (4 + index) * rows
                    pieces += [ref[own:own + rows, :], ref[clean:clean + rows, :]]
                extras.append(jnp.concatenate(pieces + [pad], axis=0))
            for half in range(2):
                head = (core ^ side) * 2 + half
                lanes = slice(half * HD, (half + 1) * HD)
                query = wide[pl.ds(step * 4 + head, block, stride=PARTS), :].astype(jnp.bfloat16)
                groups = [(ref[0:span, lanes], ref[span:2 * span, lanes], bias) for ref, bias in zip(refs, biases)]
                groups.append((extras[0][:, lanes], extras[1][:, lanes], extra_bias))
                scores = [
                    lax.dot_general(query, keys, NT, preferred_element_type=jnp.float32) + mask
                    for keys, _, mask in groups
                ]
                top = jnp.max(scores[0], axis=1, keepdims=True)
                for score in scores[1:]:
                    top = jnp.maximum(top, jnp.max(score, axis=1, keepdims=True))
                top = jnp.ceil(top)
                accum = jnp.zeros((block, 2 * HD), jnp.float32)
                for score, (_, values, _) in zip(scores, groups):
                    weights = jnp.exp2((score - top) * EXP2_SCALE).astype(jnp.bfloat16)
                    values = jnp.concatenate([values, ones[:values.shape[0]]], axis=1)
                    accum = accum + lax.dot_general(weights, values, NN, preferred_element_type=jnp.float32)
                wide_out[pl.ds(head * 2 + step, block, stride=BACK), :] = accum[:, :HD]
                total = accum[:, HD:]
                top = jnp.broadcast_to(top, (block, HD))
                top_hi = top.astype(jnp.bfloat16).astype(jnp.float32)
                total_hi = total.astype(jnp.bfloat16).astype(jnp.float32)
                for place, value in enumerate((top_hi, top - top_hi, total_hi, total - total_hi)):
                    stats = jnp.where(lane == 32 * place + head, value, stats)
        wide_out[pl.ds(8 + step, block, stride=BACK), :] = stats
    out_ref[...] = wide_out[...].astype(jnp.bfloat16)


def combine_kernel(recv_ref, out_ref, wide):
    chips = out_ref.shape[1] // (4 * HD)
    senders = recv_ref.shape[0] // BACK
    devices = senders // chips
    wide[...] = recv_ref[...].astype(jnp.float32)

    def rows_of(place):
        return wide[pl.ds(place, senders, stride=BACK), :].reshape(devices, chips, HD)

    for step in range(2):
        stats = rows_of(8 + step)
        for head in range(4):
            local = stats[:, :, head:head + 1] + stats[:, :, 32 + head:33 + head]
            total = stats[:, :, 64 + head:65 + head] + stats[:, :, 96 + head:97 + head]
            top = jnp.max(local, axis=0, keepdims=True)
            scale = jnp.exp2((local - top) * EXP2_SCALE)
            whole = jnp.sum(scale * total, axis=0)
            result = jnp.sum(scale * rows_of(head * 2 + step), axis=0) / whole
            for chip in range(chips):
                begin = (chip * 4 + head) * HD
                out_ref[step:step + 1, begin:begin + HD] = result[chip:chip + 1].astype(jnp.bfloat16)


def renew_kernel(evict_ref, near_ref, far_ref, cache_ref, new_ref):
    devices, _, rows, _ = near_ref.shape
    parity = lax.axis_index("cb")
    owner = lax.axis_index("ca") * 2 + parity == evict_ref[0]

    @pl.when(owner)
    def _():
        for ref, kind in ((near_ref, parity), (far_ref, 1 - parity)):
            for device in range(devices):
                place = pl.ds(pl.multiple_of((device * 2 + kind) * rows, rows), rows)
                for index in range(2):
                    new_ref[0, index, place, :] = ref[device, index]

    @pl.when(jnp.logical_not(owner))
    def _():
        new_ref[...] = cache_ref[...]


def call(kernel, out_shape, in_specs, scratch=(), name=None):
    several = isinstance(out_shape, tuple)
    return pl.pallas_call(
        kernel,
        out_shape=out_shape,
        in_specs=in_specs,
        out_specs=(VMEM,) * len(out_shape) if several else VMEM,
        scratch_shapes=list(scratch),
        compiler_params=pltpu.CompilerParams(vmem_limit_bytes=40 * 1024 * 1024),
        name=name,
    )


def body(queries, cache_kv, lengths, evict, own_kv, clean_kv):
    steps, _, features = queries.shape
    span, width = cache_kv.shape[2:]
    pairs = lax.axis_size("ca")
    chips = lax.axis_size("ha")
    rows = clean_kv.shape[1]
    tokens = pairs * chips
    bf16, f32 = jnp.bfloat16, jnp.float32
    shape = jax.ShapeDtypeStruct
    swap = [(0, 1), (1, 0)]
    pack, copies = call(
        pack_kernel,
        (shape((2 * span + 7 * rows, width), bf16), shape((pairs,) + clean_kv.shape, bf16)),
        [SMEM] + [VMEM] * 3,
        name="pack",
    )(lengths, cache_kv, own_kv, clean_kv)
    far = lax.ppermute(pack, "cb", swap)
    side = lax.ppermute(pack, "hb", swap)
    cross = lax.ppermute(far, "hb", swap)
    message = call(
        spread_kernel,
        shape((tokens * PARTS, HD), bf16),
        [VMEM],
        [pltpu.VMEM((chips * PARTS, HD), f32)],
        name="spread_queries",
    )(queries.reshape(steps, features))
    recv = lax.all_to_all(
        message.reshape(tokens, PARTS, HD), ("ca", "ha"), split_axis=0, concat_axis=0, tiled=True
    ).reshape(tokens * PARTS, HD)
    parts = call(
        attend_kernel,
        shape((tokens * BACK, HD), bf16),
        [SMEM] + [VMEM] * 5,
        [pltpu.VMEM((tokens * PARTS, HD), f32), pltpu.VMEM((tokens * BACK, HD), f32)],
        name="attend",
    )(evict, recv, pack, far, side, cross)
    _, copies = lax.optimization_barrier((recv, copies))
    near = lax.all_to_all(copies, "ca", split_axis=0, concat_axis=0, tiled=True)
    parts, near = lax.optimization_barrier((parts, near))
    back = lax.all_to_all(
        parts.reshape(tokens * BACK // 2, 2, HD), ("ca", "ha"), split_axis=0, concat_axis=0, tiled=True
    ).reshape(tokens * BACK, HD)
    attended = call(
        combine_kernel,
        shape((steps, features), bf16),
        [VMEM],
        [pltpu.VMEM((tokens * BACK, HD), f32)],
        name="combine",
    )(back)
    other = lax.ppermute(near, "cb", swap)
    new_cache = call(renew_kernel, shape(cache_kv.shape, bf16), [SMEM] + [VMEM] * 3, name="renew_cache")(
        evict, near, other, cache_kv
    )
    return (attended.reshape(steps, 1, features), new_cache)


def solution(mesh):
    ctx, heads = mesh.devices.shape
    split = jax.sharding.Mesh(mesh.devices.reshape(ctx // 2, 2, heads // 2, 2), ("ca", "cb", "ha", "hb"))
    ctx, heads = ("ca", "cb"), ("ha", "hb")
    in_specs = (
        P(None, ctx + heads, None),
        P(ctx, None, None, heads),
        P(ctx),
        P(),
        P(None, None, ctx, heads),
        P(None, ctx, heads),
    )
    out_specs = (P(None, ctx + heads, None), P(ctx, None, None, heads))
    return jax.shard_map(body, mesh=split, in_specs=in_specs, out_specs=out_specs, check_vma=False)
```

```python
import math

import jax
import jax.numpy as jnp
from jax import lax
from jax.experimental import pallas as pl
from jax.experimental.pallas import tpu as pltpu
from jax.sharding import PartitionSpec as P

HD = 128
PARTS = 8
BACK = 10
EXP2_SCALE = math.log2(math.e) / math.sqrt(HD)
NEG = -1e30
VMEM = pl.BlockSpec(memory_space=pltpu.VMEM)
SMEM = pl.BlockSpec(memory_space=pltpu.SMEM)
HBM = pl.BlockSpec(memory_space=pltpu.HBM)
NT = (((1,), (1,)), ((), ()))
NN = (((1,), (0,)), ((), ()))


def split_kernel(q_ref, out_ref, rows):
    for row in range(rows.shape[0]):
        chip, step, head = row // PARTS, row // 4 % 2, row % 4
        start = (chip * 4 + head) * HD
        rows[row:row + 1, :] = q_ref[step:step + 1, start:start + HD].astype(jnp.float32)
    out_ref[...] = rows[...].astype(out_ref.dtype)


def spread_kernel(q_ref, clean_ref, out_ref):
    tokens = clean_ref.shape[1]
    count = q_ref.shape[0] + 4 * tokens
    for dest in range(out_ref.shape[0] // count):
        place = dest * count
        out_ref[place:place + q_ref.shape[0], :] = q_ref[...]
        place += q_ref.shape[0]
        for half in range(2):
            for index in range(2):
                out_ref[place:place + tokens, :] = clean_ref[index, :, half * HD:(half + 1) * HD]
                place += tokens


def pack_kernel(length_ref, cache_ref, own_ref, clean_ref, pack_ref, sems):
    span, rows = cache_ref.shape[2], clean_ref.shape[1]
    pieces = [(cache_ref.at[0, index], span) for index in range(2)]
    pieces += [(own_ref.at[step, index], rows) for step in range(2) for index in range(2)]
    pieces += [(clean_ref.at[index], rows) for index in range(2)]
    place, copies = 0, []
    for number, (piece, count) in enumerate(pieces):
        copies.append(pltpu.make_async_copy(piece, pack_ref.at[pl.ds(place, count)], sems.at[number]))
        copies[-1].start()
        place += count
    length = length_ref[0]
    lane = lax.broadcasted_iota(jnp.int32, (rows, 2 * HD), 1)
    digits = jnp.where(lane < HD, length // 8, length % 8)
    pack_ref[place:place + rows, :] = digits.astype(jnp.float32).astype(pack_ref.dtype)
    for copy in copies:
        copy.wait()


def attend_kernel(evict_ref, recv_ref, pack_ref, far_ref, side_ref, cross_ref, out_ref, clean_ref, wide, wide_out):
    block = wide.shape[0] // PARTS
    rows = 16
    span = (pack_ref.shape[0] - 7 * rows) // 2
    tail = 2 * span
    me = lax.axis_index("ca") * 2 + lax.axis_index("cb")
    core = lax.axis_index("hb")
    owners = [me == evict_ref[0], (me ^ 1) == evict_ref[0]]
    senders = lax.axis_size("ca")
    count, taken = recv_ref.shape[0] // senders, wide.shape[0] // senders
    for sender in range(senders):
        place, rest = sender * count, count - taken
        wide[sender * taken:(sender + 1) * taken, :] = recv_ref[place:place + taken, :].astype(jnp.float32)
        clean_ref[sender * rest:(sender + 1) * rest, :] = recv_ref[place + taken:place + count, :]
    key = lax.broadcasted_iota(jnp.int32, (1, span), 1).astype(jnp.float32)
    lane = lax.broadcasted_iota(jnp.int32, (1, HD), 1)
    lengths = []
    for ref in (pack_ref, far_ref):
        digits = ref[tail + 6 * rows:tail + 7 * rows, :].astype(jnp.float32)[0:1]
        lengths.append(jnp.concatenate([digits[:, :HD] * 8.0 + digits[:, HD:]] * (span // HD), axis=1))
    ones = jnp.ones((span, HD), jnp.bfloat16)
    pad = jnp.zeros((HD - 4 * rows, 2 * HD), jnp.bfloat16)
    for step in range(2):
        biases = []
        for length, owner in zip(lengths, owners):
            bias = jnp.where(key < length, 0.0, NEG)
            biases.append(bias if step == 0 else jnp.where(owner, NEG, bias))
        extra_bias = jnp.where((lane % (2 * rows) < rows * (1 + step)) & (lane < 4 * rows), 0.0, NEG)
        stats = jnp.zeros((block, HD), jnp.float32)
        for side, refs in enumerate(((pack_ref, far_ref), (side_ref, cross_ref))):
            extras = []
            for index in range(2):
                pieces = []
                for ref in refs:
                    own = tail + (2 * step + index) * rows
                    clean = tail + (4 + index) * rows
                    pieces += [ref[own:own + rows, :], ref[clean:clean + rows, :]]
                extras.append(jnp.concatenate(pieces + [pad], axis=0))
            for half in range(2):
                head = (core ^ side) * 2 + half
                lanes = slice(half * HD, (half + 1) * HD)
                query = wide[pl.ds(step * 4 + head, block, stride=PARTS), :].astype(jnp.bfloat16)
                groups = [(ref[0:span, lanes], ref[span:2 * span, lanes], bias) for ref, bias in zip(refs, biases)]
                groups.append((extras[0][:, lanes], extras[1][:, lanes], extra_bias))
                scores = [
                    lax.dot_general(query, keys, NT, preferred_element_type=jnp.float32) + mask
                    for keys, _, mask in groups
                ]
                top = jnp.max(scores[0], axis=1, keepdims=True)
                for score in scores[1:]:
                    top = jnp.maximum(top, jnp.max(score, axis=1, keepdims=True))
                top = jnp.ceil(top)
                accum = jnp.zeros((block, 2 * HD), jnp.float32)
                for score, (_, values, _) in zip(scores, groups):
                    weights = jnp.exp2((score - top) * EXP2_SCALE).astype(jnp.bfloat16)
                    values = jnp.concatenate([values, ones[:values.shape[0]]], axis=1)
                    accum = accum + lax.dot_general(weights, values, NN, preferred_element_type=jnp.float32)
                wide_out[pl.ds(head * 2 + step, block, stride=BACK), :] = accum[:, :HD]
                total = accum[:, HD:]
                top = jnp.broadcast_to(top, (block, HD))
                top_hi = top.astype(jnp.bfloat16).astype(jnp.float32)
                total_hi = total.astype(jnp.bfloat16).astype(jnp.float32)
                for place, value in enumerate((top_hi, top - top_hi, total_hi, total - total_hi)):
                    stats = jnp.where(lane == 32 * place + head, value, stats)
        wide_out[pl.ds(8 + step, block, stride=BACK), :] = stats
    out_ref[...] = wide_out[...].astype(jnp.bfloat16)


def combine_kernel(recv_ref, out_ref, wide):
    chips = out_ref.shape[1] // (4 * HD)
    senders = recv_ref.shape[0] // BACK
    devices = senders // chips
    wide[...] = recv_ref[...].astype(jnp.float32)

    def rows_of(place):
        return wide[pl.ds(place, senders, stride=BACK), :].reshape(devices, chips, HD)

    for step in range(2):
        stats = rows_of(8 + step)
        for head in range(4):
            local = stats[:, :, head:head + 1] + stats[:, :, 32 + head:33 + head]
            total = stats[:, :, 64 + head:65 + head] + stats[:, :, 96 + head:97 + head]
            top = jnp.max(local, axis=0, keepdims=True)
            scale = jnp.exp2((local - top) * EXP2_SCALE)
            whole = jnp.sum(scale * total, axis=0)
            result = jnp.sum(scale * rows_of(head * 2 + step), axis=0) / whole
            for chip in range(chips):
                begin = (chip * 4 + head) * HD
                out_ref[step:step + 1, begin:begin + HD] = result[chip:chip + 1].astype(jnp.bfloat16)


def renew_kernel(evict_ref, near_ref, far_ref, cache_ref, new_ref):
    devices, rows = lax.axis_size("ca"), 16
    parity = lax.axis_index("cb")
    owner = lax.axis_index("ca") * 2 + parity == evict_ref[0]

    @pl.when(owner)
    def _():
        for ref, kind in ((near_ref, parity), (far_ref, 1 - parity)):
            for device in range(devices):
                place = pl.ds(pl.multiple_of((device * 2 + kind) * rows, rows), rows)
                for half in range(2):
                    for index in range(2):
                        start = ((device * 2 + half) * 2 + index) * rows
                        new_ref[0, index, place, half * HD:(half + 1) * HD] = ref[start:start + rows, :]

    @pl.when(jnp.logical_not(owner))
    def _():
        new_ref[...] = cache_ref[...]


def call(kernel, out_shape, in_specs, scratch=(), name=None, limit=40):
    several = isinstance(out_shape, tuple)
    return pl.pallas_call(
        kernel,
        out_shape=out_shape,
        in_specs=in_specs,
        out_specs=(VMEM,) * len(out_shape) if several else VMEM,
        scratch_shapes=list(scratch),
        compiler_params=pltpu.CompilerParams(vmem_limit_bytes=limit * 1024 * 1024),
        name=name,
    )


def body(queries, cache_kv, lengths, evict, own_kv, clean_kv):
    steps, _, features = queries.shape
    span, width = cache_kv.shape[2:]
    pairs = lax.axis_size("ca")
    chips = lax.axis_size("ha")
    rows = clean_kv.shape[1]
    tokens = pairs * chips
    bf16, f32 = jnp.bfloat16, jnp.float32
    shape = jax.ShapeDtypeStruct
    swap = [(0, 1), (1, 0)]
    pack = call(
        pack_kernel,
        shape((2 * span + 7 * rows, width), bf16),
        [SMEM] + [HBM] * 3,
        [pltpu.SemaphoreType.DMA((8,))],
        name="pack",
        limit=60,
    )(lengths, cache_kv, own_kv, clean_kv)
    far = lax.ppermute(pack, "cb", swap)
    side = lax.ppermute(pack, "hb", swap)
    cross = lax.ppermute(far, "hb", swap)
    split = call(
        split_kernel,
        shape((chips * PARTS, HD), bf16),
        [VMEM],
        [pltpu.VMEM((chips * PARTS, HD), f32)],
        name="split_queries",
    )(queries.reshape(steps, features))
    mine = lax.all_to_all(split.reshape(chips, PARTS, HD), "ha", split_axis=0, concat_axis=0, tiled=True)
    message = call(
        spread_kernel, shape((pairs * (chips * PARTS + 4 * rows), HD), bf16), [VMEM] * 2, name="spread"
    )(mine.reshape(chips * PARTS, HD), clean_kv)
    recv = lax.all_to_all(message, "ca", split_axis=0, concat_axis=0, tiled=True)
    parts, near = call(
        attend_kernel,
        (shape((tokens * BACK, HD), bf16), shape((pairs * 4 * rows, HD), bf16)),
        [SMEM] + [VMEM] * 5,
        [pltpu.VMEM((tokens * PARTS, HD), f32), pltpu.VMEM((tokens * BACK, HD), f32)],
        name="attend",
    )(evict, recv, pack, far, side, cross)
    back = lax.all_to_all(
        parts.reshape(tokens * BACK // 2, 2, HD), ("ca", "ha"), split_axis=0, concat_axis=0, tiled=True
    ).reshape(tokens * BACK, HD)
    attended = call(
        combine_kernel,
        shape((steps, features), bf16),
        [VMEM],
        [pltpu.VMEM((tokens * BACK, HD), f32)],
        name="combine",
    )(back)
    other = lax.ppermute(near, "cb", swap)
    new_cache = call(renew_kernel, shape(cache_kv.shape, bf16), [SMEM] + [VMEM] * 3, name="renew_cache")(
        evict, near, other, cache_kv
    )
    return (attended.reshape(steps, 1, features), new_cache)


def solution(mesh):
    ctx, heads = mesh.devices.shape
    split = jax.sharding.Mesh(mesh.devices.reshape(ctx // 2, 2, heads // 2, 2), ("ca", "cb", "ha", "hb"))
    ctx, heads = ("ca", "cb"), ("ha", "hb")
    in_specs = (
        P(None, ctx + heads, None),
        P(ctx, None, None, heads),
        P(ctx),
        P(),
        P(None, None, ctx, heads),
        P(None, ctx, heads),
    )
    out_specs = (P(None, ctx + heads, None), P(ctx, None, None, heads))
    return jax.shard_map(body, mesh=split, in_specs=in_specs, out_specs=out_specs, check_vma=False)
```

```python
import math

import jax
import jax.numpy as jnp
from jax import lax
from jax.experimental import pallas as pl
from jax.experimental.pallas import tpu as pltpu
from jax.sharding import PartitionSpec as P

HD = 128
PARTS = 8
BACK = 10
EXP2_SCALE = math.log2(math.e) / math.sqrt(HD)
NEG = -1e30
VMEM = pl.BlockSpec(memory_space=pltpu.VMEM)
SMEM = pl.BlockSpec(memory_space=pltpu.SMEM)
HBM = pl.BlockSpec(memory_space=pltpu.HBM)
NT = (((1,), (1,)), ((), ()))
NN = (((1,), (0,)), ((), ()))


def spread_kernel(q_ref, clean_ref, out_ref, copies_ref, rows):
    count = rows.shape[0]
    for row in range(count):
        chip, step, head = row // PARTS, row // 4 % 2, row % 4
        start = (chip * 4 + head) * HD
        rows[row:row + 1, :] = q_ref[step:step + 1, start:start + HD].astype(jnp.float32)
    message = rows[...].astype(out_ref.dtype)
    for dest in range(out_ref.shape[0] // count):
        out_ref[dest * count:(dest + 1) * count, :] = message
        copies_ref[dest] = clean_ref[...]


def pack_kernel(length_ref, cache_ref, own_ref, clean_ref, pack_ref, sems):
    span, rows = cache_ref.shape[2], clean_ref.shape[1]
    pieces = [(cache_ref.at[0, index], span) for index in range(2)]
    pieces += [(own_ref.at[step, index], rows) for step in range(2) for index in range(2)]
    pieces += [(clean_ref.at[index], rows) for index in range(2)]
    place, copies = 0, []
    for number, (piece, count) in enumerate(pieces):
        copies.append(pltpu.make_async_copy(piece, pack_ref.at[pl.ds(place, count)], sems.at[number]))
        copies[-1].start()
        place += count
    length = length_ref[0]
    lane = lax.broadcasted_iota(jnp.int32, (rows, 2 * HD), 1)
    digits = jnp.where(lane < HD, length // 8, length % 8)
    pack_ref[place:place + rows, :] = digits.astype(jnp.float32).astype(pack_ref.dtype)
    for copy in copies:
        copy.wait()


def attend_kernel(evict_ref, recv_ref, pack_ref, far_ref, side_ref, cross_ref, out_ref, wide, wide_out):
    block = recv_ref.shape[0] // PARTS
    rows = 16
    span = (pack_ref.shape[0] - 7 * rows) // 2
    tail = 2 * span
    me = lax.axis_index("ca") * 2 + lax.axis_index("cb")
    core = lax.axis_index("hb")
    owners = [me == evict_ref[0], (me ^ 1) == evict_ref[0]]
    wide[...] = recv_ref[...].astype(jnp.float32)
    key = lax.broadcasted_iota(jnp.int32, (1, span), 1).astype(jnp.float32)
    lane = lax.broadcasted_iota(jnp.int32, (1, HD), 1)
    lengths = []
    for ref in (pack_ref, far_ref):
        digits = ref[tail + 6 * rows:tail + 7 * rows, :].astype(jnp.float32)[0:1]
        lengths.append(jnp.concatenate([digits[:, :HD] * 8.0 + digits[:, HD:]] * (span // HD), axis=1))
    ones = jnp.ones((span, HD), jnp.bfloat16)
    pad = jnp.zeros((HD - 4 * rows, 2 * HD), jnp.bfloat16)
    for step in range(2):
        biases = []
        for length, owner in zip(lengths, owners):
            bias = jnp.where(key < length, 0.0, NEG)
            biases.append(bias if step == 0 else jnp.where(owner, NEG, bias))
        extra_bias = jnp.where((lane % (2 * rows) < rows * (1 + step)) & (lane < 4 * rows), 0.0, NEG)
        stats = jnp.zeros((block, HD), jnp.float32)
        for side, refs in enumerate(((pack_ref, far_ref), (side_ref, cross_ref))):
            extras = []
            for index in range(2):
                pieces = []
                for ref in refs:
                    own = tail + (2 * step + index) * rows
                    clean = tail + (4 + index) * rows
                    pieces += [ref[own:own + rows, :], ref[clean:clean + rows, :]]
                extras.append(jnp.concatenate(pieces + [pad], axis=0))
            for half in range(2):
                head = (core ^ side) * 2 + half
                lanes = slice(half * HD, (half + 1) * HD)
                query = wide[pl.ds(step * 4 + head, block, stride=PARTS), :].astype(jnp.bfloat16)
                groups = [(ref[0:span, lanes], ref[span:2 * span, lanes], bias) for ref, bias in zip(refs, biases)]
                groups.append((extras[0][:, lanes], extras[1][:, lanes], extra_bias))
                scores = [
                    lax.dot_general(query, keys, NT, preferred_element_type=jnp.float32) + mask
                    for keys, _, mask in groups
                ]
                top = jnp.max(scores[0], axis=1, keepdims=True)
                for score in scores[1:]:
                    top = jnp.maximum(top, jnp.max(score, axis=1, keepdims=True))
                top = jnp.ceil(top)
                accum = jnp.zeros((block, 2 * HD), jnp.float32)
                for score, (_, values, _) in zip(scores, groups):
                    weights = jnp.exp2((score - top) * EXP2_SCALE).astype(jnp.bfloat16)
                    values = jnp.concatenate([values, ones[:values.shape[0]]], axis=1)
                    accum = accum + lax.dot_general(weights, values, NN, preferred_element_type=jnp.float32)
                wide_out[pl.ds(head * 2 + step, block, stride=BACK), :] = accum[:, :HD]
                total = accum[:, HD:]
                top = jnp.broadcast_to(top, (block, HD))
                top_hi = top.astype(jnp.bfloat16).astype(jnp.float32)
                total_hi = total.astype(jnp.bfloat16).astype(jnp.float32)
                for place, value in enumerate((top_hi, top - top_hi, total_hi, total - total_hi)):
                    stats = jnp.where(lane == 32 * place + head, value, stats)
        wide_out[pl.ds(8 + step, block, stride=BACK), :] = stats
    out_ref[...] = wide_out[...].astype(jnp.bfloat16)


def combine_kernel(recv_ref, out_ref, wide):
    chips = out_ref.shape[1] // (4 * HD)
    senders = recv_ref.shape[0] // BACK
    devices = senders // chips
    wide[...] = recv_ref[...].astype(jnp.float32)

    def rows_of(place):
        return wide[pl.ds(place, senders, stride=BACK), :].reshape(devices, chips, HD)

    for step in range(2):
        stats = rows_of(8 + step)
        for head in range(4):
            local = stats[:, :, head:head + 1] + stats[:, :, 32 + head:33 + head]
            total = stats[:, :, 64 + head:65 + head] + stats[:, :, 96 + head:97 + head]
            top = jnp.max(local, axis=0, keepdims=True)
            scale = jnp.exp2((local - top) * EXP2_SCALE)
            whole = jnp.sum(scale * total, axis=0)
            result = jnp.sum(scale * rows_of(head * 2 + step), axis=0) / whole
            for chip in range(chips):
                begin = (chip * 4 + head) * HD
                out_ref[step:step + 1, begin:begin + HD] = result[chip:chip + 1].astype(jnp.bfloat16)


def renew_kernel(evict_ref, near_ref, far_ref, cache_ref, new_ref):
    devices, _, rows, _ = near_ref.shape
    parity = lax.axis_index("cb")
    owner = lax.axis_index("ca") * 2 + parity == evict_ref[0]

    @pl.when(owner)
    def _():
        for ref, kind in ((near_ref, parity), (far_ref, 1 - parity)):
            for device in range(devices):
                place = pl.ds(pl.multiple_of((device * 2 + kind) * rows, rows), rows)
                for index in range(2):
                    new_ref[0, index, place, :] = ref[device, index]

    @pl.when(jnp.logical_not(owner))
    def _():
        new_ref[...] = cache_ref[...]


def call(kernel, out_shape, in_specs, scratch=(), name=None, limit=40):
    several = isinstance(out_shape, tuple)
    return pl.pallas_call(
        kernel,
        out_shape=out_shape,
        in_specs=in_specs,
        out_specs=(VMEM,) * len(out_shape) if several else VMEM,
        scratch_shapes=list(scratch),
        compiler_params=pltpu.CompilerParams(vmem_limit_bytes=limit * 1024 * 1024),
        name=name,
    )


def body(queries, cache_kv, lengths, evict, own_kv, clean_kv):
    steps, _, features = queries.shape
    span, width = cache_kv.shape[2:]
    pairs = lax.axis_size("ca")
    chips = lax.axis_size("ha")
    rows = clean_kv.shape[1]
    tokens = pairs * chips
    bf16, f32 = jnp.bfloat16, jnp.float32
    shape = jax.ShapeDtypeStruct
    swap = [(0, 1), (1, 0)]
    pack = call(
        pack_kernel,
        shape((2 * span + 7 * rows, width), bf16),
        [SMEM] + [HBM] * 3,
        [pltpu.SemaphoreType.DMA((8,))],
        name="pack",
        limit=60,
    )(lengths, cache_kv, own_kv, clean_kv)
    far = lax.ppermute(pack, "cb", swap)
    side = lax.ppermute(pack, "hb", swap)
    cross = lax.ppermute(far, "hb", swap)
    message, copies = call(
        spread_kernel,
        (shape((tokens * PARTS, HD), bf16), shape((pairs,) + clean_kv.shape, bf16)),
        [VMEM] * 2,
        [pltpu.VMEM((chips * PARTS, HD), f32)],
        name="spread",
    )(queries.reshape(steps, features), clean_kv)
    near = lax.all_to_all(copies, "ca", split_axis=0, concat_axis=0, tiled=True)
    near, message = lax.optimization_barrier((near, message))
    other = lax.ppermute(near, "cb", swap)
    recv = lax.all_to_all(
        message.reshape(tokens, PARTS, HD), ("ca", "ha"), split_axis=0, concat_axis=0, tiled=True
    ).reshape(tokens * PARTS, HD)
    parts = call(
        attend_kernel,
        shape((tokens * BACK, HD), bf16),
        [SMEM] + [VMEM] * 5,
        [pltpu.VMEM((tokens * PARTS, HD), f32), pltpu.VMEM((tokens * BACK, HD), f32)],
        name="attend",
    )(evict, recv, pack, far, side, cross)
    parts, other = lax.optimization_barrier((parts, other))
    back = lax.all_to_all(
        parts.reshape(tokens * BACK // 2, 2, HD), ("ca", "ha"), split_axis=0, concat_axis=0, tiled=True
    ).reshape(tokens * BACK, HD)
    attended = call(
        combine_kernel,
        shape((steps, features), bf16),
        [VMEM],
        [pltpu.VMEM((tokens * BACK, HD), f32)],
        name="combine",
    )(back)
    new_cache = call(renew_kernel, shape(cache_kv.shape, bf16), [SMEM] + [VMEM] * 3, name="renew_cache")(
        evict, near, other, cache_kv
    )
    return (attended.reshape(steps, 1, features), new_cache)


def solution(mesh):
    ctx, heads = mesh.devices.shape
    split = jax.sharding.Mesh(mesh.devices.reshape(ctx // 2, 2, heads // 2, 2), ("ca", "cb", "ha", "hb"))
    ctx, heads = ("ca", "cb"), ("ha", "hb")
    in_specs = (
        P(None, ctx + heads, None),
        P(ctx, None, None, heads),
        P(ctx),
        P(),
        P(None, None, ctx, heads),
        P(None, ctx, heads),
    )
    out_specs = (P(None, ctx + heads, None), P(ctx, None, None, heads))
    return jax.shard_map(body, mesh=split, in_specs=in_specs, out_specs=out_specs, check_vma=False)
```

```python
import math

import jax
import jax.numpy as jnp
from jax import lax
from jax.experimental import pallas as pl
from jax.experimental.pallas import tpu as pltpu
from jax.sharding import PartitionSpec as P

HD = 128
PARTS = 8
BACK = 10
EXP2_SCALE = math.log2(math.e) / math.sqrt(HD)
NEG = -1e30
FIRST = (0, 8, 4, 12)
LAST = (0, 2, 1, 3)
VMEM = pl.BlockSpec(memory_space=pltpu.VMEM)
SMEM = pl.BlockSpec(memory_space=pltpu.SMEM)
HBM = pl.BlockSpec(memory_space=pltpu.HBM)
NT = (((1,), (1,)), ((), ()))
NN = (((1,), (0,)), ((), ()))


def spread_kernel(q_ref, out_ref, rows):
    count = rows.shape[0]
    for row in range(count):
        chip, step, head = row // PARTS, row // 4 % 2, row % 4
        start = (chip * 4 + head) * HD
        rows[row:row + 1, :] = q_ref[step:step + 1, start:start + HD].astype(jnp.float32)
    message = rows[...].astype(out_ref.dtype)
    for dest in range(out_ref.shape[0] // count):
        out_ref[dest * count:(dest + 1) * count, :] = message


def pack_kernel(length_ref, cache_ref, own_ref, clean_ref, pack_ref, sems):
    span, rows = cache_ref.shape[2], clean_ref.shape[1]
    pieces = [(cache_ref.at[0, index], span) for index in range(2)]
    pieces += [(own_ref.at[step, index], rows) for step in range(2) for index in range(2)]
    pieces += [(clean_ref.at[index], rows) for index in range(2)]
    place, copies = 0, []
    for number, (piece, count) in enumerate(pieces):
        copies.append(pltpu.make_async_copy(piece, pack_ref.at[pl.ds(place, count)], sems.at[number]))
        copies[-1].start()
        place += count
    length = length_ref[0]
    lane = lax.broadcasted_iota(jnp.int32, (rows, 2 * HD), 1)
    digits = jnp.where(lane < HD, length // 8, length % 8)
    pack_ref[place:place + rows, :] = digits.astype(jnp.float32).astype(pack_ref.dtype)
    for copy in copies:
        copy.wait()


def join_kernel(clean_ref, far_ref, out_ref):
    rows = clean_ref.shape[1]
    place = far_ref.shape[0] - 3 * rows
    for index in range(2):
        out_ref[index] = clean_ref[index]
        out_ref[2 + index] = far_ref[place + index * rows:place + (index + 1) * rows, :]


def attend_kernel(
    evict_ref, recv_ref, pack_ref, far_ref, side_ref, cross_ref, a_ref, b_ref, c_ref, d_ref, out_ref, joint_ref, wide, wide_out
):
    block = recv_ref.shape[0] // PARTS
    rows = 16
    for number, ref in enumerate((a_ref, b_ref, c_ref, d_ref)):
        joint_ref[number] = ref[...]
    span = (pack_ref.shape[0] - 7 * rows) // 2
    tail = 2 * span
    me = lax.axis_index("ca") * 2 + lax.axis_index("cb")
    core = lax.axis_index("hb")
    owners = [me == evict_ref[0], (me ^ 1) == evict_ref[0]]
    wide[...] = recv_ref[...].astype(jnp.float32)
    key = lax.broadcasted_iota(jnp.int32, (1, span), 1).astype(jnp.float32)
    lane = lax.broadcasted_iota(jnp.int32, (1, HD), 1)
    lengths = []
    for ref in (pack_ref, far_ref):
        digits = ref[tail + 6 * rows:tail + 7 * rows, :].astype(jnp.float32)[0:1]
        lengths.append(jnp.concatenate([digits[:, :HD] * 8.0 + digits[:, HD:]] * (span // HD), axis=1))
    ones = jnp.ones((span, HD), jnp.bfloat16)
    pad = jnp.zeros((HD - 4 * rows, 2 * HD), jnp.bfloat16)
    for step in range(2):
        biases = []
        for length, owner in zip(lengths, owners):
            bias = jnp.where(key < length, 0.0, NEG)
            biases.append(bias if step == 0 else jnp.where(owner, NEG, bias))
        extra_bias = jnp.where((lane % (2 * rows) < rows * (1 + step)) & (lane < 4 * rows), 0.0, NEG)
        stats = jnp.zeros((block, HD), jnp.float32)
        for side, refs in enumerate(((pack_ref, far_ref), (side_ref, cross_ref))):
            extras = []
            for index in range(2):
                pieces = []
                for ref in refs:
                    own = tail + (2 * step + index) * rows
                    clean = tail + (4 + index) * rows
                    pieces += [ref[own:own + rows, :], ref[clean:clean + rows, :]]
                extras.append(jnp.concatenate(pieces + [pad], axis=0))
            for half in range(2):
                head = (core ^ side) * 2 + half
                lanes = slice(half * HD, (half + 1) * HD)
                query = wide[pl.ds(step * 4 + head, block, stride=PARTS), :].astype(jnp.bfloat16)
                groups = [(ref[0:span, lanes], ref[span:2 * span, lanes], bias) for ref, bias in zip(refs, biases)]
                groups.append((extras[0][:, lanes], extras[1][:, lanes], extra_bias))
                scores = [
                    lax.dot_general(query, keys, NT, preferred_element_type=jnp.float32) + mask
                    for keys, _, mask in groups
                ]
                top = jnp.max(scores[0], axis=1, keepdims=True)
                for score in scores[1:]:
                    top = jnp.maximum(top, jnp.max(score, axis=1, keepdims=True))
                top = jnp.ceil(top)
                accum = jnp.zeros((block, 2 * HD), jnp.float32)
                for score, (_, values, _) in zip(scores, groups):
                    weights = jnp.exp2((score - top) * EXP2_SCALE).astype(jnp.bfloat16)
                    values = jnp.concatenate([values, ones[:values.shape[0]]], axis=1)
                    accum = accum + lax.dot_general(weights, values, NN, preferred_element_type=jnp.float32)
                wide_out[pl.ds(head * 2 + step, block, stride=BACK), :] = accum[:, :HD]
                total = accum[:, HD:]
                top = jnp.broadcast_to(top, (block, HD))
                top_hi = top.astype(jnp.bfloat16).astype(jnp.float32)
                total_hi = total.astype(jnp.bfloat16).astype(jnp.float32)
                for place, value in enumerate((top_hi, top - top_hi, total_hi, total - total_hi)):
                    stats = jnp.where(lane == 32 * place + head, value, stats)
        wide_out[pl.ds(8 + step, block, stride=BACK), :] = stats
    out_ref[...] = wide_out[...].astype(jnp.bfloat16)


def combine_kernel(recv_ref, out_ref, wide):
    chips = out_ref.shape[1] // (4 * HD)
    senders = recv_ref.shape[0] // BACK
    devices = senders // chips
    wide[...] = recv_ref[...].astype(jnp.float32)

    def rows_of(place):
        return wide[pl.ds(place, senders, stride=BACK), :].reshape(devices, chips, HD)

    for step in range(2):
        stats = rows_of(8 + step)
        for head in range(4):
            local = stats[:, :, head:head + 1] + stats[:, :, 32 + head:33 + head]
            total = stats[:, :, 64 + head:65 + head] + stats[:, :, 96 + head:97 + head]
            top = jnp.max(local, axis=0, keepdims=True)
            scale = jnp.exp2((local - top) * EXP2_SCALE)
            whole = jnp.sum(scale * total, axis=0)
            result = jnp.sum(scale * rows_of(head * 2 + step), axis=0) / whole
            for chip in range(chips):
                begin = (chip * 4 + head) * HD
                out_ref[step:step + 1, begin:begin + HD] = result[chip:chip + 1].astype(jnp.bfloat16)


def renew_kernel(evict_ref, a_ref, b_ref, c_ref, d_ref, cache_ref, new_ref):
    entries, _, rows, _ = a_ref.shape
    across, parity = lax.axis_index("ca"), lax.axis_index("cb")
    owner = across * 2 + parity == evict_ref[0]

    @pl.when(owner)
    def _():
        for last, ref in zip(LAST, (a_ref, b_ref, c_ref, d_ref)):
            for entry in range(entries):
                for kind in range(2):
                    source = (across ^ (FIRST[entry] ^ last)) * 2 + (parity ^ kind)
                    place = pl.ds(pl.multiple_of(source * rows, rows), rows)
                    for index in range(2):
                        new_ref[0, index, place, :] = ref[entry, kind * 2 + index]

    @pl.when(jnp.logical_not(owner))
    def _():
        new_ref[...] = cache_ref[...]


def call(kernel, out_shape, in_specs, scratch=(), name=None, limit=40):
    several = isinstance(out_shape, tuple)
    return pl.pallas_call(
        kernel,
        out_shape=out_shape,
        in_specs=in_specs,
        out_specs=(VMEM,) * len(out_shape) if several else VMEM,
        scratch_shapes=list(scratch),
        compiler_params=pltpu.CompilerParams(vmem_limit_bytes=limit * 1024 * 1024),
        name=name,
    )


def body(queries, cache_kv, lengths, evict, own_kv, clean_kv):
    steps, _, features = queries.shape
    span, width = cache_kv.shape[2:]
    pairs = lax.axis_size("ca")
    chips = lax.axis_size("ha")
    rows = clean_kv.shape[1]
    tokens = pairs * chips
    bf16, f32 = jnp.bfloat16, jnp.float32
    shape = jax.ShapeDtypeStruct
    swap = [(0, 1), (1, 0)]
    pack = call(
        pack_kernel,
        shape((2 * span + 7 * rows, width), bf16),
        [SMEM] + [HBM] * 3,
        [pltpu.SemaphoreType.DMA((8,))],
        name="pack",
        limit=60,
    )(lengths, cache_kv, own_kv, clean_kv)
    far = lax.ppermute(pack, "cb", swap)
    side = lax.ppermute(pack, "hb", swap)
    cross = lax.ppermute(far, "hb", swap)
    message = call(
        spread_kernel,
        shape((tokens * PARTS, HD), bf16),
        [VMEM],
        [pltpu.VMEM((chips * PARTS, HD), f32)],
        name="spread",
    )(queries.reshape(steps, features))

    def fetch(array, mask):
        return lax.ppermute(array, "ca", [(me, me ^ mask) for me in range(pairs)]) if mask else array

    own = call(join_kernel, shape((4, rows, width), bf16), [VMEM] * 2, name="join_clean")(clean_kv, far)
    first = [fetch(own, mask) for mask in FIRST]
    recv = lax.all_to_all(
        message.reshape(tokens, PARTS, HD), ("ca", "ha"), split_axis=0, concat_axis=0, tiled=True
    ).reshape(tokens * PARTS, HD)
    parts, joint = call(
        attend_kernel,
        (shape((tokens * BACK, HD), bf16), shape((4,) + own.shape, bf16)),
        [SMEM] + [VMEM] * 9,
        [pltpu.VMEM((tokens * PARTS, HD), f32), pltpu.VMEM((tokens * BACK, HD), f32)],
        name="attend",
    )(evict, recv, pack, far, side, cross, *first)
    last = [fetch(joint, mask) for mask in LAST]
    back = lax.all_to_all(
        parts.reshape(tokens * BACK // 2, 2, HD), ("ca", "ha"), split_axis=0, concat_axis=0, tiled=True
    ).reshape(tokens * BACK, HD)
    attended = call(
        combine_kernel,
        shape((steps, features), bf16),
        [VMEM],
        [pltpu.VMEM((tokens * BACK, HD), f32)],
        name="combine",
    )(back)
    new_cache = call(renew_kernel, shape(cache_kv.shape, bf16), [SMEM] + [VMEM] * 5, name="renew_cache")(
        evict, *last, cache_kv
    )
    return (attended.reshape(steps, 1, features), new_cache)


def solution(mesh):
    ctx, heads = mesh.devices.shape
    split = jax.sharding.Mesh(mesh.devices.reshape(ctx // 2, 2, heads // 2, 2), ("ca", "cb", "ha", "hb"))
    ctx, heads = ("ca", "cb"), ("ha", "hb")
    in_specs = (
        P(None, ctx + heads, None),
        P(ctx, None, None, heads),
        P(ctx),
        P(),
        P(None, None, ctx, heads),
        P(None, ctx, heads),
    )
    out_specs = (P(None, ctx + heads, None), P(ctx, None, None, heads))
    return jax.shard_map(body, mesh=split, in_specs=in_specs, out_specs=out_specs, check_vma=False)
```

```python
import math

import jax
import jax.numpy as jnp
from jax import lax
from jax.experimental import pallas as pl
from jax.experimental.pallas import tpu as pltpu
from jax.sharding import PartitionSpec as P

HD = 128
PARTS = 8
BACK = 10
EXP2_SCALE = math.log2(math.e) / math.sqrt(HD)
NEG = -1e30
VMEM = pl.BlockSpec(memory_space=pltpu.VMEM)
SMEM = pl.BlockSpec(memory_space=pltpu.SMEM)
NT = (((1,), (1,)), ((), ()))
NN = (((1,), (0,)), ((), ()))


def spread_kernel(q_ref, out_ref, rows):
    count = rows.shape[0]
    for row in range(count):
        chip, step, head = row // PARTS, row // 4 % 2, row % 4
        start = (chip * 4 + head) * HD
        rows[row:row + 1, :] = q_ref[step:step + 1, start:start + HD].astype(jnp.float32)
    message = rows[...].astype(out_ref.dtype)
    for dest in range(out_ref.shape[0] // count):
        out_ref[dest * count:(dest + 1) * count, :] = message


def pack_kernel(length_ref, own_ref, clean_ref, pack_ref, copies_ref):
    rows = clean_ref.shape[1]
    place = 0
    for step in range(2):
        for index in range(2):
            pack_ref[place:place + rows, :] = own_ref[step, index]
            place += rows
    for index in range(2):
        pack_ref[place:place + rows, :] = clean_ref[index]
        place += rows
    length = length_ref[0]
    lane = lax.broadcasted_iota(jnp.int32, (rows, 2 * HD), 1)
    digits = jnp.where(lane < HD, length // 8, length % 8)
    pack_ref[place:place + rows, :] = digits.astype(jnp.float32).astype(pack_ref.dtype)
    for dest in range(copies_ref.shape[0]):
        copies_ref[dest] = clean_ref[...]


def attend_kernel(
    evict_ref, recv_ref, cache_ref, far_ref, side_ref, cross_ref, pack_ref, far_pack, side_pack, cross_pack, out_ref, wide, wide_out
):
    block = recv_ref.shape[0] // PARTS
    rows = 16
    span = cache_ref.shape[2]
    me = lax.axis_index("ca") * 2 + lax.axis_index("cb")
    core = lax.axis_index("hb")
    owners = [me == evict_ref[0], (me ^ 1) == evict_ref[0]]
    wide[...] = recv_ref[...].astype(jnp.float32)
    key = lax.broadcasted_iota(jnp.int32, (1, span), 1).astype(jnp.float32)
    lane = lax.broadcasted_iota(jnp.int32, (1, HD), 1)
    lengths = []
    for ref in (pack_ref, far_pack):
        digits = ref[6 * rows:7 * rows, :].astype(jnp.float32)[0:1]
        lengths.append(jnp.concatenate([digits[:, :HD] * 8.0 + digits[:, HD:]] * (span // HD), axis=1))
    ones = jnp.ones((span, HD), jnp.bfloat16)
    pad = jnp.zeros((HD - 4 * rows, 2 * HD), jnp.bfloat16)
    for step in range(2):
        biases = []
        for length, owner in zip(lengths, owners):
            bias = jnp.where(key < length, 0.0, NEG)
            biases.append(bias if step == 0 else jnp.where(owner, NEG, bias))
        extra_bias = jnp.where((lane % (2 * rows) < rows * (1 + step)) & (lane < 4 * rows), 0.0, NEG)
        stats = jnp.zeros((block, HD), jnp.float32)
        sides = (((cache_ref, far_ref), (pack_ref, far_pack)), ((side_ref, cross_ref), (side_pack, cross_pack)))
        for side, (refs, packs) in enumerate(sides):
            extras = []
            for index in range(2):
                pieces = []
                for ref in packs:
                    own = (2 * step + index) * rows
                    clean = (4 + index) * rows
                    pieces += [ref[own:own + rows, :], ref[clean:clean + rows, :]]
                extras.append(jnp.concatenate(pieces + [pad], axis=0))
            for half in range(2):
                head = (core ^ side) * 2 + half
                lanes = slice(half * HD, (half + 1) * HD)
                query = wide[pl.ds(step * 4 + head, block, stride=PARTS), :].astype(jnp.bfloat16)
                groups = [(ref[0, 0, :, lanes], ref[0, 1, :, lanes], bias) for ref, bias in zip(refs, biases)]
                groups.append((extras[0][:, lanes], extras[1][:, lanes], extra_bias))
                scores = [
                    lax.dot_general(query, keys, NT, preferred_element_type=jnp.float32) + mask
                    for keys, _, mask in groups
                ]
                top = jnp.max(scores[0], axis=1, keepdims=True)
                for score in scores[1:]:
                    top = jnp.maximum(top, jnp.max(score, axis=1, keepdims=True))
                top = jnp.ceil(top)
                accum = jnp.zeros((block, 2 * HD), jnp.float32)
                for score, (_, values, _) in zip(scores, groups):
                    weights = jnp.exp2((score - top) * EXP2_SCALE).astype(jnp.bfloat16)
                    values = jnp.concatenate([values, ones[:values.shape[0]]], axis=1)
                    accum = accum + lax.dot_general(weights, values, NN, preferred_element_type=jnp.float32)
                wide_out[pl.ds(head * 2 + step, block, stride=BACK), :] = accum[:, :HD]
                total = accum[:, HD:]
                top = jnp.broadcast_to(top, (block, HD))
                top_hi = top.astype(jnp.bfloat16).astype(jnp.float32)
                total_hi = total.astype(jnp.bfloat16).astype(jnp.float32)
                for place, value in enumerate((top_hi, top - top_hi, total_hi, total - total_hi)):
                    stats = jnp.where(lane == 32 * place + head, value, stats)
        wide_out[pl.ds(8 + step, block, stride=BACK), :] = stats
    out_ref[...] = wide_out[...].astype(jnp.bfloat16)


def combine_kernel(recv_ref, out_ref, wide):
    chips = out_ref.shape[1] // (4 * HD)
    senders = recv_ref.shape[0] // BACK
    devices = senders // chips
    wide[...] = recv_ref[...].astype(jnp.float32)

    def rows_of(place):
        return wide[pl.ds(place, senders, stride=BACK), :].reshape(devices, chips, HD)

    for step in range(2):
        stats = rows_of(8 + step)
        for head in range(4):
            local = stats[:, :, head:head + 1] + stats[:, :, 32 + head:33 + head]
            total = stats[:, :, 64 + head:65 + head] + stats[:, :, 96 + head:97 + head]
            top = jnp.max(local, axis=0, keepdims=True)
            scale = jnp.exp2((local - top) * EXP2_SCALE)
            whole = jnp.sum(scale * total, axis=0)
            result = jnp.sum(scale * rows_of(head * 2 + step), axis=0) / whole
            for chip in range(chips):
                begin = (chip * 4 + head) * HD
                out_ref[step:step + 1, begin:begin + HD] = result[chip:chip + 1].astype(jnp.bfloat16)


def renew_kernel(evict_ref, near_ref, far_ref, cache_ref, new_ref):
    devices, _, rows, _ = near_ref.shape
    parity = lax.axis_index("cb")
    owner = lax.axis_index("ca") * 2 + parity == evict_ref[0]

    @pl.when(owner)
    def _():
        for ref, kind in ((near_ref, parity), (far_ref, 1 - parity)):
            for device in range(devices):
                place = pl.ds(pl.multiple_of((device * 2 + kind) * rows, rows), rows)
                for index in range(2):
                    new_ref[0, index, place, :] = ref[device, index]

    @pl.when(jnp.logical_not(owner))
    def _():
        new_ref[...] = cache_ref[...]


def call(kernel, out_shape, in_specs, scratch=(), name=None):
    several = isinstance(out_shape, tuple)
    return pl.pallas_call(
        kernel,
        out_shape=out_shape,
        in_specs=in_specs,
        out_specs=(VMEM,) * len(out_shape) if several else VMEM,
        scratch_shapes=list(scratch),
        compiler_params=pltpu.CompilerParams(vmem_limit_bytes=40 * 1024 * 1024),
        name=name,
    )


def body(queries, cache_kv, lengths, evict, own_kv, clean_kv):
    steps, _, features = queries.shape
    span, width = cache_kv.shape[2:]
    pairs = lax.axis_size("ca")
    chips = lax.axis_size("ha")
    rows = clean_kv.shape[1]
    tokens = pairs * chips
    bf16, f32 = jnp.bfloat16, jnp.float32
    shape = jax.ShapeDtypeStruct
    swap = [(0, 1), (1, 0)]
    far = lax.ppermute(cache_kv, "cb", swap)
    side = lax.ppermute(cache_kv, "hb", swap)
    cross = lax.ppermute(far, "hb", swap)
    pack, copies = call(
        pack_kernel,
        (shape((7 * rows, width), bf16), shape((pairs,) + clean_kv.shape, bf16)),
        [SMEM] + [VMEM] * 2,
        name="pack",
    )(lengths, own_kv, clean_kv)
    packs = (
        pack,
        lax.ppermute(pack, "cb", swap),
        lax.ppermute(pack, "hb", swap),
        lax.ppermute(pack, ("cb", "hb"), [(0, 3), (1, 2), (2, 1), (3, 0)]),
    )
    message = call(
        spread_kernel,
        shape((tokens * PARTS, HD), bf16),
        [VMEM],
        [pltpu.VMEM((chips * PARTS, HD), f32)],
        name="spread_queries",
    )(queries.reshape(steps, features))
    recv = lax.all_to_all(
        message.reshape(tokens, PARTS, HD), ("ca", "ha"), split_axis=0, concat_axis=0, tiled=True
    ).reshape(tokens * PARTS, HD)
    parts = call(
        attend_kernel,
        shape((tokens * BACK, HD), bf16),
        [SMEM] + [VMEM] * 9,
        [pltpu.VMEM((tokens * PARTS, HD), f32), pltpu.VMEM((tokens * BACK, HD), f32)],
        name="attend",
    )(evict, recv, cache_kv, far, side, cross, *packs)
    _, copies = lax.optimization_barrier((recv, copies))
    near = lax.all_to_all(copies, "ca", split_axis=0, concat_axis=0, tiled=True)
    parts, near = lax.optimization_barrier((parts, near))
    back = lax.all_to_all(
        parts.reshape(tokens * BACK // 2, 2, HD), ("ca", "ha"), split_axis=0, concat_axis=0, tiled=True
    ).reshape(tokens * BACK, HD)
    attended = call(
        combine_kernel,
        shape((steps, features), bf16),
        [VMEM],
        [pltpu.VMEM((tokens * BACK, HD), f32)],
        name="combine",
    )(back)
    other = lax.ppermute(near, "cb", swap)
    new_cache = call(renew_kernel, shape(cache_kv.shape, bf16), [SMEM] + [VMEM] * 3, name="renew_cache")(
        evict, near, other, cache_kv
    )
    return (attended.reshape(steps, 1, features), new_cache)


def solution(mesh):
    ctx, heads = mesh.devices.shape
    split = jax.sharding.Mesh(mesh.devices.reshape(ctx // 2, 2, heads // 2, 2), ("ca", "cb", "ha", "hb"))
    ctx, heads = ("ca", "cb"), ("ha", "hb")
    in_specs = (
        P(None, ctx + heads, None),
        P(ctx, None, None, heads),
        P(ctx),
        P(),
        P(None, None, ctx, heads),
        P(None, ctx, heads),
    )
    out_specs = (P(None, ctx + heads, None), P(ctx, None, None, heads))
    return jax.shard_map(body, mesh=split, in_specs=in_specs, out_specs=out_specs, check_vma=False)
```

```python
import math

import jax
import jax.numpy as jnp
from jax import lax
from jax.experimental import pallas as pl
from jax.experimental.pallas import tpu as pltpu
from jax.sharding import PartitionSpec as P

HD = 128
PARTS = 8
BACK = 10
EXP2_SCALE = math.log2(math.e) / math.sqrt(HD)
NEG = -1e30
VMEM = pl.BlockSpec(memory_space=pltpu.VMEM)
SMEM = pl.BlockSpec(memory_space=pltpu.SMEM)
HBM = pl.BlockSpec(memory_space=pltpu.HBM)
NT = (((1,), (1,)), ((), ()))
NN = (((1,), (0,)), ((), ()))


def spread_kernel(q_ref, clean_ref, out_ref, copies_ref, rows):
    count = rows.shape[0]
    for row in range(count):
        chip, step, head = row // PARTS, row // 4 % 2, row % 4
        start = (chip * 4 + head) * HD
        rows[row:row + 1, :] = q_ref[step:step + 1, start:start + HD].astype(jnp.float32)
    message = rows[...].astype(out_ref.dtype)
    for dest in range(out_ref.shape[0] // count):
        out_ref[dest * count:(dest + 1) * count, :] = message
        copies_ref[dest] = clean_ref[...]


def pack_kernel(length_ref, cache_ref, own_ref, clean_ref, pack_ref, digit_rows, sems):
    span, rows = cache_ref.shape[2], clean_ref.shape[1]
    pieces = [(cache_ref.at[0, index], span) for index in range(2)]
    pieces += [(own_ref.at[step, index], rows) for step in range(2) for index in range(2)]
    pieces += [(clean_ref.at[index], rows) for index in range(2)]
    pieces += [(digit_rows, rows)]
    length = length_ref[0]
    lane = lax.broadcasted_iota(jnp.int32, (rows, 2 * HD), 1)
    digits = jnp.where(lane < HD, length // 8, length % 8)
    digit_rows[...] = digits.astype(jnp.float32).astype(digit_rows.dtype)
    place, copies = 0, []
    for number, (piece, count) in enumerate(pieces):
        copies.append(pltpu.make_async_copy(piece, pack_ref.at[pl.ds(place, count)], sems.at[number]))
        copies[-1].start()
        place += count
    for copy in copies:
        copy.wait()


def attend_kernel(evict_ref, recv_ref, pack_ref, far_ref, side_ref, cross_ref, out_ref, wide, wide_out):
    block = recv_ref.shape[0] // PARTS
    rows = 16
    span = (pack_ref.shape[0] - 7 * rows) // 2
    tail = 2 * span
    me = lax.axis_index("ca") * 2 + lax.axis_index("cb")
    core = lax.axis_index("hb")
    owners = [me == evict_ref[0], (me ^ 1) == evict_ref[0]]
    wide[...] = recv_ref[...].astype(jnp.float32)
    key = lax.broadcasted_iota(jnp.int32, (1, span), 1).astype(jnp.float32)
    lane = lax.broadcasted_iota(jnp.int32, (1, HD), 1)
    lengths = []
    for ref in (pack_ref, far_ref):
        digits = ref[tail + 6 * rows:tail + 7 * rows, :].astype(jnp.float32)[0:1]
        lengths.append(jnp.concatenate([digits[:, :HD] * 8.0 + digits[:, HD:]] * (span // HD), axis=1))
    ones = jnp.ones((span, HD), jnp.bfloat16)
    pad = jnp.zeros((HD - 4 * rows, 2 * HD), jnp.bfloat16)
    for step in range(2):
        biases = []
        for length, owner in zip(lengths, owners):
            bias = jnp.where(key < length, 0.0, NEG)
            biases.append(bias if step == 0 else jnp.where(owner, NEG, bias))
        extra_bias = jnp.where((lane % (2 * rows) < rows * (1 + step)) & (lane < 4 * rows), 0.0, NEG)
        stats = jnp.zeros((block, HD), jnp.float32)
        for side, refs in enumerate(((pack_ref, far_ref), (side_ref, cross_ref))):
            extras = []
            for index in range(2):
                pieces = []
                for ref in refs:
                    own = tail + (2 * step + index) * rows
                    clean = tail + (4 + index) * rows
                    pieces += [ref[own:own + rows, :], ref[clean:clean + rows, :]]
                extras.append(jnp.concatenate(pieces + [pad], axis=0))
            for half in range(2):
                head = (core ^ side) * 2 + half
                lanes = slice(half * HD, (half + 1) * HD)
                query = wide[pl.ds(step * 4 + head, block, stride=PARTS), :].astype(jnp.bfloat16)
                groups = [(ref[0:span, lanes], ref[span:2 * span, lanes], bias) for ref, bias in zip(refs, biases)]
                groups.append((extras[0][:, lanes], extras[1][:, lanes], extra_bias))
                scores = [
                    lax.dot_general(query, keys, NT, preferred_element_type=jnp.float32) + mask
                    for keys, _, mask in groups
                ]
                top = jnp.max(scores[0], axis=1, keepdims=True)
                for score in scores[1:]:
                    top = jnp.maximum(top, jnp.max(score, axis=1, keepdims=True))
                top = jnp.ceil(top)
                accum = jnp.zeros((block, 2 * HD), jnp.float32)
                for score, (_, values, _) in zip(scores, groups):
                    weights = jnp.exp2((score - top) * EXP2_SCALE).astype(jnp.bfloat16)
                    values = jnp.concatenate([values, ones[:values.shape[0]]], axis=1)
                    accum = accum + lax.dot_general(weights, values, NN, preferred_element_type=jnp.float32)
                wide_out[pl.ds(head * 2 + step, block, stride=BACK), :] = accum[:, :HD]
                total = accum[:, HD:]
                top = jnp.broadcast_to(top, (block, HD))
                top_hi = top.astype(jnp.bfloat16).astype(jnp.float32)
                total_hi = total.astype(jnp.bfloat16).astype(jnp.float32)
                for place, value in enumerate((top_hi, top - top_hi, total_hi, total - total_hi)):
                    stats = jnp.where(lane == 32 * place + head, value, stats)
        wide_out[pl.ds(8 + step, block, stride=BACK), :] = stats
    out_ref[...] = wide_out[...].astype(jnp.bfloat16)


def combine_kernel(recv_ref, out_ref, wide):
    chips = out_ref.shape[1] // (4 * HD)
    senders = recv_ref.shape[0] // BACK
    devices = senders // chips
    wide[...] = recv_ref[...].astype(jnp.float32)

    def rows_of(place):
        return wide[pl.ds(place, senders, stride=BACK), :].reshape(devices, chips, HD)

    for step in range(2):
        stats = rows_of(8 + step)
        for head in range(4):
            local = stats[:, :, head:head + 1] + stats[:, :, 32 + head:33 + head]
            total = stats[:, :, 64 + head:65 + head] + stats[:, :, 96 + head:97 + head]
            top = jnp.max(local, axis=0, keepdims=True)
            scale = jnp.exp2((local - top) * EXP2_SCALE)
            whole = jnp.sum(scale * total, axis=0)
            result = jnp.sum(scale * rows_of(head * 2 + step), axis=0) / whole
            for chip in range(chips):
                begin = (chip * 4 + head) * HD
                out_ref[step:step + 1, begin:begin + HD] = result[chip:chip + 1].astype(jnp.bfloat16)


def renew_kernel(evict_ref, near_ref, far_ref, cache_ref, new_ref):
    devices, _, rows, _ = near_ref.shape
    parity = lax.axis_index("cb")
    owner = lax.axis_index("ca") * 2 + parity == evict_ref[0]

    @pl.when(owner)
    def _():
        for ref, kind in ((near_ref, parity), (far_ref, 1 - parity)):
            for device in range(devices):
                place = pl.ds(pl.multiple_of((device * 2 + kind) * rows, rows), rows)
                for index in range(2):
                    new_ref[0, index, place, :] = ref[device, index]

    @pl.when(jnp.logical_not(owner))
    def _():
        new_ref[...] = cache_ref[...]


def call(kernel, out_shape, in_specs, scratch=(), name=None, limit=40, out=VMEM):
    several = isinstance(out_shape, tuple)
    return pl.pallas_call(
        kernel,
        out_shape=out_shape,
        in_specs=in_specs,
        out_specs=(out,) * len(out_shape) if several else out,
        scratch_shapes=list(scratch),
        compiler_params=pltpu.CompilerParams(vmem_limit_bytes=limit * 1024 * 1024),
        name=name,
    )


def body(queries, cache_kv, lengths, evict, own_kv, clean_kv):
    steps, _, features = queries.shape
    span, width = cache_kv.shape[2:]
    pairs = lax.axis_size("ca")
    chips = lax.axis_size("ha")
    rows = clean_kv.shape[1]
    tokens = pairs * chips
    bf16, f32 = jnp.bfloat16, jnp.float32
    shape = jax.ShapeDtypeStruct
    swap = [(0, 1), (1, 0)]
    pack = call(
        pack_kernel,
        shape((2 * span + 7 * rows, width), bf16),
        [SMEM] + [HBM] * 3,
        [pltpu.VMEM((rows, width), bf16), pltpu.SemaphoreType.DMA((9,))],
        name="pack",
        limit=60,
        out=HBM,
    )(lengths, cache_kv, own_kv, clean_kv)
    far = lax.ppermute(pack, "cb", swap)
    side = lax.ppermute(pack, "hb", swap)
    cross = lax.ppermute(far, "hb", swap)
    message, copies = call(
        spread_kernel,
        (shape((tokens * PARTS, HD), bf16), shape((pairs,) + clean_kv.shape, bf16)),
        [VMEM] * 2,
        [pltpu.VMEM((chips * PARTS, HD), f32)],
        name="spread",
    )(queries.reshape(steps, features), clean_kv)
    recv = lax.all_to_all(
        message.reshape(tokens, PARTS, HD), ("ca", "ha"), split_axis=0, concat_axis=0, tiled=True
    ).reshape(tokens * PARTS, HD)
    parts = call(
        attend_kernel,
        shape((tokens * BACK, HD), bf16),
        [SMEM] + [VMEM] * 5,
        [pltpu.VMEM((tokens * PARTS, HD), f32), pltpu.VMEM((tokens * BACK, HD), f32)],
        name="attend",
    )(evict, recv, pack, far, side, cross)
    _, copies = lax.optimization_barrier((recv, copies))
    near = lax.all_to_all(copies, "ca", split_axis=0, concat_axis=0, tiled=True)
    parts, near = lax.optimization_barrier((parts, near))
    back = lax.all_to_all(
        parts.reshape(tokens * BACK // 2, 2, HD), ("ca", "ha"), split_axis=0, concat_axis=0, tiled=True
    ).reshape(tokens * BACK, HD)
    attended = call(
        combine_kernel,
        shape((steps, features), bf16),
        [VMEM],
        [pltpu.VMEM((tokens * BACK, HD), f32)],
        name="combine",
    )(back)
    other = lax.ppermute(near, "cb", swap)
    new_cache = call(renew_kernel, shape(cache_kv.shape, bf16), [SMEM] + [VMEM] * 3, name="renew_cache")(
        evict, near, other, cache_kv
    )
    return (attended.reshape(steps, 1, features), new_cache)


def solution(mesh):
    ctx, heads = mesh.devices.shape
    split = jax.sharding.Mesh(mesh.devices.reshape(ctx // 2, 2, heads // 2, 2), ("ca", "cb", "ha", "hb"))
    ctx, heads = ("ca", "cb"), ("ha", "hb")
    in_specs = (
        P(None, ctx + heads, None),
        P(ctx, None, None, heads),
        P(ctx),
        P(),
        P(None, None, ctx, heads),
        P(None, ctx, heads),
    )
    out_specs = (P(None, ctx + heads, None), P(ctx, None, None, heads))
    return jax.shard_map(body, mesh=split, in_specs=in_specs, out_specs=out_specs, check_vma=False)
```

```python
import math

import jax
import jax.numpy as jnp
from jax import lax
from jax.experimental import pallas as pl
from jax.experimental.pallas import tpu as pltpu
from jax.sharding import PartitionSpec as P

HD = 128
PARTS = 8
BACK = 10
EXP2_SCALE = math.log2(math.e) / math.sqrt(HD)
NEG = -1e30
VMEM = pl.BlockSpec(memory_space=pltpu.VMEM)
SMEM = pl.BlockSpec(memory_space=pltpu.SMEM)
HBM = pl.BlockSpec(memory_space=pltpu.HBM)
NT = (((1,), (1,)), ((), ()))
NN = (((1,), (0,)), ((), ()))


def spread_kernel(q_ref, clean_ref, out_ref, copies_ref, rows):
    count = rows.shape[0]
    for row in range(count):
        chip, step, head = row // PARTS, row // 4 % 2, row % 4
        start = (chip * 4 + head) * HD
        rows[row:row + 1, :] = q_ref[step:step + 1, start:start + HD].astype(jnp.float32)
    message = rows[...].astype(out_ref.dtype)
    for dest in range(out_ref.shape[0] // count):
        out_ref[dest * count:(dest + 1) * count, :] = message
        copies_ref[dest] = clean_ref[...]


def pack_kernel(length_ref, cache_ref, own_ref, clean_ref, pack_ref, digit_rows, sems):
    span, rows = cache_ref.shape[2], clean_ref.shape[1]
    pieces = [(cache_ref.at[0, index], span) for index in range(2)]
    pieces += [(own_ref.at[step, index], rows) for step in range(2) for index in range(2)]
    pieces += [(clean_ref.at[index], rows) for index in range(2)]
    pieces += [(digit_rows, rows)]
    length = length_ref[0]
    lane = lax.broadcasted_iota(jnp.int32, (rows, 2 * HD), 1)
    digits = jnp.where(lane < HD, length // 8, length % 8)
    digit_rows[...] = digits.astype(jnp.float32).astype(digit_rows.dtype)
    place, copies = 0, []
    for number, (piece, count) in enumerate(pieces):
        copies.append(pltpu.make_async_copy(piece, pack_ref.at[pl.ds(place, count)], sems.at[number]))
        copies[-1].start()
        place += count
    for copy in copies:
        copy.wait()


def attend_kernel(evict_ref, recv_ref, pack_ref, far_ref, side_ref, cross_ref, out_ref, wide, wide_out):
    block = recv_ref.shape[0] // PARTS
    rows = 16
    span = (pack_ref.shape[0] - 7 * rows) // 2
    tail = 2 * span
    me = lax.axis_index("ca") * 2 + lax.axis_index("cb")
    core = lax.axis_index("hb")
    owners = [me == evict_ref[0], (me ^ 1) == evict_ref[0]]
    wide[...] = recv_ref[...].astype(jnp.float32)
    key = lax.broadcasted_iota(jnp.int32, (1, span), 1).astype(jnp.float32)
    lane = lax.broadcasted_iota(jnp.int32, (1, HD), 1)
    lengths = []
    for ref in (pack_ref, far_ref):
        digits = ref[tail + 6 * rows:tail + 7 * rows, :].astype(jnp.float32)[0:1]
        lengths.append(jnp.concatenate([digits[:, :HD] * 8.0 + digits[:, HD:]] * (span // HD), axis=1))
    ones = jnp.ones((span, HD), jnp.bfloat16)
    pad = jnp.zeros((HD - 4 * rows, 2 * HD), jnp.bfloat16)
    for step in range(2):
        biases = []
        for length, owner in zip(lengths, owners):
            bias = jnp.where(key < length, 0.0, NEG)
            biases.append(bias if step == 0 else jnp.where(owner, NEG, bias))
        extra_bias = jnp.where((lane % (2 * rows) < rows * (1 + step)) & (lane < 4 * rows), 0.0, NEG)
        stats = jnp.zeros((block, HD), jnp.float32)
        for side, refs in enumerate(((pack_ref, far_ref), (side_ref, cross_ref))):
            extras = []
            for index in range(2):
                pieces = []
                for ref in refs:
                    own = tail + (2 * step + index) * rows
                    clean = tail + (4 + index) * rows
                    pieces += [ref[own:own + rows, :], ref[clean:clean + rows, :]]
                extras.append(jnp.concatenate(pieces + [pad], axis=0))
            for half in range(2):
                head = (core ^ side) * 2 + half
                lanes = slice(half * HD, (half + 1) * HD)
                query = wide[pl.ds(step * 4 + head, block, stride=PARTS), :].astype(jnp.bfloat16)
                groups = [(ref[0:span, lanes], ref[span:2 * span, lanes], bias) for ref, bias in zip(refs, biases)]
                groups.append((extras[0][:, lanes], extras[1][:, lanes], extra_bias))
                scores = [
                    lax.dot_general(query, keys, NT, preferred_element_type=jnp.float32) + mask
                    for keys, _, mask in groups
                ]
                top = jnp.max(scores[0], axis=1, keepdims=True)
                for score in scores[1:]:
                    top = jnp.maximum(top, jnp.max(score, axis=1, keepdims=True))
                top = jnp.ceil(top)
                accum = jnp.zeros((block, 2 * HD), jnp.float32)
                for score, (_, values, _) in zip(scores, groups):
                    weights = jnp.exp2((score - top) * EXP2_SCALE).astype(jnp.bfloat16)
                    values = jnp.concatenate([values, ones[:values.shape[0]]], axis=1)
                    accum = accum + lax.dot_general(weights, values, NN, preferred_element_type=jnp.float32)
                wide_out[pl.ds(head * 2 + step, block, stride=BACK), :] = accum[:, :HD]
                total = accum[:, HD:]
                top = jnp.broadcast_to(top, (block, HD))
                top_hi = top.astype(jnp.bfloat16).astype(jnp.float32)
                total_hi = total.astype(jnp.bfloat16).astype(jnp.float32)
                for place, value in enumerate((top_hi, top - top_hi, total_hi, total - total_hi)):
                    stats = jnp.where(lane == 32 * place + head, value, stats)
        wide_out[pl.ds(8 + step, block, stride=BACK), :] = stats
    out_ref[...] = wide_out[...].astype(jnp.bfloat16)


def combine_kernel(recv_ref, out_ref, wide):
    chips = out_ref.shape[1] // (4 * HD)
    senders = recv_ref.shape[0] // BACK
    devices = senders // chips
    wide[...] = recv_ref[...].astype(jnp.float32)

    def rows_of(place):
        return wide[pl.ds(place, senders, stride=BACK), :].reshape(devices, chips, HD)

    for step in range(2):
        stats = rows_of(8 + step)
        for head in range(4):
            local = stats[:, :, head:head + 1] + stats[:, :, 32 + head:33 + head]
            total = stats[:, :, 64 + head:65 + head] + stats[:, :, 96 + head:97 + head]
            top = jnp.max(local, axis=0, keepdims=True)
            scale = jnp.exp2((local - top) * EXP2_SCALE)
            whole = jnp.sum(scale * total, axis=0)
            result = jnp.sum(scale * rows_of(head * 2 + step), axis=0) / whole
            for chip in range(chips):
                begin = (chip * 4 + head) * HD
                out_ref[step:step + 1, begin:begin + HD] = result[chip:chip + 1].astype(jnp.bfloat16)


def renew_kernel(evict_ref, near_ref, far_ref, cache_ref, new_ref):
    devices, _, rows, _ = near_ref.shape
    parity = lax.axis_index("cb")
    owner = lax.axis_index("ca") * 2 + parity == evict_ref[0]

    @pl.when(owner)
    def _():
        for ref, kind in ((near_ref, parity), (far_ref, 1 - parity)):
            for device in range(devices):
                place = pl.ds(pl.multiple_of((device * 2 + kind) * rows, rows), rows)
                for index in range(2):
                    new_ref[0, index, place, :] = ref[device, index]

    @pl.when(jnp.logical_not(owner))
    def _():
        new_ref[...] = cache_ref[...]


def call(kernel, out_shape, in_specs, scratch=(), name=None, limit=40, out=VMEM):
    several = isinstance(out_shape, tuple)
    return pl.pallas_call(
        kernel,
        out_shape=out_shape,
        in_specs=in_specs,
        out_specs=(out,) * len(out_shape) if several else out,
        scratch_shapes=list(scratch),
        compiler_params=pltpu.CompilerParams(vmem_limit_bytes=limit * 1024 * 1024),
        name=name,
    )


def body(queries, cache_kv, lengths, evict, own_kv, clean_kv):
    steps, _, features = queries.shape
    span, width = cache_kv.shape[2:]
    pairs = lax.axis_size("ca")
    chips = lax.axis_size("ha")
    rows = clean_kv.shape[1]
    tokens = pairs * chips
    bf16, f32 = jnp.bfloat16, jnp.float32
    shape = jax.ShapeDtypeStruct
    swap = [(0, 1), (1, 0)]
    pack = call(
        pack_kernel,
        shape((2 * span + 7 * rows, width), bf16),
        [SMEM] + [HBM] * 3,
        [pltpu.VMEM((rows, width), bf16), pltpu.SemaphoreType.DMA((9,))],
        name="pack",
        limit=60,
    )(lengths, cache_kv, own_kv, clean_kv)
    far = lax.ppermute(pack, "cb", swap)
    side = lax.ppermute(pack, "hb", swap)
    cross = lax.ppermute(far, "hb", swap)
    message, copies = call(
        spread_kernel,
        (shape((tokens * PARTS, HD), bf16), shape((pairs,) + clean_kv.shape, bf16)),
        [VMEM] * 2,
        [pltpu.VMEM((chips * PARTS, HD), f32)],
        name="spread",
    )(queries.reshape(steps, features), clean_kv)
    recv = lax.all_to_all(
        message.reshape(tokens, PARTS, HD), ("ca", "ha"), split_axis=0, concat_axis=0, tiled=True
    ).reshape(tokens * PARTS, HD)
    parts = call(
        attend_kernel,
        shape((tokens * BACK, HD), bf16),
        [SMEM] + [VMEM] * 5,
        [pltpu.VMEM((tokens * PARTS, HD), f32), pltpu.VMEM((tokens * BACK, HD), f32)],
        name="attend",
    )(evict, recv, pack, far, side, cross)
    _, copies = lax.optimization_barrier((recv, copies))
    near = lax.all_to_all(copies, "ca", split_axis=0, concat_axis=0, tiled=True)
    parts, near = lax.optimization_barrier((parts, near))
    back = lax.all_to_all(
        parts.reshape(tokens * BACK // 2, 2, HD), ("ca", "ha"), split_axis=0, concat_axis=0, tiled=True
    ).reshape(tokens * BACK, HD)
    attended = call(
        combine_kernel,
        shape((steps, features), bf16),
        [VMEM],
        [pltpu.VMEM((tokens * BACK, HD), f32)],
        name="combine",
    )(back)
    other = lax.ppermute(near, "cb", swap)
    new_cache = call(renew_kernel, shape(cache_kv.shape, bf16), [SMEM] + [VMEM] * 3, name="renew_cache")(
        evict, near, other, cache_kv
    )
    return (attended.reshape(steps, 1, features), new_cache)


def solution(mesh):
    ctx, heads = mesh.devices.shape
    split = jax.sharding.Mesh(mesh.devices.reshape(ctx // 2, 2, heads // 2, 2), ("ca", "cb", "ha", "hb"))
    ctx, heads = ("ca", "cb"), ("ha", "hb")
    in_specs = (
        P(None, ctx + heads, None),
        P(ctx, None, None, heads),
        P(ctx),
        P(),
        P(None, None, ctx, heads),
        P(None, ctx, heads),
    )
    out_specs = (P(None, ctx + heads, None), P(ctx, None, None, heads))
    return jax.shard_map(body, mesh=split, in_specs=in_specs, out_specs=out_specs, check_vma=False)
```

```python
import math

import jax
import jax.numpy as jnp
from jax import lax
from jax.experimental import pallas as pl
from jax.experimental.pallas import tpu as pltpu
from jax.sharding import PartitionSpec as P

HD = 128
PARTS = 8
BACK = 10
EXP2_SCALE = math.log2(math.e) / math.sqrt(HD)
NEG = -1e30
VMEM = pl.BlockSpec(memory_space=pltpu.VMEM)
SMEM = pl.BlockSpec(memory_space=pltpu.SMEM)
HBM = pl.BlockSpec(memory_space=pltpu.HBM)
NT = (((1,), (1,)), ((), ()))
NN = (((1,), (0,)), ((), ()))


def spread_kernel(q_ref, clean_ref, out_ref, copies_ref, rows):
    count = rows.shape[0]
    for row in range(count):
        chip, step, head = row // PARTS, row // 4 % 2, row % 4
        start = (chip * 4 + head) * HD
        rows[row:row + 1, :] = q_ref[step:step + 1, start:start + HD].astype(jnp.float32)
    message = rows[...].astype(out_ref.dtype)
    for dest in range(out_ref.shape[0] // count):
        out_ref[dest * count:(dest + 1) * count, :] = message
        copies_ref[dest] = clean_ref[...]


def pack_kernel(length_ref, cache_ref, own_ref, clean_ref, pack_ref, digit_rows, sems):
    span, rows = cache_ref.shape[2], clean_ref.shape[1]
    pieces = [(cache_ref.at[0, index], span) for index in range(2)]
    pieces += [(own_ref.at[step, index], rows) for step in range(2) for index in range(2)]
    pieces += [(clean_ref.at[index], rows) for index in range(2)]
    pieces += [(digit_rows, rows)]
    length = length_ref[0]
    lane = lax.broadcasted_iota(jnp.int32, (rows, 2 * HD), 1)
    digits = jnp.where(lane < HD, length // 8, length % 8)
    digit_rows[...] = digits.astype(jnp.float32).astype(digit_rows.dtype)
    place, copies = 0, []
    for number, (piece, count) in enumerate(pieces):
        copies.append(pltpu.make_async_copy(piece, pack_ref.at[pl.ds(place, count)], sems.at[number]))
        copies[-1].start()
        place += count
    for copy in copies:
        copy.wait()


def attend_kernel(evict_ref, recv_ref, pack_ref, far_ref, side_ref, cross_ref, out_ref, wide, wide_out):
    block = recv_ref.shape[0] // PARTS
    rows = 16
    span = (pack_ref.shape[0] - 7 * rows) // 2
    tail = 2 * span
    me = lax.axis_index("ca") * 2 + lax.axis_index("cb")
    core = lax.axis_index("hb")
    owners = [me == evict_ref[0], (me ^ 1) == evict_ref[0]]
    wide[...] = recv_ref[...].astype(jnp.float32)
    key = lax.broadcasted_iota(jnp.int32, (1, span), 1).astype(jnp.float32)
    lane = lax.broadcasted_iota(jnp.int32, (1, HD), 1)
    lengths = []
    for ref in (pack_ref, far_ref):
        digits = ref[tail + 6 * rows:tail + 7 * rows, :].astype(jnp.float32)[0:1]
        lengths.append(jnp.concatenate([digits[:, :HD] * 8.0 + digits[:, HD:]] * (span // HD), axis=1))
    ones = jnp.ones((span, HD), jnp.bfloat16)
    pad = jnp.zeros((HD - 4 * rows, 2 * HD), jnp.bfloat16)
    for step in range(2):
        biases = []
        for length, owner in zip(lengths, owners):
            bias = jnp.where(key < length, 0.0, NEG)
            biases.append(bias if step == 0 else jnp.where(owner, NEG, bias))
        extra_bias = jnp.where((lane % (2 * rows) < rows * (1 + step)) & (lane < 4 * rows), 0.0, NEG)
        stats = jnp.zeros((block, HD), jnp.float32)
        for side, refs in enumerate(((pack_ref, far_ref), (side_ref, cross_ref))):
            extras = []
            for index in range(2):
                pieces = []
                for ref in refs:
                    own = tail + (2 * step + index) * rows
                    clean = tail + (4 + index) * rows
                    pieces += [ref[own:own + rows, :], ref[clean:clean + rows, :]]
                extras.append(jnp.concatenate(pieces + [pad], axis=0))
            for half in range(2):
                head = (core ^ side) * 2 + half
                lanes = slice(half * HD, (half + 1) * HD)
                query = wide[pl.ds(step * 4 + head, block, stride=PARTS), :].astype(jnp.bfloat16)
                groups = [(ref[0:span, lanes], ref[span:2 * span, lanes], bias) for ref, bias in zip(refs, biases)]
                groups.append((extras[0][:, lanes], extras[1][:, lanes], extra_bias))
                scores = [
                    lax.dot_general(query, keys, NT, preferred_element_type=jnp.float32) + mask
                    for keys, _, mask in groups
                ]
                top = jnp.max(scores[0], axis=1, keepdims=True)
                for score in scores[1:]:
                    top = jnp.maximum(top, jnp.max(score, axis=1, keepdims=True))
                top = jnp.ceil(top)
                accum = jnp.zeros((block, 2 * HD), jnp.float32)
                for score, (_, values, _) in zip(scores, groups):
                    weights = jnp.exp2((score - top) * EXP2_SCALE).astype(jnp.bfloat16)
                    values = jnp.concatenate([values, ones[:values.shape[0]]], axis=1)
                    accum = accum + lax.dot_general(weights, values, NN, preferred_element_type=jnp.float32)
                wide_out[pl.ds(head * 2 + step, block, stride=BACK), :] = accum[:, :HD]
                total = accum[:, HD:]
                top = jnp.broadcast_to(top, (block, HD))
                top_hi = top.astype(jnp.bfloat16).astype(jnp.float32)
                total_hi = total.astype(jnp.bfloat16).astype(jnp.float32)
                for place, value in enumerate((top_hi, top - top_hi, total_hi, total - total_hi)):
                    stats = jnp.where(lane == 32 * place + head, value, stats)
        wide_out[pl.ds(8 + step, block, stride=BACK), :] = stats
    out_ref[...] = wide_out[...].astype(jnp.bfloat16)


def combine_kernel(recv_ref, out_ref, wide):
    chips = out_ref.shape[1] // (4 * HD)
    senders = recv_ref.shape[0] // BACK
    devices = senders // chips
    wide[...] = recv_ref[...].astype(jnp.float32)

    def rows_of(place):
        return wide[pl.ds(place, senders, stride=BACK), :].reshape(devices, chips, HD)

    for step in range(2):
        stats = rows_of(8 + step)
        for head in range(4):
            local = stats[:, :, head:head + 1] + stats[:, :, 32 + head:33 + head]
            total = stats[:, :, 64 + head:65 + head] + stats[:, :, 96 + head:97 + head]
            top = jnp.max(local, axis=0, keepdims=True)
            scale = jnp.exp2((local - top) * EXP2_SCALE)
            whole = jnp.sum(scale * total, axis=0)
            result = jnp.sum(scale * rows_of(head * 2 + step), axis=0) / whole
            for chip in range(chips):
                begin = (chip * 4 + head) * HD
                out_ref[step:step + 1, begin:begin + HD] = result[chip:chip + 1].astype(jnp.bfloat16)


def renew_kernel(evict_ref, near_ref, far_ref, cache_ref, new_ref):
    devices, _, rows, _ = near_ref.shape
    parity = lax.axis_index("cb")
    owner = lax.axis_index("ca") * 2 + parity == evict_ref[0]

    @pl.when(owner)
    def _():
        for ref, kind in ((near_ref, parity), (far_ref, 1 - parity)):
            for device in range(devices):
                place = pl.ds(pl.multiple_of((device * 2 + kind) * rows, rows), rows)
                for index in range(2):
                    new_ref[0, index, place, :] = ref[device, index]

    @pl.when(jnp.logical_not(owner))
    def _():
        new_ref[...] = cache_ref[...]


def call(kernel, out_shape, in_specs, scratch=(), name=None, limit=40, out=VMEM):
    several = isinstance(out_shape, tuple)
    return pl.pallas_call(
        kernel,
        out_shape=out_shape,
        in_specs=in_specs,
        out_specs=(out,) * len(out_shape) if several else out,
        scratch_shapes=list(scratch),
        compiler_params=pltpu.CompilerParams(vmem_limit_bytes=limit * 1024 * 1024),
        name=name,
    )


def body(queries, cache_kv, lengths, evict, own_kv, clean_kv):
    steps, _, features = queries.shape
    span, width = cache_kv.shape[2:]
    pairs = lax.axis_size("ca")
    chips = lax.axis_size("ha")
    rows = clean_kv.shape[1]
    tokens = pairs * chips
    bf16, f32 = jnp.bfloat16, jnp.float32
    shape = jax.ShapeDtypeStruct
    swap = [(0, 1), (1, 0)]
    pack = call(
        pack_kernel,
        shape((2 * span + 7 * rows, width), bf16),
        [SMEM] + [HBM] * 3,
        [pltpu.VMEM((rows, width), bf16), pltpu.SemaphoreType.DMA((9,))],
        name="pack",
        limit=60,
    )(lengths, cache_kv, own_kv, clean_kv)
    far = lax.ppermute(pack, "cb", swap)
    side = lax.ppermute(pack, "hb", swap)
    message, copies = call(
        spread_kernel,
        (shape((tokens * PARTS, HD), bf16), shape((pairs,) + clean_kv.shape, bf16)),
        [VMEM] * 2,
        [pltpu.VMEM((chips * PARTS, HD), f32)],
        name="spread",
    )(queries.reshape(steps, features), clean_kv)
    recv = lax.all_to_all(
        message.reshape(tokens, PARTS, HD), ("ca", "ha"), split_axis=0, concat_axis=0, tiled=True
    ).reshape(tokens * PARTS, HD)
    recv, late_far = lax.optimization_barrier((recv, far))
    cross = lax.ppermute(late_far, "hb", swap)
    parts = call(
        attend_kernel,
        shape((tokens * BACK, HD), bf16),
        [SMEM] + [VMEM] * 5,
        [pltpu.VMEM((tokens * PARTS, HD), f32), pltpu.VMEM((tokens * BACK, HD), f32)],
        name="attend",
    )(evict, recv, pack, far, side, cross)
    _, copies = lax.optimization_barrier((recv, copies))
    near = lax.all_to_all(copies, "ca", split_axis=0, concat_axis=0, tiled=True)
    parts, near = lax.optimization_barrier((parts, near))
    back = lax.all_to_all(
        parts.reshape(tokens * BACK // 2, 2, HD), ("ca", "ha"), split_axis=0, concat_axis=0, tiled=True
    ).reshape(tokens * BACK, HD)
    attended = call(
        combine_kernel,
        shape((steps, features), bf16),
        [VMEM],
        [pltpu.VMEM((tokens * BACK, HD), f32)],
        name="combine",
    )(back)
    other = lax.ppermute(near, "cb", swap)
    new_cache = call(renew_kernel, shape(cache_kv.shape, bf16), [SMEM] + [VMEM] * 3, name="renew_cache")(
        evict, near, other, cache_kv
    )
    return (attended.reshape(steps, 1, features), new_cache)


def solution(mesh):
    ctx, heads = mesh.devices.shape
    split = jax.sharding.Mesh(mesh.devices.reshape(ctx // 2, 2, heads // 2, 2), ("ca", "cb", "ha", "hb"))
    ctx, heads = ("ca", "cb"), ("ha", "hb")
    in_specs = (
        P(None, ctx + heads, None),
        P(ctx, None, None, heads),
        P(ctx),
        P(),
        P(None, None, ctx, heads),
        P(None, ctx, heads),
    )
    out_specs = (P(None, ctx + heads, None), P(ctx, None, None, heads))
    return jax.shard_map(body, mesh=split, in_specs=in_specs, out_specs=out_specs, check_vma=False)
```

```python
import math

import jax
import jax.numpy as jnp
from jax import lax
from jax.experimental import pallas as pl
from jax.experimental.pallas import tpu as pltpu
from jax.sharding import PartitionSpec as P

HD = 128
PARTS = 8
BACK = 10
EXP2_SCALE = math.log2(math.e) / math.sqrt(HD)
NEG = -1e30
VMEM = pl.BlockSpec(memory_space=pltpu.VMEM)
SMEM = pl.BlockSpec(memory_space=pltpu.SMEM)
HBM = pl.BlockSpec(memory_space=pltpu.HBM)
NT = (((1,), (1,)), ((), ()))
NN = (((1,), (0,)), ((), ()))


def spread_kernel(q_ref, clean_ref, out_ref, copies_ref, rows):
    count = rows.shape[0]
    for head in range(count // 2):
        piece = q_ref[:, head * HD:(head + 1) * HD].astype(jnp.float32)
        rows[pl.ds(head // 4 * PARTS + head % 4, 2, stride=4), :] = piece
    message = rows[...].astype(out_ref.dtype)
    for dest in range(out_ref.shape[0] // count):
        out_ref[dest * count:(dest + 1) * count, :] = message
        copies_ref[dest] = clean_ref[...]


def pack_kernel(length_ref, cache_ref, own_ref, clean_ref, pack_ref, digit_rows, sems):
    span, rows = cache_ref.shape[2], clean_ref.shape[1]
    pieces = [(cache_ref.at[0, index], span) for index in range(2)]
    pieces += [(own_ref.at[step, index], rows) for step in range(2) for index in range(2)]
    pieces += [(clean_ref.at[index], rows) for index in range(2)]
    pieces += [(digit_rows, rows)]
    length = length_ref[0]
    lane = lax.broadcasted_iota(jnp.int32, (rows, 2 * HD), 1)
    digits = jnp.where(lane < HD, length // 8, length % 8)
    digit_rows[...] = digits.astype(jnp.float32).astype(digit_rows.dtype)
    place, copies = 0, []
    for number, (piece, count) in enumerate(pieces):
        copies.append(pltpu.make_async_copy(piece, pack_ref.at[pl.ds(place, count)], sems.at[number]))
        copies[-1].start()
        place += count
    for copy in copies:
        copy.wait()


def attend_kernel(evict_ref, recv_ref, pack_ref, far_ref, side_ref, cross_ref, out_ref, wide, wide_out):
    block = recv_ref.shape[0] // PARTS
    rows = 16
    span = (pack_ref.shape[0] - 7 * rows) // 2
    tail = 2 * span
    me = lax.axis_index("ca") * 2 + lax.axis_index("cb")
    core = lax.axis_index("hb")
    owners = [me == evict_ref[0], (me ^ 1) == evict_ref[0]]
    wide[...] = recv_ref[...].astype(jnp.float32)
    key = lax.broadcasted_iota(jnp.int32, (1, span), 1).astype(jnp.float32)
    lane = lax.broadcasted_iota(jnp.int32, (1, HD), 1)
    lengths = []
    for ref in (pack_ref, far_ref):
        digits = ref[tail + 6 * rows:tail + 7 * rows, :].astype(jnp.float32)[0:1]
        lengths.append(jnp.concatenate([digits[:, :HD] * 8.0 + digits[:, HD:]] * (span // HD), axis=1))
    ones = jnp.ones((span, HD), jnp.bfloat16)
    pad = jnp.zeros((HD - 4 * rows, 2 * HD), jnp.bfloat16)
    for step in range(2):
        biases = []
        for length, owner in zip(lengths, owners):
            bias = jnp.where(key < length, 0.0, NEG)
            biases.append(bias if step == 0 else jnp.where(owner, NEG, bias))
        extra_bias = jnp.where((lane % (2 * rows) < rows * (1 + step)) & (lane < 4 * rows), 0.0, NEG)
        stats = jnp.zeros((block, HD), jnp.float32)
        for side, refs in enumerate(((pack_ref, far_ref), (side_ref, cross_ref))):
            extras = []
            for index in range(2):
                pieces = []
                for ref in refs:
                    own = tail + (2 * step + index) * rows
                    clean = tail + (4 + index) * rows
                    pieces += [ref[own:own + rows, :], ref[clean:clean + rows, :]]
                extras.append(jnp.concatenate(pieces + [pad], axis=0))
            for half in range(2):
                head = (core ^ side) * 2 + half
                lanes = slice(half * HD, (half + 1) * HD)
                query = wide[pl.ds(step * 4 + head, block, stride=PARTS), :].astype(jnp.bfloat16)
                groups = [(ref[0:span, lanes], ref[span:2 * span, lanes], bias) for ref, bias in zip(refs, biases)]
                groups.append((extras[0][:, lanes], extras[1][:, lanes], extra_bias))
                scores = [
                    lax.dot_general(query, keys, NT, preferred_element_type=jnp.float32) + mask
                    for keys, _, mask in groups
                ]
                top = jnp.max(scores[0], axis=1, keepdims=True)
                for score in scores[1:]:
                    top = jnp.maximum(top, jnp.max(score, axis=1, keepdims=True))
                top = jnp.ceil(top)
                accum = jnp.zeros((block, 2 * HD), jnp.float32)
                for score, (_, values, _) in zip(scores, groups):
                    weights = jnp.exp2((score - top) * EXP2_SCALE).astype(jnp.bfloat16)
                    values = jnp.concatenate([values, ones[:values.shape[0]]], axis=1)
                    accum = accum + lax.dot_general(weights, values, NN, preferred_element_type=jnp.float32)
                wide_out[pl.ds(head * 2 + step, block, stride=BACK), :] = accum[:, :HD]
                total = accum[:, HD:]
                top = jnp.broadcast_to(top, (block, HD))
                top_hi = top.astype(jnp.bfloat16).astype(jnp.float32)
                total_hi = total.astype(jnp.bfloat16).astype(jnp.float32)
                for place, value in enumerate((top_hi, top - top_hi, total_hi, total - total_hi)):
                    stats = jnp.where(lane == 32 * place + head, value, stats)
        wide_out[pl.ds(8 + step, block, stride=BACK), :] = stats
    out_ref[...] = wide_out[...].astype(jnp.bfloat16)


def combine_kernel(recv_ref, out_ref, wide):
    chips = out_ref.shape[1] // (4 * HD)
    senders = recv_ref.shape[0] // BACK
    devices = senders // chips
    wide[...] = recv_ref[...].astype(jnp.float32)

    def rows_of(place):
        return wide[pl.ds(place, senders, stride=BACK), :]

    for step in range(2):
        stats = rows_of(8 + step)
        local = (stats + pltpu.roll(stats, HD - 32, axis=1)).reshape(devices, chips, HD)
        total = (pltpu.roll(stats, HD - 64, axis=1) + pltpu.roll(stats, HD - 96, axis=1)).reshape(devices, chips, HD)
        top = jnp.max(local, axis=0, keepdims=True)
        scale = jnp.exp2((local - top) * EXP2_SCALE)
        scale = scale / jnp.sum(scale * total, axis=0, keepdims=True)
        for head in range(4):
            accum = rows_of(head * 2 + step).reshape(devices, chips, HD)
            result = jnp.sum(scale[:, :, head:head + 1] * accum, axis=0)
            for chip in range(chips):
                begin = (chip * 4 + head) * HD
                out_ref[step:step + 1, begin:begin + HD] = result[chip:chip + 1].astype(jnp.bfloat16)


def renew_kernel(evict_ref, near_ref, far_ref, cache_ref, new_ref):
    devices, _, rows, _ = near_ref.shape
    parity = lax.axis_index("cb")
    owner = lax.axis_index("ca") * 2 + parity == evict_ref[0]

    @pl.when(owner)
    def _():
        for ref, kind in ((near_ref, parity), (far_ref, 1 - parity)):
            for device in range(devices):
                place = pl.ds(pl.multiple_of((device * 2 + kind) * rows, rows), rows)
                for index in range(2):
                    new_ref[0, index, place, :] = ref[device, index]

    @pl.when(jnp.logical_not(owner))
    def _():
        new_ref[...] = cache_ref[...]


def call(kernel, out_shape, in_specs, scratch=(), name=None, limit=40, out=VMEM):
    several = isinstance(out_shape, tuple)
    return pl.pallas_call(
        kernel,
        out_shape=out_shape,
        in_specs=in_specs,
        out_specs=(out,) * len(out_shape) if several else out,
        scratch_shapes=list(scratch),
        compiler_params=pltpu.CompilerParams(vmem_limit_bytes=limit * 1024 * 1024),
        name=name,
    )


def body(queries, cache_kv, lengths, evict, own_kv, clean_kv):
    steps, _, features = queries.shape
    span, width = cache_kv.shape[2:]
    pairs = lax.axis_size("ca")
    chips = lax.axis_size("ha")
    rows = clean_kv.shape[1]
    tokens = pairs * chips
    bf16, f32 = jnp.bfloat16, jnp.float32
    shape = jax.ShapeDtypeStruct
    swap = [(0, 1), (1, 0)]
    pack = call(
        pack_kernel,
        shape((2 * span + 7 * rows, width), bf16),
        [SMEM] + [HBM] * 3,
        [pltpu.VMEM((rows, width), bf16), pltpu.SemaphoreType.DMA((9,))],
        name="pack",
        limit=60,
    )(lengths, cache_kv, own_kv, clean_kv)
    far = lax.ppermute(pack, "cb", swap)
    side = lax.ppermute(pack, "hb", swap)
    cross = lax.ppermute(far, "hb", swap)
    message, copies = call(
        spread_kernel,
        (shape((tokens * PARTS, HD), bf16), shape((pairs,) + clean_kv.shape, bf16)),
        [VMEM] * 2,
        [pltpu.VMEM((chips * PARTS, HD), f32)],
        name="spread",
    )(queries.reshape(steps, features), clean_kv)
    recv = lax.all_to_all(
        message.reshape(tokens, PARTS, HD), ("ca", "ha"), split_axis=0, concat_axis=0, tiled=True
    ).reshape(tokens * PARTS, HD)
    parts = call(
        attend_kernel,
        shape((tokens * BACK, HD), bf16),
        [SMEM] + [VMEM] * 5,
        [pltpu.VMEM((tokens * PARTS, HD), f32), pltpu.VMEM((tokens * BACK, HD), f32)],
        name="attend",
    )(evict, recv, pack, far, side, cross)
    _, copies = lax.optimization_barrier((recv, copies))
    near = lax.all_to_all(copies, "ca", split_axis=0, concat_axis=0, tiled=True)
    parts, near = lax.optimization_barrier((parts, near))
    back = lax.all_to_all(
        parts.reshape(tokens * BACK // 2, 2, HD), ("ca", "ha"), split_axis=0, concat_axis=0, tiled=True
    ).reshape(tokens * BACK, HD)
    attended = call(
        combine_kernel,
        shape((steps, features), bf16),
        [VMEM],
        [pltpu.VMEM((tokens * BACK, HD), f32)],
        name="combine",
    )(back)
    other = lax.ppermute(near, "cb", swap)
    new_cache = call(renew_kernel, shape(cache_kv.shape, bf16), [SMEM] + [VMEM] * 3, name="renew_cache")(
        evict, near, other, cache_kv
    )
    return (attended.reshape(steps, 1, features), new_cache)


def solution(mesh):
    ctx, heads = mesh.devices.shape
    split = jax.sharding.Mesh(mesh.devices.reshape(ctx // 2, 2, heads // 2, 2), ("ca", "cb", "ha", "hb"))
    ctx, heads = ("ca", "cb"), ("ha", "hb")
    in_specs = (
        P(None, ctx + heads, None),
        P(ctx, None, None, heads),
        P(ctx),
        P(),
        P(None, None, ctx, heads),
        P(None, ctx, heads),
    )
    out_specs = (P(None, ctx + heads, None), P(ctx, None, None, heads))
    return jax.shard_map(body, mesh=split, in_specs=in_specs, out_specs=out_specs, check_vma=False)
```

```python
import math

import jax
import jax.numpy as jnp
from jax import lax
from jax.experimental import pallas as pl
from jax.experimental.pallas import tpu as pltpu
from jax.sharding import PartitionSpec as P

HD = 128
PARTS = 8
BACK = 10
EXP2_SCALE = math.log2(math.e) / math.sqrt(HD)
NEG = -1e30
VMEM = pl.BlockSpec(memory_space=pltpu.VMEM)
SMEM = pl.BlockSpec(memory_space=pltpu.SMEM)
HBM = pl.BlockSpec(memory_space=pltpu.HBM)
NT = (((1,), (1,)), ((), ()))
NN = (((1,), (0,)), ((), ()))


def spread_kernel(q_ref, clean_ref, out_ref, copies_ref, rows):
    count = rows.shape[0]
    for row in range(count):
        chip, step, head = row // PARTS, row // 4 % 2, row % 4
        start = (chip * 4 + head) * HD
        rows[row:row + 1, :] = q_ref[step:step + 1, start:start + HD].astype(jnp.float32)
    message = rows[...].astype(out_ref.dtype)
    for dest in range(out_ref.shape[0] // count):
        out_ref[dest * count:(dest + 1) * count, :] = message
        copies_ref[dest] = clean_ref[...]


def pack_kernel(length_ref, cache_ref, own_ref, clean_ref, keys_ref, values_ref, sems):
    span, rows = cache_ref.shape[2], clean_ref.shape[1]
    length = length_ref[0]
    lane = lax.broadcasted_iota(jnp.int32, (rows, 2 * HD), 1)
    digits = jnp.where(lane < HD, length // 8, length % 8).astype(jnp.float32)
    copies = []
    for index, out_ref in enumerate((keys_ref, values_ref)):
        pieces = ((cache_ref.at[0, index], span), (own_ref.at[0, index], rows))
        pieces += ((own_ref.at[1, index], rows), (clean_ref.at[index], rows))
        place = 0
        for piece, count in pieces:
            copies.append(pltpu.make_async_copy(piece, out_ref.at[pl.ds(place, count)], sems.at[len(copies)]))
            copies[-1].start()
            place += count
        out_ref[place:place + rows, :] = digits.astype(out_ref.dtype)
    for copy in copies:
        copy.wait()


def attend_kernel(evict_ref, recv_ref, *refs):
    *packs, out_ref, wide, wide_out = refs
    pack, far, side_pack, cross = packs[0:2], packs[2:4], packs[4:6], packs[6:8]
    block = recv_ref.shape[0] // PARTS
    rows = 16
    span = pack[0].shape[0] - 4 * rows
    me = lax.axis_index("ca") * 2 + lax.axis_index("cb")
    core = lax.axis_index("hb")
    owners = [me == evict_ref[0], (me ^ 1) == evict_ref[0]]
    wide[...] = recv_ref[...].astype(jnp.float32)
    key = lax.broadcasted_iota(jnp.int32, (1, span), 1).astype(jnp.float32)
    lane = lax.broadcasted_iota(jnp.int32, (1, HD), 1)
    lengths = []
    for ref in (pack[0], far[0]):
        digits = ref[span + 3 * rows:span + 4 * rows, :].astype(jnp.float32)[0:1]
        lengths.append(jnp.concatenate([digits[:, :HD] * 8.0 + digits[:, HD:]] * (span // HD), axis=1))
    ones = jnp.ones((span, HD), jnp.bfloat16)
    pad = jnp.zeros((HD - 4 * rows, 2 * HD), jnp.bfloat16)
    for step in range(2):
        biases = []
        for length, owner in zip(lengths, owners):
            bias = jnp.where(key < length, 0.0, NEG)
            biases.append(bias if step == 0 else jnp.where(owner, NEG, bias))
        extra_bias = jnp.where((lane % (2 * rows) < rows * (1 + step)) & (lane < 4 * rows), 0.0, NEG)
        stats = jnp.zeros((block, HD), jnp.float32)
        for side, pairs in enumerate(((pack, far), (side_pack, cross))):
            extras = []
            for index in range(2):
                pieces = []
                for pair in pairs:
                    own = span + step * rows
                    clean = span + 2 * rows
                    pieces += [pair[index][own:own + rows, :], pair[index][clean:clean + rows, :]]
                extras.append(jnp.concatenate(pieces + [pad], axis=0))
            for half in range(2):
                head = (core ^ side) * 2 + half
                lanes = slice(half * HD, (half + 1) * HD)
                query = wide[pl.ds(step * 4 + head, block, stride=PARTS), :].astype(jnp.bfloat16)
                groups = [(pair[0][0:span, lanes], pair[1][0:span, lanes], bias) for pair, bias in zip(pairs, biases)]
                groups.append((extras[0][:, lanes], extras[1][:, lanes], extra_bias))
                scores = [
                    lax.dot_general(query, keys, NT, preferred_element_type=jnp.float32) + mask
                    for keys, _, mask in groups
                ]
                top = jnp.max(scores[0], axis=1, keepdims=True)
                for score in scores[1:]:
                    top = jnp.maximum(top, jnp.max(score, axis=1, keepdims=True))
                top = jnp.ceil(top)
                accum = jnp.zeros((block, 2 * HD), jnp.float32)
                for score, (_, values, _) in zip(scores, groups):
                    weights = jnp.exp2((score - top) * EXP2_SCALE).astype(jnp.bfloat16)
                    values = jnp.concatenate([values, ones[:values.shape[0]]], axis=1)
                    accum = accum + lax.dot_general(weights, values, NN, preferred_element_type=jnp.float32)
                wide_out[pl.ds(head * 2 + step, block, stride=BACK), :] = accum[:, :HD]
                total = accum[:, HD:]
                top = jnp.broadcast_to(top, (block, HD))
                top_hi = top.astype(jnp.bfloat16).astype(jnp.float32)
                total_hi = total.astype(jnp.bfloat16).astype(jnp.float32)
                for place, value in enumerate((top_hi, top - top_hi, total_hi, total - total_hi)):
                    stats = jnp.where(lane == 32 * place + head, value, stats)
        wide_out[pl.ds(8 + step, block, stride=BACK), :] = stats
    out_ref[...] = wide_out[...].astype(jnp.bfloat16)


def combine_kernel(recv_ref, out_ref, wide):
    chips = out_ref.shape[1] // (4 * HD)
    senders = recv_ref.shape[0] // BACK
    devices = senders // chips
    wide[...] = recv_ref[...].astype(jnp.float32)

    def rows_of(place):
        return wide[pl.ds(place, senders, stride=BACK), :].reshape(devices, chips, HD)

    for step in range(2):
        stats = rows_of(8 + step)
        for head in range(4):
            local = stats[:, :, head:head + 1] + stats[:, :, 32 + head:33 + head]
            total = stats[:, :, 64 + head:65 + head] + stats[:, :, 96 + head:97 + head]
            top = jnp.max(local, axis=0, keepdims=True)
            scale = jnp.exp2((local - top) * EXP2_SCALE)
            whole = jnp.sum(scale * total, axis=0)
            result = jnp.sum(scale * rows_of(head * 2 + step), axis=0) / whole
            for chip in range(chips):
                begin = (chip * 4 + head) * HD
                out_ref[step:step + 1, begin:begin + HD] = result[chip:chip + 1].astype(jnp.bfloat16)


def renew_kernel(evict_ref, near_ref, far_ref, cache_ref, new_ref):
    devices, _, rows, _ = near_ref.shape
    parity = lax.axis_index("cb")
    owner = lax.axis_index("ca") * 2 + parity == evict_ref[0]

    @pl.when(owner)
    def _():
        for ref, kind in ((near_ref, parity), (far_ref, 1 - parity)):
            for device in range(devices):
                place = pl.ds(pl.multiple_of((device * 2 + kind) * rows, rows), rows)
                for index in range(2):
                    new_ref[0, index, place, :] = ref[device, index]

    @pl.when(jnp.logical_not(owner))
    def _():
        new_ref[...] = cache_ref[...]


def call(kernel, out_shape, in_specs, scratch=(), name=None, limit=40, out=VMEM):
    several = isinstance(out_shape, tuple)
    return pl.pallas_call(
        kernel,
        out_shape=out_shape,
        in_specs=in_specs,
        out_specs=(out,) * len(out_shape) if several else out,
        scratch_shapes=list(scratch),
        compiler_params=pltpu.CompilerParams(vmem_limit_bytes=limit * 1024 * 1024),
        name=name,
    )


def body(queries, cache_kv, lengths, evict, own_kv, clean_kv):
    steps, _, features = queries.shape
    span, width = cache_kv.shape[2:]
    pairs = lax.axis_size("ca")
    chips = lax.axis_size("ha")
    rows = clean_kv.shape[1]
    tokens = pairs * chips
    bf16, f32 = jnp.bfloat16, jnp.float32
    shape = jax.ShapeDtypeStruct
    swap = [(0, 1), (1, 0)]
    pack = call(
        pack_kernel,
        (shape((span + 4 * rows, width), bf16),) * 2,
        [SMEM] + [HBM] * 3,
        [pltpu.SemaphoreType.DMA((8,))],
        name="pack",
        limit=60,
    )(lengths, cache_kv, own_kv, clean_kv)
    far = [lax.ppermute(array, "cb", swap) for array in pack]
    side = [lax.ppermute(array, "hb", swap) for array in pack]
    cross = [lax.ppermute(array, "hb", swap) for array in far]
    message, copies = call(
        spread_kernel,
        (shape((tokens * PARTS, HD), bf16), shape((pairs,) + clean_kv.shape, bf16)),
        [VMEM] * 2,
        [pltpu.VMEM((chips * PARTS, HD), f32)],
        name="spread",
    )(queries.reshape(steps, features), clean_kv)
    recv = lax.all_to_all(
        message.reshape(tokens, PARTS, HD), ("ca", "ha"), split_axis=0, concat_axis=0, tiled=True
    ).reshape(tokens * PARTS, HD)
    parts = call(
        attend_kernel,
        shape((tokens * BACK, HD), bf16),
        [SMEM] + [VMEM] * 9,
        [pltpu.VMEM((tokens * PARTS, HD), f32), pltpu.VMEM((tokens * BACK, HD), f32)],
        name="attend",
    )(evict, recv, *pack, *far, *side, *cross)
    _, copies = lax.optimization_barrier((recv, copies))
    near = lax.all_to_all(copies, "ca", split_axis=0, concat_axis=0, tiled=True)
    parts, near = lax.optimization_barrier((parts, near))
    back = lax.all_to_all(
        parts.reshape(tokens * BACK // 2, 2, HD), ("ca", "ha"), split_axis=0, concat_axis=0, tiled=True
    ).reshape(tokens * BACK, HD)
    attended = call(
        combine_kernel,
        shape((steps, features), bf16),
        [VMEM],
        [pltpu.VMEM((tokens * BACK, HD), f32)],
        name="combine",
    )(back)
    other = lax.ppermute(near, "cb", swap)
    new_cache = call(renew_kernel, shape(cache_kv.shape, bf16), [SMEM] + [VMEM] * 3, name="renew_cache")(
        evict, near, other, cache_kv
    )
    return (attended.reshape(steps, 1, features), new_cache)


def solution(mesh):
    ctx, heads = mesh.devices.shape
    split = jax.sharding.Mesh(mesh.devices.reshape(ctx // 2, 2, heads // 2, 2), ("ca", "cb", "ha", "hb"))
    ctx, heads = ("ca", "cb"), ("ha", "hb")
    in_specs = (
        P(None, ctx + heads, None),
        P(ctx, None, None, heads),
        P(ctx),
        P(),
        P(None, None, ctx, heads),
        P(None, ctx, heads),
    )
    out_specs = (P(None, ctx + heads, None), P(ctx, None, None, heads))
    return jax.shard_map(body, mesh=split, in_specs=in_specs, out_specs=out_specs, check_vma=False)
```

```python
import math

import jax
import jax.numpy as jnp
from jax import lax
from jax.experimental import pallas as pl
from jax.experimental.pallas import tpu as pltpu
from jax.sharding import PartitionSpec as P

HD = 128
PARTS = 8
BACK = 10
EXP2_SCALE = math.log2(math.e) / math.sqrt(HD)
NEG = -1e30
VMEM = pl.BlockSpec(memory_space=pltpu.VMEM)
SMEM = pl.BlockSpec(memory_space=pltpu.SMEM)
HBM = pl.BlockSpec(memory_space=pltpu.HBM)
NT = (((1,), (1,)), ((), ()))
NN = (((1,), (0,)), ((), ()))


def spread_kernel(q_ref, clean_ref, out_ref, copies_ref, rows):
    count = rows.shape[0]
    for row in range(count):
        chip, step, head = row // PARTS, row // 4 % 2, row % 4
        start = (chip * 4 + head) * HD
        rows[row:row + 1, :] = q_ref[step:step + 1, start:start + HD].astype(jnp.float32)
    message = rows[...].astype(out_ref.dtype)
    for dest in range(out_ref.shape[0] // count):
        out_ref[dest * count:(dest + 1) * count, :] = message
        copies_ref[dest] = clean_ref[...]


def pack_kernel(length_ref, cache_ref, own_ref, clean_ref, keys_ref, values_ref, sems):
    span, rows = cache_ref.shape[2], clean_ref.shape[1]
    length = length_ref[0]
    lane = lax.broadcasted_iota(jnp.int32, (rows, 2 * HD), 1)
    digits = jnp.where(lane < HD, length // 8, length % 8).astype(jnp.float32)
    copies = []
    for index, out_ref in enumerate((keys_ref, values_ref)):
        pieces = ((cache_ref.at[0, index], span), (own_ref.at[0, index], rows))
        pieces += ((own_ref.at[1, index], rows), (clean_ref.at[index], rows))
        place = 0
        for piece, count in pieces:
            copies.append(pltpu.make_async_copy(piece, out_ref.at[pl.ds(place, count)], sems.at[len(copies)]))
            copies[-1].start()
            place += count
        out_ref[place:place + rows, :] = digits.astype(out_ref.dtype)
    for copy in copies:
        copy.wait()


def attend_kernel(evict_ref, recv_ref, *refs):
    *packs, out_ref, wide, wide_out = refs
    pack, far, side_pack, cross = packs[0:2], packs[2:4], packs[4:6], packs[6:8]
    block = recv_ref.shape[0] // PARTS
    rows = 16
    span = pack[0].shape[0] - 4 * rows
    me = lax.axis_index("ca") * 2 + lax.axis_index("cb")
    core = lax.axis_index("hb")
    owners = [me == evict_ref[0], (me ^ 1) == evict_ref[0]]
    wide[...] = recv_ref[...].astype(jnp.float32)
    key = lax.broadcasted_iota(jnp.int32, (1, span), 1).astype(jnp.float32)
    lane = lax.broadcasted_iota(jnp.int32, (1, HD), 1)
    lengths = []
    for ref in (pack[0], far[0]):
        digits = ref[span + 3 * rows:span + 4 * rows, :].astype(jnp.float32)[0:1]
        lengths.append(jnp.concatenate([digits[:, :HD] * 8.0 + digits[:, HD:]] * (span // HD), axis=1))
    ones = jnp.ones((span, HD), jnp.bfloat16)
    pad = jnp.zeros((HD - 4 * rows, 2 * HD), jnp.bfloat16)
    for step in range(2):
        biases = []
        for length, owner in zip(lengths, owners):
            bias = jnp.where(key < length, 0.0, NEG)
            biases.append(bias if step == 0 else jnp.where(owner, NEG, bias))
        extra_bias = jnp.where((lane % (2 * rows) < rows * (1 + step)) & (lane < 4 * rows), 0.0, NEG)
        stats = jnp.zeros((block, HD), jnp.float32)
        for side, pairs in enumerate(((pack, far), (side_pack, cross))):
            extras = []
            for index in range(2):
                pieces = []
                for pair in pairs:
                    own = span + step * rows
                    clean = span + 2 * rows
                    pieces += [pair[index][own:own + rows, :], pair[index][clean:clean + rows, :]]
                extras.append(jnp.concatenate(pieces + [pad], axis=0))
            for half in range(2):
                head = (core ^ side) * 2 + half
                lanes = slice(half * HD, (half + 1) * HD)
                query = wide[pl.ds(step * 4 + head, block, stride=PARTS), :].astype(jnp.bfloat16)
                groups = [(pair[0][0:span, lanes], pair[1][0:span, lanes], bias) for pair, bias in zip(pairs, biases)]
                groups.append((extras[0][:, lanes], extras[1][:, lanes], extra_bias))
                scores = [
                    lax.dot_general(query, keys, NT, preferred_element_type=jnp.float32) + mask
                    for keys, _, mask in groups
                ]
                top = jnp.max(scores[0], axis=1, keepdims=True)
                for score in scores[1:]:
                    top = jnp.maximum(top, jnp.max(score, axis=1, keepdims=True))
                top = jnp.ceil(top)
                accum = jnp.zeros((block, 2 * HD), jnp.float32)
                for score, (_, values, _) in zip(scores, groups):
                    weights = jnp.exp2((score - top) * EXP2_SCALE).astype(jnp.bfloat16)
                    values = jnp.concatenate([values, ones[:values.shape[0]]], axis=1)
                    accum = accum + lax.dot_general(weights, values, NN, preferred_element_type=jnp.float32)
                wide_out[pl.ds(head * 2 + step, block, stride=BACK), :] = accum[:, :HD]
                total = accum[:, HD:]
                top = jnp.broadcast_to(top, (block, HD))
                top_hi = top.astype(jnp.bfloat16).astype(jnp.float32)
                total_hi = total.astype(jnp.bfloat16).astype(jnp.float32)
                for place, value in enumerate((top_hi, top - top_hi, total_hi, total - total_hi)):
                    stats = jnp.where(lane == 32 * place + head, value, stats)
        wide_out[pl.ds(8 + step, block, stride=BACK), :] = stats
    out_ref[...] = wide_out[...].astype(jnp.bfloat16)


def combine_kernel(recv_ref, out_ref, wide):
    chips = out_ref.shape[1] // (4 * HD)
    senders = recv_ref.shape[0] // BACK
    devices = senders // chips
    wide[...] = recv_ref[...].astype(jnp.float32)

    def rows_of(place):
        return wide[pl.ds(place, senders, stride=BACK), :].reshape(devices, chips, HD)

    for step in range(2):
        stats = rows_of(8 + step)
        for head in range(4):
            local = stats[:, :, head:head + 1] + stats[:, :, 32 + head:33 + head]
            total = stats[:, :, 64 + head:65 + head] + stats[:, :, 96 + head:97 + head]
            top = jnp.max(local, axis=0, keepdims=True)
            scale = jnp.exp2((local - top) * EXP2_SCALE)
            whole = jnp.sum(scale * total, axis=0)
            result = jnp.sum(scale * rows_of(head * 2 + step), axis=0) / whole
            for chip in range(chips):
                begin = (chip * 4 + head) * HD
                out_ref[step:step + 1, begin:begin + HD] = result[chip:chip + 1].astype(jnp.bfloat16)


def renew_kernel(evict_ref, near_ref, far_ref, cache_ref, new_ref):
    devices, _, rows, _ = near_ref.shape
    parity = lax.axis_index("cb")
    owner = lax.axis_index("ca") * 2 + parity == evict_ref[0]

    @pl.when(owner)
    def _():
        for ref, kind in ((near_ref, parity), (far_ref, 1 - parity)):
            for device in range(devices):
                place = pl.ds(pl.multiple_of((device * 2 + kind) * rows, rows), rows)
                for index in range(2):
                    new_ref[0, index, place, :] = ref[device, index]

    @pl.when(jnp.logical_not(owner))
    def _():
        new_ref[...] = cache_ref[...]


def call(kernel, out_shape, in_specs, scratch=(), name=None, limit=40, out=VMEM):
    several = isinstance(out_shape, tuple)
    return pl.pallas_call(
        kernel,
        out_shape=out_shape,
        in_specs=in_specs,
        out_specs=(out,) * len(out_shape) if several else out,
        scratch_shapes=list(scratch),
        compiler_params=pltpu.CompilerParams(vmem_limit_bytes=limit * 1024 * 1024),
        name=name,
    )


def body(queries, cache_kv, lengths, evict, own_kv, clean_kv):
    steps, _, features = queries.shape
    span, width = cache_kv.shape[2:]
    pairs = lax.axis_size("ca")
    chips = lax.axis_size("ha")
    rows = clean_kv.shape[1]
    tokens = pairs * chips
    bf16, f32 = jnp.bfloat16, jnp.float32
    shape = jax.ShapeDtypeStruct
    swap = [(0, 1), (1, 0)]
    pack = call(
        pack_kernel,
        (shape((span + 4 * rows, width), bf16),) * 2,
        [SMEM] + [HBM] * 3,
        [pltpu.SemaphoreType.DMA((8,))],
        name="pack",
        limit=60,
    )(lengths, cache_kv, own_kv, clean_kv)
    far = [lax.ppermute(array, "cb", swap) for array in pack]
    side = [lax.ppermute(array, "hb", swap) for array in pack]
    cross = [lax.ppermute(array, "hb", swap) for array in far]
    message, copies = call(
        spread_kernel,
        (shape((tokens * PARTS, HD), bf16), shape((pairs,) + clean_kv.shape, bf16)),
        [VMEM] * 2,
        [pltpu.VMEM((chips * PARTS, HD), f32)],
        name="spread",
    )(queries.reshape(steps, features), clean_kv)
    recv = lax.all_to_all(
        message.reshape(tokens, PARTS, HD), ("ca", "ha"), split_axis=0, concat_axis=0, tiled=True
    ).reshape(tokens * PARTS, HD)
    parts = call(
        attend_kernel,
        shape((tokens * BACK, HD), bf16),
        [SMEM] + [VMEM] * 9,
        [pltpu.VMEM((tokens * PARTS, HD), f32), pltpu.VMEM((tokens * BACK, HD), f32)],
        name="attend",
    )(evict, recv, *pack, *far, *side, *cross)
    _, copies = lax.optimization_barrier((side, copies))
    _, copies = lax.optimization_barrier((recv, copies))
    near = lax.all_to_all(copies, "ca", split_axis=0, concat_axis=0, tiled=True)
    parts, near = lax.optimization_barrier((parts, near))
    back = lax.all_to_all(
        parts.reshape(tokens * BACK // 2, 2, HD), ("ca", "ha"), split_axis=0, concat_axis=0, tiled=True
    ).reshape(tokens * BACK, HD)
    attended = call(
        combine_kernel,
        shape((steps, features), bf16),
        [VMEM],
        [pltpu.VMEM((tokens * BACK, HD), f32)],
        name="combine",
    )(back)
    other = lax.ppermute(near, "cb", swap)
    new_cache = call(renew_kernel, shape(cache_kv.shape, bf16), [SMEM] + [VMEM] * 3, name="renew_cache")(
        evict, near, other, cache_kv
    )
    return (attended.reshape(steps, 1, features), new_cache)


def solution(mesh):
    ctx, heads = mesh.devices.shape
    split = jax.sharding.Mesh(mesh.devices.reshape(ctx // 2, 2, heads // 2, 2), ("ca", "cb", "ha", "hb"))
    ctx, heads = ("ca", "cb"), ("ha", "hb")
    in_specs = (
        P(None, ctx + heads, None),
        P(ctx, None, None, heads),
        P(ctx),
        P(),
        P(None, None, ctx, heads),
        P(None, ctx, heads),
    )
    out_specs = (P(None, ctx + heads, None), P(ctx, None, None, heads))
    return jax.shard_map(body, mesh=split, in_specs=in_specs, out_specs=out_specs, check_vma=False)
```

```python
import math

import jax
import jax.numpy as jnp
from jax import lax
from jax.experimental import pallas as pl
from jax.experimental.pallas import tpu as pltpu
from jax.sharding import PartitionSpec as P

HD = 128
PARTS = 8
BACK = 10
EXP2_SCALE = math.log2(math.e) / math.sqrt(HD)
NEG = -1e30
VMEM = pl.BlockSpec(memory_space=pltpu.VMEM)
SMEM = pl.BlockSpec(memory_space=pltpu.SMEM)
HBM = pl.BlockSpec(memory_space=pltpu.HBM)
NT = (((1,), (1,)), ((), ()))
NN = (((1,), (0,)), ((), ()))


def spread_kernel(q_ref, clean_ref, out_ref, copies_ref, rows):
    count = rows.shape[0]
    for row in range(count):
        chip, step, head = row // PARTS, row // 4 % 2, row % 4
        start = (chip * 4 + head) * HD
        rows[row:row + 1, :] = q_ref[step:step + 1, start:start + HD].astype(jnp.float32)
    message = rows[...].astype(out_ref.dtype)
    for dest in range(out_ref.shape[0] // count):
        out_ref[dest * count:(dest + 1) * count, :] = message
        copies_ref[dest] = clean_ref[...]


def pack_kernel(length_ref, cache_ref, own_ref, clean_ref, pack_ref, digit_rows, sems, meanwhile):
    span, rows = cache_ref.shape[2], clean_ref.shape[1]
    pieces = [(cache_ref.at[0, index], span) for index in range(2)]
    pieces += [(own_ref.at[step, index], rows) for step in range(2) for index in range(2)]
    pieces += [(clean_ref.at[index], rows) for index in range(2)]
    pieces += [(digit_rows, rows)]
    length = length_ref[0]
    lane = lax.broadcasted_iota(jnp.int32, (rows, 2 * HD), 1)
    digits = jnp.where(lane < HD, length // 8, length % 8)
    digit_rows[...] = digits.astype(jnp.float32).astype(digit_rows.dtype)
    place, copies = 0, []
    for number, (piece, count) in enumerate(pieces):
        copies.append(pltpu.make_async_copy(piece, pack_ref.at[pl.ds(place, count)], sems.at[number]))
        copies[-1].start()
        place += count
    meanwhile()
    for copy in copies:
        copy.wait()


def front_kernel(
    length_ref, cache_ref, own_ref, far_clean_ref, q_ref, clean_ref, pack_ref, out_ref, copies_ref, digit_rows, sems, rows
):
    pack_kernel(
        length_ref, cache_ref, own_ref, far_clean_ref, pack_ref, digit_rows, sems,
        lambda: spread_kernel(q_ref, clean_ref, out_ref, copies_ref, rows),
    )


def attend_kernel(evict_ref, recv_ref, pack_ref, far_ref, side_ref, cross_ref, out_ref, wide, wide_out):
    block = recv_ref.shape[0] // PARTS
    rows = 16
    span = (pack_ref.shape[0] - 7 * rows) // 2
    tail = 2 * span
    me = lax.axis_index("ca") * 2 + lax.axis_index("cb")
    core = lax.axis_index("hb")
    owners = [me == evict_ref[0], (me ^ 1) == evict_ref[0]]
    wide[...] = recv_ref[...].astype(jnp.float32)
    key = lax.broadcasted_iota(jnp.int32, (1, span), 1).astype(jnp.float32)
    lane = lax.broadcasted_iota(jnp.int32, (1, HD), 1)
    lengths = []
    for ref in (pack_ref, far_ref):
        digits = ref[tail + 6 * rows:tail + 7 * rows, :].astype(jnp.float32)[0:1]
        lengths.append(jnp.concatenate([digits[:, :HD] * 8.0 + digits[:, HD:]] * (span // HD), axis=1))
    ones = jnp.ones((span, HD), jnp.bfloat16)
    pad = jnp.zeros((HD - 4 * rows, 2 * HD), jnp.bfloat16)
    for step in range(2):
        biases = []
        for length, owner in zip(lengths, owners):
            bias = jnp.where(key < length, 0.0, NEG)
            biases.append(bias if step == 0 else jnp.where(owner, NEG, bias))
        extra_bias = jnp.where((lane % (2 * rows) < rows * (1 + step)) & (lane < 4 * rows), 0.0, NEG)
        stats = jnp.zeros((block, HD), jnp.float32)
        for side, refs in enumerate(((pack_ref, far_ref), (side_ref, cross_ref))):
            extras = []
            for index in range(2):
                pieces = []
                for ref in refs:
                    own = tail + (2 * step + index) * rows
                    clean = tail + (4 + index) * rows
                    pieces += [ref[own:own + rows, :], ref[clean:clean + rows, :]]
                extras.append(jnp.concatenate(pieces + [pad], axis=0))
            for half in range(2):
                head = (core ^ side) * 2 + half
                lanes = slice(half * HD, (half + 1) * HD)
                query = wide[pl.ds(step * 4 + head, block, stride=PARTS), :].astype(jnp.bfloat16)
                groups = [(ref[0:span, lanes], ref[span:2 * span, lanes], bias) for ref, bias in zip(refs, biases)]
                groups.append((extras[0][:, lanes], extras[1][:, lanes], extra_bias))
                scores = [
                    lax.dot_general(query, keys, NT, preferred_element_type=jnp.float32) + mask
                    for keys, _, mask in groups
                ]
                top = jnp.max(scores[0], axis=1, keepdims=True)
                for score in scores[1:]:
                    top = jnp.maximum(top, jnp.max(score, axis=1, keepdims=True))
                top = jnp.ceil(top)
                accum = jnp.zeros((block, 2 * HD), jnp.float32)
                for score, (_, values, _) in zip(scores, groups):
                    weights = jnp.exp2((score - top) * EXP2_SCALE).astype(jnp.bfloat16)
                    values = jnp.concatenate([values, ones[:values.shape[0]]], axis=1)
                    accum = accum + lax.dot_general(weights, values, NN, preferred_element_type=jnp.float32)
                wide_out[pl.ds(head * 2 + step, block, stride=BACK), :] = accum[:, :HD]
                total = accum[:, HD:]
                top = jnp.broadcast_to(top, (block, HD))
                top_hi = top.astype(jnp.bfloat16).astype(jnp.float32)
                total_hi = total.astype(jnp.bfloat16).astype(jnp.float32)
                for place, value in enumerate((top_hi, top - top_hi, total_hi, total - total_hi)):
                    stats = jnp.where(lane == 32 * place + head, value, stats)
        wide_out[pl.ds(8 + step, block, stride=BACK), :] = stats
    out_ref[...] = wide_out[...].astype(jnp.bfloat16)


def combine_kernel(recv_ref, out_ref, wide):
    chips = out_ref.shape[1] // (4 * HD)
    senders = recv_ref.shape[0] // BACK
    devices = senders // chips
    wide[...] = recv_ref[...].astype(jnp.float32)

    def rows_of(place):
        return wide[pl.ds(place, senders, stride=BACK), :].reshape(devices, chips, HD)

    for step in range(2):
        stats = rows_of(8 + step)
        for head in range(4):
            local = stats[:, :, head:head + 1] + stats[:, :, 32 + head:33 + head]
            total = stats[:, :, 64 + head:65 + head] + stats[:, :, 96 + head:97 + head]
            top = jnp.max(local, axis=0, keepdims=True)
            scale = jnp.exp2((local - top) * EXP2_SCALE)
            whole = jnp.sum(scale * total, axis=0)
            result = jnp.sum(scale * rows_of(head * 2 + step), axis=0) / whole
            for chip in range(chips):
                begin = (chip * 4 + head) * HD
                out_ref[step:step + 1, begin:begin + HD] = result[chip:chip + 1].astype(jnp.bfloat16)


def renew_kernel(evict_ref, near_ref, far_ref, cache_ref, new_ref):
    devices, _, rows, _ = near_ref.shape
    parity = lax.axis_index("cb")
    owner = lax.axis_index("ca") * 2 + parity == evict_ref[0]

    @pl.when(owner)
    def _():
        for ref, kind in ((near_ref, parity), (far_ref, 1 - parity)):
            for device in range(devices):
                place = pl.ds(pl.multiple_of((device * 2 + kind) * rows, rows), rows)
                for index in range(2):
                    new_ref[0, index, place, :] = ref[device, index]

    @pl.when(jnp.logical_not(owner))
    def _():
        new_ref[...] = cache_ref[...]


def call(kernel, out_shape, in_specs, scratch=(), name=None, limit=40, out=VMEM):
    several = isinstance(out_shape, tuple)
    return pl.pallas_call(
        kernel,
        out_shape=out_shape,
        in_specs=in_specs,
        out_specs=(out,) * len(out_shape) if several else out,
        scratch_shapes=list(scratch),
        compiler_params=pltpu.CompilerParams(vmem_limit_bytes=limit * 1024 * 1024),
        name=name,
    )


def body(queries, cache_kv, lengths, evict, own_kv, clean_kv):
    steps, _, features = queries.shape
    span, width = cache_kv.shape[2:]
    pairs = lax.axis_size("ca")
    chips = lax.axis_size("ha")
    rows = clean_kv.shape[1]
    tokens = pairs * chips
    bf16, f32 = jnp.bfloat16, jnp.float32
    shape = jax.ShapeDtypeStruct
    swap = [(0, 1), (1, 0)]
    pack, message, copies = call(
        front_kernel,
        (
            shape((2 * span + 7 * rows, width), bf16),
            shape((tokens * PARTS, HD), bf16),
            shape((pairs,) + clean_kv.shape, bf16),
        ),
        [SMEM] + [HBM] * 3 + [VMEM] * 2,
        [
            pltpu.VMEM((rows, width), bf16),
            pltpu.SemaphoreType.DMA((9,)),
            pltpu.VMEM((chips * PARTS, HD), f32),
        ],
        name="front",
        limit=60,
    )(lengths, cache_kv, own_kv, clean_kv, queries.reshape(steps, features), clean_kv)
    far = lax.ppermute(pack, "cb", swap)
    side = lax.ppermute(pack, "hb", swap)
    cross = lax.ppermute(far, "hb", swap)
    recv = lax.all_to_all(
        message.reshape(tokens, PARTS, HD), ("ca", "ha"), split_axis=0, concat_axis=0, tiled=True
    ).reshape(tokens * PARTS, HD)
    parts = call(
        attend_kernel,
        shape((tokens * BACK, HD), bf16),
        [SMEM] + [VMEM] * 5,
        [pltpu.VMEM((tokens * PARTS, HD), f32), pltpu.VMEM((tokens * BACK, HD), f32)],
        name="attend",
    )(evict, recv, pack, far, side, cross)
    _, copies = lax.optimization_barrier((recv, copies))
    near = lax.all_to_all(copies, "ca", split_axis=0, concat_axis=0, tiled=True)
    parts, near = lax.optimization_barrier((parts, near))
    back = lax.all_to_all(
        parts.reshape(tokens * BACK // 2, 2, HD), ("ca", "ha"), split_axis=0, concat_axis=0, tiled=True
    ).reshape(tokens * BACK, HD)
    attended = call(
        combine_kernel,
        shape((steps, features), bf16),
        [VMEM],
        [pltpu.VMEM((tokens * BACK, HD), f32)],
        name="combine",
    )(back)
    other = lax.ppermute(near, "cb", swap)
    new_cache = call(renew_kernel, shape(cache_kv.shape, bf16), [SMEM] + [VMEM] * 3, name="renew_cache")(
        evict, near, other, cache_kv
    )
    return (attended.reshape(steps, 1, features), new_cache)


def solution(mesh):
    ctx, heads = mesh.devices.shape
    split = jax.sharding.Mesh(mesh.devices.reshape(ctx // 2, 2, heads // 2, 2), ("ca", "cb", "ha", "hb"))
    ctx, heads = ("ca", "cb"), ("ha", "hb")
    in_specs = (
        P(None, ctx + heads, None),
        P(ctx, None, None, heads),
        P(ctx),
        P(),
        P(None, None, ctx, heads),
        P(None, ctx, heads),
    )
    out_specs = (P(None, ctx + heads, None), P(ctx, None, None, heads))
    return jax.shard_map(body, mesh=split, in_specs=in_specs, out_specs=out_specs, check_vma=False)
```
